32 devices in a mesh: gx: 8 (over y, x, core), gy: 4 (over z).
Axes of the slice: x: 2, y: 2, z: 4, core: 2. Of those that a mesh axis runs over, the one named last changes fastest.
Arguments:
- populations: float32 [19, 64, 64, 128], P(None, 'gx', 'gy')
- anchor: int32 [8, 4, 1024], P('gx', 'gy'), may hold values from 0 to 20606, as said below
- offsets: float32 [8, 4, 3, 1024], P('gx', 'gy'), may hold values from 0 to 0.999
- heading: float32 [8, 4, 2, 1024], P('gx', 'gy'), may hold values from -3.140625 to 3.140625
- velocity: float32 [8, 4, 3, 1024], P('gx', 'gy'), may hold values from -0.6 to 0.6
- live_count: int32 [8, 4], P('gx', 'gy'), may hold values from 1 to 1024, as said below
Outputs:
- populations_next: float32 [19, 64, 64, 128], P(None, 'gx', 'gy')
- swimmer_force: float32 [8, 4, 3, 1024], P('gx', 'gy')
The draws below stay inside these ranges and needn't reach their ends.
Inputs may be any that keep to these rules, and one draw needn't show every extreme that they name: The anchor is (ax (18) + ay) * 128 + az with 0 <= ax <= 8, 0 <= ay <= 16, 0 <= az <= 126. Live swimmers fill slots 0 to live_count - 1 of their device; some device holds 1024.
All inputs are finite; a program needn't handle non-finite values.
Results may differ from the reference program's by a relative error of at most 0.0003.
Values sent between devices are 32-bit elements; how exact they have to be, the bound alone decides.
No kernel may reach another device: no remote copies, remote signals or barrier semaphores. Data moves between devices by JAX's collectives and lax.ppermute only.
A program may use at most 64 MiB of HBM per device.

```python
import jax
import jax.numpy as jnp
from jax import lax

CX = 8
CY = 16
NZ = 128
SW_DEV = 1024
N_GX = 8
N_GY = 4


def draw_populations(key, part):
    weight = jnp.asarray((1.0 / 3.0,) + (1.0 / 18.0,) * 6 + (1.0 / 36.0,) * 12, jnp.float32)
    spread = jax.random.uniform(key, (19, CX * N_GX, CY * N_GY, NZ), jnp.float32)
    factor = 0.6 + 0.8 * spread
    return weight[:, None, None, None] * factor


def draw_anchor(key, part):
    first, second, third = jax.random.split(jax.random.fold_in(key, 11), 3)
    shape = (N_GX, N_GY, SW_DEV)
    cell_x = jax.random.randint(first, shape, 0, CX + 1)
    cell_y = jax.random.randint(second, shape, 0, CY + 1)
    cell_z = jax.random.randint(third, shape, 0, NZ - 1)
    return ((cell_x * (CY + 2) + cell_y) * NZ + cell_z).astype(jnp.int32)


def draw_live_count(key, part):
    first, second = jax.random.split(jax.random.fold_in(key, 23))
    lowest = max(1, SW_DEV // 8)
    counts = jax.random.randint(first, (N_GX, N_GY), lowest, SW_DEV // 2 + 1)
    chosen = jax.random.randint(second, (), 0, N_GX * N_GY)
    places = jnp.arange(N_GX * N_GY, dtype=jnp.int32).reshape(N_GX, N_GY)
    return jnp.where(places == chosen, SW_DEV, counts).astype(jnp.int32)


def shard_levels(stream_key, extent, cuts, low, top_value):
    factor_of = 1.0
    for position, shards_of in cuts:
        heights = jax.random.uniform(jax.random.fold_in(jax.random.fold_in(stream_key, 6), position), (shards_of,), jnp.float32, low / len(cuts), top_value / len(cuts))
        factor_of = factor_of * jnp.repeat(jnp.exp(heights), extent[position] // shards_of).reshape((-1,) + (1,) * (len(extent) - 1 - position))
    return factor_of


def normal_values(key, shape, scale, bound, shards=(), held_as=jnp.bfloat16):
    drawn = scale * jax.random.normal(key, shape, jnp.float32)
    if shards:
        drawn = drawn * shard_levels(key, shape, shards, -0.22, 0.18)
    return jnp.clip(drawn, -bound, bound).astype(held_as)


def setup_inputs(seed: int = 0) -> dict:
    keys = jax.random.split(jax.random.key(seed), 7)
    populations = draw_populations(jax.random.fold_in(keys[6], 71), 0)
    anchor = draw_anchor(jax.random.fold_in(keys[6], 71), 0)
    offsets = jnp.clip(0.999 * jax.random.uniform(keys[2], (N_GX, N_GY, 3, SW_DEV), jnp.float32) ** shard_levels(keys[2], (N_GX, N_GY, 3, SW_DEV), ((0, 8), (1, 4)), -0.2, 0.2), 0.0, 0.999)
    heading = jnp.clip(jax.random.uniform(keys[3], (N_GX, N_GY, 2, SW_DEV), jnp.float32, -3.140625, 3.140625), -3.140625, 3.140625)
    velocity = normal_values(keys[4], (N_GX, N_GY, 3, SW_DEV), 0.1, 0.6, ((0, 8), (1, 4)), jnp.float32)
    live_count = draw_live_count(jax.random.fold_in(keys[6], 71), 0)
    return dict(populations=populations, anchor=anchor, offsets=offsets, heading=heading, velocity=velocity, live_count=live_count)


lattice_dirs = ((0, 0, 0), (1, 0, 0), (-1, 0, 0), (0, 1, 0), (0, -1, 0), (0, 0, 1), (0, 0, -1),
                (1, 1, 0), (-1, -1, 0), (1, -1, 0), (-1, 1, 0), (1, 0, 1), (-1, 0, -1),
                (1, 0, -1), (-1, 0, 1), (0, 1, 1), (0, -1, -1), (0, 1, -1), (0, -1, 1))
lattice_weights = (1.0 / 3.0,) + (1.0 / 18.0,) * 6 + (1.0 / 36.0,) * 12
relax_time = 0.8
friction = 2.0
propulsion = 0.5
wca_energy = 0.01
floor_square = 0.8
cutoff_square = 2.0 ** (1.0 / 3.0)


def moments(fluid):
    dirs = jnp.asarray(lattice_dirs, jnp.float32)
    density = jnp.sum(fluid, axis=0)
    momentum = jnp.einsum("qc,qxyz->cxyz", dirs, fluid, precision=lax.Precision.HIGHEST)
    return density, momentum


def collide(fluid, forcing):
    dirs = jnp.asarray(lattice_dirs, jnp.float32)
    density, momentum = moments(fluid)
    speed = (momentum + 0.5 * forcing) / density
    along = jnp.einsum("qc,cxyz->qxyz", dirs, speed, precision=lax.Precision.HIGHEST)
    pushed = jnp.einsum("qc,cxyz->qxyz", dirs, forcing, precision=lax.Precision.HIGHEST)
    square = jnp.sum(speed * speed, axis=0)
    dotted = jnp.sum(speed * forcing, axis=0)
    weight = jnp.asarray(lattice_weights, jnp.float32)[:, None, None, None]
    balance = weight * density * (1.0 + 3.0 * along + 4.5 * along * along - 1.5 * square)
    source = (1.0 - 0.5 / relax_time) * weight * (3.0 * (pushed - dotted) + 9.0 * along * pushed)
    return fluid - (fluid - balance) / relax_time + source


def stencil(root, offsets, stride_x, stride_y):
    indices = []
    shares = []
    for step_x in (0, 1):
        for step_y in (0, 1):
            for step_z in (0, 1):
                part_x = offsets[..., 0, :] if step_x else 1.0 - offsets[..., 0, :]
                part_y = offsets[..., 1, :] if step_y else 1.0 - offsets[..., 1, :]
                part_z = offsets[..., 2, :] if step_z else 1.0 - offsets[..., 2, :]
                indices.append(root + step_x * stride_x + step_y * stride_y + step_z)
                shares.append(part_x * part_y * part_z)
    return indices, shares


def direction(heading):
    first = heading[..., 0, :]
    second = heading[..., 1, :]
    return jnp.stack([jnp.cos(first) * jnp.cos(second), jnp.sin(first) * jnp.cos(second), jnp.sin(second)], axis=-2)


def pair_force(own, ghosts, depth):
    delta = own[:3, :, None] - ghosts[:3, None, :]
    along_z = delta[2]
    along_z = jnp.where(along_z > 0.5 * depth, along_z - depth, jnp.where(along_z < -0.5 * depth, along_z + depth, along_z))
    delta = jnp.stack([delta[0], delta[1], along_z])
    raw = jnp.sum(delta * delta, axis=0)
    square = jnp.maximum(raw, floor_square)
    inverse = 1.0 / square
    sixth = inverse * inverse * inverse
    magnitude = 24.0 * wca_energy * (2.0 * sixth * sixth - sixth) * inverse
    keep = jnp.where(raw < cutoff_square, ghosts[3][None, :], 0.0)
    return jnp.sum(delta * (magnitude * keep)[None], axis=2)


def reference(populations, anchor, offsets, heading, velocity, live_count):
    grid_x = CX * N_GX
    grid_y = CY * N_GY
    density, momentum = moments(populations)
    speed = momentum / density
    framed = jnp.pad(speed, ((0, 0), (1, 1), (1, 1), (0, 0)), mode="wrap").reshape(3, -1)
    block_row = (CY + 2) * NZ
    cell_x = anchor // block_row
    rest = anchor % block_row
    cell_y = rest // NZ
    cell_z = rest % NZ
    dev_x = jnp.arange(N_GX, dtype=jnp.int32)[:, None, None]
    dev_y = jnp.arange(N_GY, dtype=jnp.int32)[None, :, None]
    root = ((dev_x * CX + cell_x) * (grid_y + 2) + dev_y * CY + cell_y) * NZ + cell_z
    indices, shares = stencil(root, offsets, (grid_y + 2) * NZ, NZ)
    sampled = jnp.zeros(velocity.shape, jnp.float32)
    for index, share in zip(indices, shares):
        sampled = sampled + share[:, :, None, :] * jnp.moveaxis(framed[:, index], 0, 2)
    slots = jnp.arange(SW_DEV, dtype=jnp.int32)
    live = (slots[None, None, :] < live_count[:, :, None]).astype(jnp.float32)
    drag = friction * (sampled - velocity)
    push = propulsion * direction(heading)
    reaction = -(drag + push) * live[:, :, None, :]
    spread = jnp.zeros((3, (grid_x + 2) * (grid_y + 2) * NZ), jnp.float32)
    for index, share in zip(indices, shares):
        spread = spread.at[:, index.reshape(-1)].add(jnp.moveaxis(reaction * share[:, :, None, :], 2, 0).reshape(3, -1))
    spread = spread.reshape(3, grid_x + 2, grid_y + 2, NZ)
    inner = spread[:, 1:grid_x + 1]
    inner = inner.at[:, 0].add(spread[:, grid_x + 1]).at[:, grid_x - 1].add(spread[:, 0])
    forcing = inner[:, :, 1:grid_y + 1]
    forcing = forcing.at[:, :, 0].add(inner[:, :, grid_y + 1]).at[:, :, grid_y - 1].add(inner[:, :, 0])
    post = collide(populations, forcing)
    moved = jnp.stack([jnp.roll(post[q], lattice_dirs[q], axis=(0, 1, 2)) for q in range(19)])
    place_x = cell_x.astype(jnp.float32) - 1.0 + offsets[:, :, 0]
    place_y = cell_y.astype(jnp.float32) - 1.0 + offsets[:, :, 1]
    place_z = cell_z.astype(jnp.float32) + offsets[:, :, 2]
    own = jnp.stack([place_x, place_y, place_z, live], axis=2)
    seen = []
    for step_a in (-1, 0, 1):
        for step_b in (-1, 0, 1):
            rolled = jnp.roll(own, (-step_a, -step_b), axis=(0, 1))
            moved_by = jnp.asarray([step_a * CX, step_b * CY, 0, 0], jnp.float32)[:, None]
            seen.append(rolled + moved_by)
    ghosts = jnp.concatenate(seen, axis=3)
    depth = jnp.float32(NZ)
    pairs = lax.map(lambda item: pair_force(item[0], item[1], depth),
                    (own.reshape(-1, 4, SW_DEV), ghosts.reshape(-1, 4, 9 * SW_DEV)))
    pairs = pairs.reshape(N_GX, N_GY, 3, SW_DEV)
    force = (pairs + drag + push) * live[:, :, None, :]
    return moved, force
```

```python
import functools

import jax
import jax.numpy as jnp
from jax import lax
from jax.experimental import pallas as pl
from jax.experimental.pallas import tpu as pltpu
from jax.sharding import PartitionSpec as P

lattice_dirs = (
    (0, 0, 0),
    (1, 0, 0),
    (-1, 0, 0),
    (0, 1, 0),
    (0, -1, 0),
    (0, 0, 1),
    (0, 0, -1),
    (1, 1, 0),
    (-1, -1, 0),
    (1, -1, 0),
    (-1, 1, 0),
    (1, 0, 1),
    (-1, 0, -1),
    (1, 0, -1),
    (-1, 0, 1),
    (0, 1, 1),
    (0, -1, -1),
    (0, 1, -1),
    (0, -1, 1),
)
lattice_weights = (1.0 / 3.0,) + (1.0 / 18.0,) * 6 + (1.0 / 36.0,) * 12
relax_time = 0.8
friction = 2.0
propulsion = 0.5
wca_energy = 0.01
floor_square = 0.8
cutoff_square = 2.0 ** (1.0 / 3.0)

f32 = jnp.float32
bf16 = jnp.bfloat16
LANES = 128
SUB = 8
FAR = 1.0e9
YPAD = 24
STRIP = 12


def outward(axis, sign):
    return [q for q in range(19) if lattice_dirs[q][axis] == sign]


def split(value):
    high = value.astype(bf16)
    low = (value - high.astype(f32)).astype(bf16)
    return high, low


def pack_y(pops, anchor, offsets, heading, velocity, count, mom, up, down, *, cx, cy, nz, slots):
    rho = pops[0]
    for q in range(1, 19):
        rho = rho + pops[q]
    inverse = 1.0 / rho
    mom[3] = rho
    for c in range(3):
        total = None
        for q in range(19):
            sign = lattice_dirs[q][c]
            if sign == 0:
                continue
            term = pops[q] if sign == 1 else -pops[q]
            total = term if total is None else total + term
        mom[c] = total * inverse
    for ref, rows, sign in ((up, (cy - 2, cy - 1), 1), (down, (0, 1), -1)):
        ring = cy - 1 if sign == 1 else 0
        for c in range(3):
            for k in range(2):
                ref[2 * c + k] = mom[c, :, rows[k], :]
        ref[6] = mom[3, :, ring, :]
        for k, q in enumerate(outward(1, sign)):
            ref[7 + k] = pops[q, :, ring, :]
    number = anchor[0].astype(f32)
    block_row = (cy + 2) * nz
    cell_x = jnp.floor((number + 0.5) * (1.0 / block_row))
    rest = number - cell_x * block_row
    cell_y = jnp.floor((rest + 0.5) * (1.0 / nz))
    cell_z = rest - cell_y * nz
    live = lax.broadcasted_iota(jnp.int32, (1, slots), 1) < count[0, 0]
    local = offsets[0, 0]
    place_x = jnp.where(live, cell_x - 1.0 + local[0:1], FAR)
    place_y = cell_y - 1.0 + local[1:2]
    place_z = cell_z + local[2:3]
    cosine = jnp.cos(heading[0, 0])
    sine = jnp.sin(heading[0, 0])
    speed = velocity[0, 0]
    rows = [
        place_x,
        place_y,
        place_z,
        friction * speed[0:1] - propulsion * cosine[0:1] * cosine[1:2],
        friction * speed[1:2] - propulsion * sine[0:1] * cosine[1:2],
        friction * speed[2:3] - propulsion * sine[1:2],
        live.astype(f32),
        jnp.full((1, slots), count[0, 0].astype(f32)),
    ]
    for k in range(slots // LANES):
        for f in range(8):
            piece = rows[f][:, k * LANES : (k + 1) * LANES]
            up[STRIP + k, f : f + 1, :] = piece
            down[STRIP + k, f : f + 1, :] = piece


def pack_x(pops, mom, own_up, from_down, from_up, right, left, *, cx, cy, nz, slots):
    chunks = slots // LANES
    for ref, cols, sign in ((right, (cx - 2, cx - 1), 1), (left, (0, 1), -1)):
        ring = cx - 1 if sign == 1 else 0
        names = outward(0, sign)
        zero = jnp.zeros((YPAD, LANES), f32)
        for f in range(STRIP):
            ref[f] = zero
        for c in range(3):
            for k in range(2):
                ref[2 * c + k, 2 : 2 + cy, :] = mom[c, cols[k]]
                ref[2 * c + k, 0:2, :] = from_down[2 * c : 2 * c + 2, cols[k], :]
                ref[2 * c + k, 2 + cy : 4 + cy, :] = from_up[2 * c : 2 * c + 2, cols[k], :]
        ref[6, 2 : 2 + cy, :] = mom[3, ring]
        ref[6, 1:2, :] = from_down[6, ring : ring + 1, :]
        ref[6, 2 + cy : 3 + cy, :] = from_up[6, ring : ring + 1, :]
        for k, q in enumerate(names):
            ref[7 + k, 2 : 2 + cy, :] = pops[q, ring]
            if lattice_dirs[q][1] == 1:
                at = 7 + outward(1, 1).index(q)
                ref[7 + k, 1:2, :] = from_down[at, ring : ring + 1, :]
            if lattice_dirs[q][1] == -1:
                at = 7 + outward(1, -1).index(q)
                ref[7 + k, 2 + cy : 3 + cy, :] = from_up[at, ring : ring + 1, :]
        for part, source in enumerate((own_up, from_down, from_up)):
            for k in range(chunks):
                ref[STRIP + part * (chunks // 3 + 1) + k // 3, (k % 3) * SUB : (k % 3 + 1) * SUB, :] = source[STRIP + k]


def tent(length, first, place):
    cell = jnp.floor(place)
    part = place - cell
    rows = lax.broadcasted_iota(jnp.int32, (length, LANES), 0).astype(f32) + first
    return jnp.where(rows == cell, 1.0 - part, jnp.where(rows == cell + 1.0, part, 0.0))


def post_of(q, pop, rho, u, force, common):
    c = lattice_dirs[q]
    w = lattice_weights[q]

    def dot(v):
        total = None
        for k in range(3):
            if c[k] == 0:
                continue
            term = v[k] if c[k] == 1 else -v[k]
            total = term if total is None else total + term
        return total

    base, dotted = common
    kept = (1.0 - 1.0 / relax_time) * pop
    scale = (1.0 - 0.5 / relax_time) * w
    if q == 0:
        return kept + (w / relax_time) * rho * base - (3.0 * scale) * dotted
    along = dot(u)
    pushed = dot(force)
    balance = (w / relax_time) * rho * (base + along * (3.0 + 4.5 * along))
    source = (3.0 * scale) * (pushed * (1.0 + 3.0 * along) - dotted)
    return kept + balance + source


def main_kernel(pops, mom, own, from_down, from_up, from_left, from_right, moved, out,
                ext, ub, ulo, uhi, fe, flo, fhi, post, gb, pacc, sacc, *, cx, cy, nz, slots):
    chunks = slots // LANES
    wide = cx + 4

    ext[...] = jnp.zeros_like(ext)
    for c in range(3):
        for x in range(cx):
            ext[x + 2, c, 2 : 2 + cy, :] = mom[c, x]
            ext[x + 2, c, 0:2, :] = from_down[2 * c : 2 * c + 2, x, :]
            ext[x + 2, c, 2 + cy : 4 + cy, :] = from_up[2 * c : 2 * c + 2, x, :]
        for k in range(2):
            ext[k, c] = from_left[2 * c + k]
            ext[cx + 2 + k, c] = from_right[2 * c + k]

    def both(value, rows):
        high, low = split(value.reshape(rows, LANES))
        return jnp.concatenate([high, low], axis=1)

    for x in range(0, wide, 2):
        rows = 2 * 3 * YPAD
        ub[x * 3 * YPAD : x * 3 * YPAD + rows, :] = both(ext[x : x + 2], rows)
        rows = 2 * 3 * SUB
        ulo[x * 3 * SUB : x * 3 * SUB + rows, :] = both(ext[x : x + 2, :, 0:SUB, :], rows)
        uhi[x * 3 * SUB : x * 3 * SUB + rows, :] = both(ext[x : x + 2, :, 2 * SUB : 3 * SUB, :], rows)
    fe[...] = jnp.zeros_like(fe)
    flo[...] = jnp.zeros_like(flo)
    fhi[...] = jnp.zeros_like(fhi)

    def own_tile(k):
        return own[STRIP + k]

    def swimmer_set(tile_at, live_chunks, shift_x, shift_y, table, depth, first_y, span, target, lanes_x, keep):
        x0, x1 = span
        f0, f1 = lanes_x
        per = 3 * depth

        def step(k, carry):
            tile = tile_at(k)
            tz = tent(nz, 0.0, tile[2:3])
            high, low = split(tz)
            top = jnp.concatenate([high, low], axis=1)
            right = jnp.concatenate([top, top], axis=0)
            wx = tent(wide + 4, -2.0, tile[0:1] + shift_x)
            wy = tent(depth, first_y, tile[1:2] + shift_y)
            full = jnp.dot(table[x0 * per : x1 * per, :], right, preferred_element_type=f32)
            full = (full[:, :LANES] + full[:, LANES:]).reshape(x1 - x0, 3, depth, LANES)
            total = full[0] * wx[x0 : x0 + 1]
            for x in range(x0 + 1, x1):
                total = total + full[x - x0] * wx[x : x + 1]
            sampled = jnp.sum(total * wy[None], axis=1)
            react = tile[3:6] - friction * sampled
            if keep:
                sacc[k, 0:3, :] = -react
            react = react * tile[6:7]
            pieces = []
            for x in range(f0, f1):
                for c in range(3):
                    pieces.append((wx[x : x + 1] * react[c : c + 1]) * wy)
            left = both(jnp.stack(pieces), (f1 - f0) * per)
            tall = jnp.concatenate(
                [jnp.concatenate([high, high], axis=1), jnp.concatenate([low, low], axis=1)], axis=0
            )
            spread = lax.dot_general(left, tall, (((1,), (1,)), ((), ())), preferred_element_type=f32)
            spread = (spread[:, :LANES] + spread[:, LANES:]).reshape(f1 - f0, 3, depth, LANES)
            target[f0:f1] += spread
            return carry

        lax.fori_loop(0, live_chunks, step, 0)

    def y_tile(ref):
        return lambda k: ref[STRIP + k]

    def x_tile(ref, part):
        def at(k):
            row = pl.multiple_of(lax.rem(k, 3) * SUB, SUB)
            return ref[STRIP + part * (chunks // 3 + 1) + lax.div(k, 3), pl.ds(row, SUB), :]

        return at

    sets = []
    for a in (0, -1, 1):
        for b in (0, -1, 1):
            if a == 0:
                source = y_tile((own, from_down, from_up)[b if b >= 0 else 1] if b != 1 else from_up)
            else:
                source = x_tile(from_left if a == -1 else from_right, {0: 0, -1: 1, 1: 2}[b])
            sets.append((a, b, source))

    counts = []
    for a, b, source in sets:
        value = jnp.max(source(0)[7:8, :]).astype(jnp.int32)
        counts.append(value)

    for (a, b, source), count in zip(sets, counts):
        live_chunks = lax.div(count + (LANES - 1), LANES)
        if b == 0:
            table, depth, first_y, target = ub, YPAD, -2.0, fe
        elif b == -1:
            table, depth, first_y, target = ulo, SUB, -2.0, flo
        else:
            table, depth, first_y, target = uhi, SUB, -2.0 + 2 * SUB, fhi
        span = {0: (0, wide), -1: (0, 4), 1: (wide - 4, wide)}[a]
        lanes_x = {0: (0, wide), -1: (0, 4), 1: (wide - 4, wide)}[a]
        swimmer_set(source, live_chunks, float(a * cx), float(b * cy), table, depth, first_y, span, target,
                    lanes_x, a == 0 and b == 0)

    for x in range(wide):
        fe[x, :, 0:SUB, :] += flo[x]
        fe[x, :, 2 * SUB : 3 * SUB, :] += fhi[x]

    base_row = SUB

    def prepared(rho, u0, force):
        half = 0.5 / rho
        u = [u0[c] + half * force[c] for c in range(3)]
        base = 1.0 - 1.5 * (u[0] * u[0] + u[1] * u[1] + u[2] * u[2])
        dotted = u[0] * force[0] + u[1] * force[1] + u[2] * force[2]
        return u, (base, dotted)

    for x in range(cx):
        for h in range(0, cy, SUB):
            force = [fe[x + 2, c, 2 + h : 2 + h + SUB, :] for c in range(3)]
            rho = mom[3, x, h : h + SUB, :]
            u, common = prepared(rho, [mom[c, x, h : h + SUB, :] for c in range(3)], force)
            for q in range(19):
                post[q, x + 1, base_row + h : base_row + h + SUB, :] = post_of(
                    q, pops[q, x, h : h + SUB, :], rho, u, force, common
                )
    for ref, row, at, layer, sign in ((from_left, 0, 1, 1, 1), (from_right, cx + 1, cx + 2, 0, -1)):
        force = [fe[at, c] for c in range(3)]
        rho = ref[6]
        u, common = prepared(rho, [ref[2 * c + layer] for c in range(3)], force)
        for k, q in enumerate(outward(0, sign)):
            post[q, row, base_row - 2 : base_row - 2 + YPAD, :] = post_of(q, ref[7 + k], rho, u, force, common)
    for ref, row, at, layer, sign in (
        (from_down, base_row - 1, 1, 1, 1),
        (from_up, base_row + cy, cy + 2, 0, -1),
    ):
        force = [fe[2 : 2 + cx, c, at, :] for c in range(3)]
        rho = ref[6]
        u, common = prepared(rho, [ref[2 * c + layer] for c in range(3)], force)
        for k, q in enumerate(outward(1, sign)):
            post[q, 1 : 1 + cx, row, :] = post_of(q, ref[7 + k], rho, u, force, common)
    for q in range(19):
        dx, dy, dz = lattice_dirs[q]
        for x in range(cx):
            plane = post[q, x + 1 - dx, base_row - dy : base_row - dy + cy, :]
            if dz != 0:
                plane = pltpu.roll(plane, dz % nz, 1)
            moved[q, x] = plane

    pacc[...] = jnp.zeros_like(pacc)
    own_chunks = lax.div(counts[0] + (LANES - 1), LANES)
    depth = float(nz)
    for (a, b, source), count in zip(sets, counts):
        live_chunks = lax.div(count + (LANES - 1), LANES)

        def ghost_step(g, carry, source=source, a=a, b=b):
            tile = source(g)
            flat = jnp.transpose(tile)
            gb[0] = jnp.broadcast_to(flat[:, 0:1] + float(a * cx), (LANES, LANES))
            gb[1] = jnp.broadcast_to(flat[:, 1:2] + float(b * cy), (LANES, LANES))
            gb[2] = jnp.broadcast_to(flat[:, 2:3], (LANES, LANES))

            def own_step(k, carry):
                tile = own_tile(k)
                px, py, pz = (jnp.broadcast_to(tile[c : c + 1], (SUB, LANES)) for c in range(3))
                total = [pacc[k, c] for c in range(3)]
                for r in range(0, LANES, SUB):
                    dx = px - gb[0, r : r + SUB, :]
                    dy = py - gb[1, r : r + SUB, :]
                    dz = pz - gb[2, r : r + SUB, :]
                    dz = dz - depth * jnp.round(dz * (1.0 / depth))
                    raw = dx * dx + dy * dy + dz * dz
                    inverse = pl.reciprocal(jnp.maximum(raw, floor_square), approx=False)
                    sixth = inverse * inverse * inverse
                    size = (48.0 * wca_energy) * (sixth * (sixth - 0.5)) * inverse
                    size = jnp.where(raw < cutoff_square, size, 0.0)
                    total[0] = total[0] + size * dx
                    total[1] = total[1] + size * dy
                    total[2] = total[2] + size * dz
                for c in range(3):
                    pacc[k, c] = total[c]
                return carry

            return lax.fori_loop(0, own_chunks, own_step, carry)

        lax.fori_loop(0, live_chunks, ghost_step, 0)

    for k in range(chunks):
        tile = own[STRIP + k]
        pair = jnp.sum(pacc[k], axis=1)
        value = jnp.where(tile[6:7] > 0.0, pair + sacc[k, 0:3, :], 0.0)
        out[0, 0, :, k * LANES : (k + 1) * LANES] = value


def shifted(value, axis, by):
    devices = lax.axis_size(axis)
    return lax.ppermute(value, axis, [(i, (i + by) % devices) for i in range(devices)])


def body(populations, anchor, offsets, heading, velocity, live_count):
    _, cx, cy, nz = populations.shape
    slots = anchor.shape[2]
    chunks = slots // LANES
    sizes = dict(cx=cx, cy=cy, nz=nz, slots=slots)
    vmem = pl.BlockSpec(memory_space=pltpu.VMEM)
    smem = pl.BlockSpec(memory_space=pltpu.SMEM)
    params = pltpu.CompilerParams(vmem_limit_bytes=40 * 2**20)
    shape = jax.ShapeDtypeStruct

    face_y = shape((STRIP + chunks, cx, nz), f32)
    mom, up, down = pl.pallas_call(
        functools.partial(pack_y, **sizes),
        out_shape=(shape((4, cx, cy, nz), f32), face_y, face_y),
        in_specs=[vmem] * 5 + [smem],
        out_specs=(vmem,) * 3,
        compiler_params=params,
        name="pack_y",
    )(populations, anchor, offsets, heading, velocity, live_count)
    from_down = shifted(up, "gy", 1)
    from_up = shifted(down, "gy", -1)

    face_x = shape((STRIP + 3 * (chunks // 3 + 1), YPAD, nz), f32)
    right, left = pl.pallas_call(
        functools.partial(pack_x, **sizes),
        out_shape=(face_x, face_x),
        in_specs=[vmem] * 5,
        out_specs=(vmem,) * 2,
        compiler_params=params,
        name="pack_x",
    )(populations, mom, up, from_down, from_up)
    from_left = shifted(right, "gx", 1)
    from_right = shifted(left, "gx", -1)

    wide = cx + 4
    moved, force = pl.pallas_call(
        functools.partial(main_kernel, **sizes),
        out_shape=(shape(populations.shape, f32), shape((1, 1, 3, slots), f32)),
        in_specs=[vmem] * 7,
        out_specs=(vmem,) * 2,
        scratch_shapes=[
            pltpu.VMEM((wide, 3, YPAD, nz), f32),
            pltpu.VMEM((wide * 3 * YPAD, 2 * nz), bf16),
            pltpu.VMEM((wide * 3 * SUB, 2 * nz), bf16),
            pltpu.VMEM((wide * 3 * SUB, 2 * nz), bf16),
            pltpu.VMEM((wide, 3, YPAD, nz), f32),
            pltpu.VMEM((wide, 3, SUB, nz), f32),
            pltpu.VMEM((wide, 3, SUB, nz), f32),
            pltpu.VMEM((19, cx + 2, cy + 2 * SUB, nz), f32),
            pltpu.VMEM((3, LANES, LANES), f32),
            pltpu.VMEM((chunks, 3, SUB, LANES), f32),
            pltpu.VMEM((chunks, SUB, LANES), f32),
        ],
        compiler_params=params,
        name="main",
    )(populations, mom, up, from_down, from_up, from_left, from_right)
    return moved, force


def solution(mesh):
    return jax.shard_map(
        body,
        mesh=mesh,
        in_specs=(
            P(None, "gx", "gy", None),
            P("gx", "gy", None),
            P("gx", "gy", None, None),
            P("gx", "gy", None, None),
            P("gx", "gy", None, None),
            P("gx", "gy"),
        ),
        out_specs=(P(None, "gx", "gy", None), P("gx", "gy", None, None)),
        check_vma=False,
    )
```

```python
import functools

import jax
import jax.numpy as jnp
from jax import lax
from jax.experimental import pallas as pl
from jax.experimental.pallas import tpu as pltpu
from jax.sharding import PartitionSpec as P

lattice_dirs = (
    (0, 0, 0),
    (1, 0, 0),
    (-1, 0, 0),
    (0, 1, 0),
    (0, -1, 0),
    (0, 0, 1),
    (0, 0, -1),
    (1, 1, 0),
    (-1, -1, 0),
    (1, -1, 0),
    (-1, 1, 0),
    (1, 0, 1),
    (-1, 0, -1),
    (1, 0, -1),
    (-1, 0, 1),
    (0, 1, 1),
    (0, -1, -1),
    (0, 1, -1),
    (0, -1, 1),
)
lattice_weights = (1.0 / 3.0,) + (1.0 / 18.0,) * 6 + (1.0 / 36.0,) * 12
relax_time = 0.8
friction = 2.0
propulsion = 0.5
wca_energy = 0.01
floor_square = 0.8
cutoff_square = 2.0 ** (1.0 / 3.0)

f32 = jnp.float32
bf16 = jnp.bfloat16
LANES = 128
SUB = 8
FAR = 1.0e9
YPAD = 24
STRIP = 12


def outward(axis, sign):
    return [q for q in range(19) if lattice_dirs[q][axis] == sign]


def split(value):
    high = value.astype(bf16)
    low = (value - high.astype(f32)).astype(bf16)
    return high, low


REACH = 1.1225


def moments_into(pops, mom):
    rho = pops[0]
    for q in range(1, 19):
        rho = rho + pops[q]
    inverse = 1.0 / rho
    mom[3] = rho
    for c in range(3):
        total = None
        for q in range(19):
            sign = lattice_dirs[q][c]
            if sign == 0:
                continue
            term = pops[q] if sign == 1 else -pops[q]
            total = term if total is None else total + term
        mom[c] = total * inverse


def thirds(fields):
    first = fields.astype(bf16).astype(f32)
    second = (fields - first).astype(bf16).astype(f32)
    third = fields - first - second
    return jnp.concatenate([first, second, third, jnp.zeros_like(first)], axis=0).astype(bf16)


def ranks_of(mask, chunks):
    rows = mask.shape[0]
    i = lax.broadcasted_iota(jnp.int32, (LANES, LANES), 0)
    j = lax.broadcasted_iota(jnp.int32, (LANES, LANES), 1)
    upper = jnp.where(i <= j, 1.0, 0.0).astype(bf16)
    ones = jnp.ones((LANES, LANES), bf16)
    held = mask.astype(bf16)
    inside = jnp.dot(held, upper, preferred_element_type=f32)
    total = jnp.dot(held, ones, preferred_element_type=f32)
    i = lax.broadcasted_iota(jnp.int32, (rows, rows), 0)
    j = lax.broadcasted_iota(jnp.int32, (rows, rows), 1)
    ahead = (i > j) & (lax.div(i, chunks) == lax.div(j, chunks))
    before = jnp.dot(jnp.where(ahead, 1.0, 0.0).astype(bf16), total.astype(bf16), preferred_element_type=f32)
    return jnp.where(mask > 0.5, inside + before - 1.0, -1.0)


def chunks_of(count):
    return lax.div(count + (LANES - 1), LANES)


def compact_into(put, parts, rank, count, chunks):
    def step(j, carry):
        rows = lax.broadcasted_iota(jnp.int32, (LANES, LANES), 0).astype(f32) + (j * LANES).astype(f32)
        chosen = [jnp.where(rows == rank[k : k + 1], 1.0, 0.0).astype(bf16) for k in range(chunks)]
        got = lax.dot_general(
            parts, jnp.concatenate(chosen, axis=1), (((1,), (1,)), ((), ())), preferred_element_type=f32
        )
        tile = got[0:8] + got[8:16] + got[16:24]
        row = lax.broadcasted_iota(jnp.int32, (SUB, LANES), 0)
        tile = jnp.where((row == 0) & (tile[6:7] < 0.5), FAR, tile)
        tile = jnp.where(row == 7, count.astype(f32), tile)
        put(j, tile)
        return carry

    step(jnp.int32(0), 0)
    lax.fori_loop(1, chunks_of(count), step, 0)


def pack_y(pops, anchor, swim, count, mom, own, ranks, up, down, fields, *, cx, cy, nz, slots):
    chunks = slots // LANES
    moments_into(pops, mom)
    for ref, rows, sign in ((up, (cy - 2, cy - 1), 1), (down, (0, 1), -1)):
        ring = cy - 1 if sign == 1 else 0
        for c in range(3):
            for k in range(2):
                ref[2 * c + k] = mom[c, :, rows[k], :]
        ref[6] = mom[3, :, ring, :]
        for k, q in enumerate(outward(1, sign)):
            ref[7 + k] = pops[q, :, ring, :]
    number = anchor[0].astype(f32)
    block_row = (cy + 2) * nz
    cell_x = jnp.floor((number + 0.5) * (1.0 / block_row))
    rest = number - cell_x * block_row
    cell_y = jnp.floor((rest + 0.5) * (1.0 / nz))
    cell_z = rest - cell_y * nz
    live = lax.broadcasted_iota(jnp.int32, (1, slots), 1) < count[0, 0]
    cosine = jnp.cos(swim[6:8])
    sine = jnp.sin(swim[6:8])
    rows = [
        jnp.where(live, cell_x - 1.0 + swim[0:1], FAR),
        cell_y - 1.0 + swim[1:2],
        cell_z + swim[2:3],
        friction * swim[3:4] - propulsion * cosine[0:1] * cosine[1:2],
        friction * swim[4:5] - propulsion * sine[0:1] * cosine[1:2],
        friction * swim[5:6] - propulsion * sine[1:2],
        live.astype(f32),
        jnp.full((1, slots), count[0, 0].astype(f32)),
    ]
    for f in range(8):
        fields[f : f + 1, :] = rows[f]
    for k in range(chunks):
        own[k] = fields[:, k * LANES : (k + 1) * LANES]
    place_x = own[:, 0, :]
    place_y = own[:, 1, :]
    alive = own[:, 6, :]
    masks = [
        jnp.where(place_y > cy - 1 - REACH, alive, 0.0),
        jnp.where(place_y < REACH, alive, 0.0),
        jnp.where(place_x > cx - 1 - REACH, alive, 0.0),
        jnp.where(place_x < REACH, alive, 0.0),
    ]
    place = ranks_of(jnp.concatenate(masks, axis=0), chunks)
    ranks[...] = place
    parts = thirds(fields[...])
    for n, ref in ((0, up), (1, down)):
        rank = place[n * chunks : (n + 1) * chunks]
        total = jnp.max(rank).astype(jnp.int32) + 1

        def put(j, tile, ref=ref):
            ref[STRIP + j] = tile

        compact_into(put, parts, rank, total, chunks)


def tent(length, first, place):
    cell = jnp.floor(place)
    part = place - cell
    rows = lax.broadcasted_iota(jnp.int32, (length, LANES), 0).astype(f32) + first
    return jnp.where(rows == cell, 1.0 - part, jnp.where(rows == cell + 1.0, part, 0.0))


def both(value, rows, padded=None):
    value = value.reshape(rows, LANES)
    if padded is not None:
        value = jnp.concatenate([value, jnp.zeros((padded - rows, LANES), f32)], axis=0)
    high, low = split(value)
    return jnp.concatenate([high, low], axis=1)


def along_z(tile, nz):
    high, low = split(tent(nz, 0.0, tile[2:3]))
    return high, low


def sample_table(high, low):
    top = jnp.concatenate([high, low], axis=1)
    return jnp.concatenate([top, top], axis=0)


def gather_rows(table, right):
    full = jnp.dot(table, right, preferred_element_type=f32)
    return full[:, :LANES] + full[:, LANES:]


def spread_rows(left, high, low):
    tall = jnp.concatenate([jnp.concatenate([high, high], axis=1), jnp.concatenate([low, low], axis=1)], axis=0)
    full = lax.dot_general(left, tall, (((1,), (1,)), ((), ())), preferred_element_type=f32)
    return full[:, :LANES] + full[:, LANES:]


def own_first(mom, own, ranks, part, sides, table, *, cx, cy, nz, slots):
    chunks = slots // LANES
    fields = jnp.concatenate([own[k] for k in range(chunks)], axis=1)
    parts = thirds(fields)
    for n in range(2):
        rank = ranks[(2 + n) * chunks : (3 + n) * chunks, :]
        total = jnp.max(rank).astype(jnp.int32) + 1

        def put(j, tile, n=n):
            sides[n, j] = tile

        compact_into(put, parts, rank, total, chunks)
    for c in range(3):
        table[c * cx * cy : (c + 1) * cx * cy, :] = both(mom[c], cx * cy)

    def step(k, carry):
        tile = own[k]
        right = sample_table(*along_z(tile, nz))
        wx = tent(cx, 0.0, tile[0:1])
        wy = tent(cy, 0.0, tile[1:2])
        for c in range(3):
            full = gather_rows(table[c * cx * cy : (c + 1) * cx * cy, :], right).reshape(cx, cy, LANES)
            total = full[0] * wx[0:1]
            for x in range(1, cx):
                total = total + full[x] * wx[x : x + 1]
            part[k, c : c + 1, :] = jnp.sum(total * wy, axis=0, keepdims=True)
        return carry

    count = jnp.max(own[0, 7:8, :]).astype(jnp.int32)
    lax.fori_loop(0, chunks_of(count), step, 0)


def pack_x(pops, mom, sides, from_down, from_up, right, left, *, cx, cy, nz, slots):
    chunks = slots // LANES
    for side, ref, cols, sign in ((0, right, (cx - 2, cx - 1), 1), (1, left, (0, 1), -1)):
        ring = cx - 1 if sign == 1 else 0
        names = outward(0, sign)
        zero = jnp.zeros((YPAD, LANES), f32)
        for f in range(STRIP):
            ref[f] = zero
        for c in range(3):
            for k in range(2):
                ref[2 * c + k, 2 : 2 + cy, :] = mom[c, cols[k]]
                ref[2 * c + k, 0:2, :] = from_down[2 * c : 2 * c + 2, cols[k], :]
                ref[2 * c + k, 2 + cy : 4 + cy, :] = from_up[2 * c : 2 * c + 2, cols[k], :]
        ref[6, 2 : 2 + cy, :] = mom[3, ring]
        ref[6, 1:2, :] = from_down[6, ring : ring + 1, :]
        ref[6, 2 + cy : 3 + cy, :] = from_up[6, ring : ring + 1, :]
        for k, q in enumerate(names):
            ref[7 + k, 2 : 2 + cy, :] = pops[q, ring]
            if lattice_dirs[q][1] == 1:
                at = 7 + outward(1, 1).index(q)
                ref[7 + k, 1:2, :] = from_down[at, ring : ring + 1, :]
            if lattice_dirs[q][1] == -1:
                at = 7 + outward(1, -1).index(q)
                ref[7 + k, 2 + cy : 3 + cy, :] = from_up[at, ring : ring + 1, :]
        for part in range(3):
            for k in range(chunks):
                tile = (sides[side, k], from_down[STRIP + k], from_up[STRIP + k])[part]
                ref[STRIP + part * (chunks // 3 + 1) + k // 3, (k % 3) * SUB : (k % 3 + 1) * SUB, :] = tile


def ghost_rows(gb, tile, at, shift_x, shift_y, nz):
    flat = jnp.transpose(tile)
    rows = pl.ds(pl.multiple_of(at, SUB), LANES)
    gb[0, rows, :] = jnp.broadcast_to(flat[:, 0:1] + shift_x, (LANES, LANES))
    gb[1, rows, :] = jnp.broadcast_to(flat[:, 1:2] + shift_y, (LANES, LANES))
    gb[2, rows, :] = jnp.broadcast_to(flat[:, 2:3] * (1.0 / nz), (LANES, LANES))


GROUP = 4


def pair_rows(gb, tile, rows, total, nz):
    px, py = (jnp.broadcast_to(tile[c : c + 1], (SUB, LANES)) for c in range(2))
    pz = jnp.broadcast_to(tile[2:3] * (1.0 / nz), (SUB, LANES))

    def step(g, total):
        fx, fy, fz = total
        for r in range(GROUP):
            at = pl.ds(pl.multiple_of((g * GROUP + r) * SUB, SUB), SUB)
            dx = px - gb[0, at, :]
            dy = py - gb[1, at, :]
            dz = pz - gb[2, at, :]
            dz = (dz - jnp.round(dz)) * float(nz)
            raw = dx * dx + dy * dy + dz * dz
            square = jnp.maximum(raw, floor_square)
            inverse = pl.reciprocal(square, approx=True)
            inverse = inverse * (2.0 - square * inverse)
            sixth = inverse * inverse * inverse
            size = (sixth * (sixth - 0.5)) * inverse
            size = jnp.where(raw < cutoff_square, size, 0.0)
            fx = fx + size * dx
            fy = fy + size * dy
            fz = fz + size * dz
        return fx, fy, fz

    return lax.fori_loop(0, rows, step, total)


def own_second(own, part, from_down, from_up, mom, spread_out, react_out, pairs, gb, ytable, *, cx, cy, nz, slots):
    chunks = slots // LANES
    count = jnp.max(own[0, 7:8, :]).astype(jnp.int32)
    live_chunks = chunks_of(count)
    wide = cx + 2
    ring = jnp.concatenate(
        [from_down[2 * c + 1] for c in range(3)] + [from_up[2 * c] for c in range(3)], axis=0
    )
    ytable[...] = both(ring, 6 * cx)
    spread_out[...] = jnp.zeros_like(spread_out)

    def step(k, carry):
        tile = own[k]
        high, low = along_z(tile, nz)
        wx = tent(wide + 6, -1.0, tile[0:1])
        wy = tent(YPAD, -2.0, tile[1:2])
        full = gather_rows(ytable[...], sample_table(high, low)).reshape(2, 3, cx, LANES)
        inner = tent(cx, 0.0, tile[0:1])
        lower = jnp.sum(full[0] * inner[None], axis=1) * wy[1:2]
        upper = jnp.sum(full[1] * inner[None], axis=1) * wy[cy + 2 : cy + 3]
        react = tile[3:6] - friction * (part[k, 0:3, :] + lower + upper)
        react_out[k, 0:3, :] = react
        react = react * tile[6:7]
        pieces = []
        for x in range(wide):
            for c in range(3):
                pieces.append((wx[x : x + 1] * react[c : c + 1]) * wy)
        left = both(jnp.stack(pieces), wide * 3 * YPAD)
        spread_out[...] += spread_rows(left, high, low).reshape(wide, 3, YPAD, LANES)
        return carry

    lax.fori_loop(0, live_chunks, step, 0)

    pairs[...] = jnp.zeros_like(pairs)

    def fill(k, carry):
        ghost_rows(gb, own[k], k * LANES, 0.0, 0.0, nz)
        return carry

    lax.fori_loop(0, live_chunks, fill, 0)
    groups = lax.div(count + (GROUP * SUB - 1), GROUP * SUB)

    def own_step(k, carry):
        zero = jnp.zeros((SUB, LANES), f32)
        total = pair_rows(gb, own[k], groups, (zero, zero, zero), nz)
        for c in range(3):
            pairs[k, c] = total[c]
        return carry

    lax.fori_loop(0, live_chunks, own_step, 0)


def post_of(q, pop, rho, u, force, common):
    c = lattice_dirs[q]
    w = lattice_weights[q]

    def dot(v):
        total = None
        for k in range(3):
            if c[k] == 0:
                continue
            term = v[k] if c[k] == 1 else -v[k]
            total = term if total is None else total + term
        return total

    base, dotted = common
    kept = (1.0 - 1.0 / relax_time) * pop
    scale = (1.0 - 0.5 / relax_time) * w
    if q == 0:
        return kept + (w / relax_time) * rho * base - (3.0 * scale) * dotted
    along = dot(u)
    pushed = dot(force)
    balance = (w / relax_time) * rho * (base + along * (3.0 + 4.5 * along))
    source = (3.0 * scale) * (pushed * (1.0 + 3.0 * along) - dotted)
    return kept + balance + source


def main_kernel(pops, mom, own, react_in, pairs, spread, from_down, from_up, from_left, from_right, moved, out,
                ext, tside, tflat, tcorner, xtable, flo, fhi, post, gb, sacc, fe, *, cx, cy, nz, slots):
    chunks = slots // LANES
    wide = cx + 2

    ext[...] = jnp.zeros_like(ext)
    for c in range(3):
        for x in range(cx):
            ext[x + 2, c, 0:2, :] = from_down[2 * c : 2 * c + 2, x, :]
            ext[x + 2, c, 2 + cy : 4 + cy, :] = from_up[2 * c : 2 * c + 2, x, :]
        for x in (0, 1, cx - 2, cx - 1):
            ext[x + 2, c, 2 : 2 + cy, :] = mom[c, x]
        for x in range(2, cx - 2):
            ext[x + 2, c, 2 : 2 + SUB - 2, :] = mom[c, x, 0 : SUB - 2, :]
            ext[x + 2, c, 2 * SUB : 2 + cy, :] = mom[c, x, 2 * SUB - 2 : cy, :]
        for k in range(2):
            ext[k, c] = from_left[2 * c + k]
            ext[cx + 2 + k, c] = from_right[2 * c + k]
    for n, x in ((0, 0), (1, cx + 1)):
        tside[n] = both(ext[x : x + 3], 9 * YPAD, 9 * YPAD + SUB)
        for m, y in ((0, 0), (1, 2 * SUB)):
            tcorner[2 * n + m] = both(ext[x : x + 3, :, y : y + SUB, :], 9 * SUB, 10 * SUB)
    for m, y in ((0, 0), (1, 2 * SUB)):
        tflat[m] = both(ext[1 : cx + 3, :, y : y + SUB, :], wide * 3 * SUB)
    xtable[...] = both(jnp.concatenate([ext[1:2], ext[cx + 2 : cx + 3]], axis=0), 6 * YPAD)
    fe[...] = spread[...]
    flo[...] = jnp.zeros_like(flo)
    fhi[...] = jnp.zeros_like(fhi)

    def scatter(react, wx, wy, high, low, slots_x, depth, target):
        pieces = []
        for _, w in slots_x:
            for c in range(3):
                pieces.append((wx[w : w + 1] * react[c : c + 1]) * wy)
        got = spread_rows(both(jnp.stack(pieces), len(slots_x) * 3 * depth), high, low)
        got = got.reshape(len(slots_x), 3, depth, LANES)
        for n, (f, _) in enumerate(slots_x):
            target[f] += got[n]

    def swimmer_list(source, count, shift_x, shift_y, table, rows, first_x, cols, depth, first_y, slots_x, target):
        def step(k, carry):
            tile = source(k)
            high, low = along_z(tile, nz)
            wx = tent(2 * SUB, first_x, tile[0:1] + shift_x)
            wy = tent(depth, first_y, tile[1:2] + shift_y)
            full = gather_rows(table(), sample_table(high, low))[:rows].reshape(cols, 3, depth, LANES)
            total = full[0] * wx[0:1]
            for x in range(1, cols):
                total = total + full[x] * wx[x : x + 1]
            react = tile[3:6] - friction * jnp.sum(total * wy[None], axis=1)
            react = react * tile[6:7]
            scatter(react, wx, wy, high, low, slots_x, depth, target)
            return carry

        step(0, 0)
        lax.fori_loop(1, chunks_of(count), step, 0)

    def y_tile(ref):
        return lambda k: ref[STRIP + k]

    def x_tile(ref, part):
        def at(k):
            row = lax.rem(k, 3) * SUB
            return ref[STRIP + part * (chunks // 3 + 1) + lax.div(k, 3), pl.ds(pl.multiple_of(row, SUB), SUB), :]

        def first(k):
            if isinstance(k, int):
                return ref[STRIP + part * (chunks // 3 + 1) + k // 3, (k % 3) * SUB : (k % 3 + 1) * SUB, :]
            return at(k)

        return first

    sets = [(0, -1, y_tile(from_down)), (0, 1, y_tile(from_up))]
    for a, ref in ((-1, from_left), (1, from_right)):
        for part, b in enumerate((0, -1, 1)):
            sets.append((a, b, x_tile(ref, part)))
    counts = [jnp.max(source(0)[7:8, :]).astype(jnp.int32) for _, _, source in sets]
    own_count = jnp.max(own[0, 7:8, :]).astype(jnp.int32)
    own_chunks = chunks_of(own_count)

    def own_step(k, carry):
        tile = own[k]
        high, low = along_z(tile, nz)
        wx = tent(2 * SUB, -1.0, tile[0:1])
        wy = tent(YPAD, -2.0, tile[1:2])
        full = gather_rows(xtable[...], sample_table(high, low)).reshape(2, 3, YPAD, LANES)
        total = full[0] * wx[0:1] + full[1] * wx[cx + 1 : cx + 2]
        extra = -friction * jnp.sum(total * wy[None], axis=1)
        sacc[k, 0:3, :] = -(react_in[k, 0:3, :] + extra)
        scatter(extra * tile[6:7], wx, wy, high, low, [(x, x) for x in (0, 1, cx, cx + 1)], YPAD, fe)
        return carry

    lax.fori_loop(0, own_chunks, own_step, 0)

    for (a, b, source), count in zip(sets, counts):
        side = 0 if a == -1 else 1
        half = 0 if b == -1 else 1
        if b == 0:
            depth, first_y, target = YPAD, -2.0, fe
        else:
            depth, first_y, target = SUB, -2.0 + 2 * SUB * half, (flo, fhi)[half]
        if a == 0:
            first_x, cols, slots_x = -1.0, wide, [(x, x) for x in range(wide)]
            table = lambda half=half: tflat[half]
        else:
            cols = 3
            first_x = -2.0 if a == -1 else float(cx - 1)
            slots_x = [(0, 1), (1, 2)] if a == -1 else [(cx, 0), (cx + 1, 1)]
            if b == 0:
                table = lambda side=side: tside[side]
            else:
                table = lambda at=2 * side + half: tcorner[at]
        swimmer_list(source, count, float(a * cx), float(b * cy), table, cols * 3 * depth, first_x, cols, depth,
                     first_y, slots_x, target)

    for x in range(wide):
        fe[x, :, 0:SUB, :] += flo[x]
        fe[x, :, 2 * SUB : 3 * SUB, :] += fhi[x]

    base_row = SUB

    def prepared(rho, u0, force):
        half = 0.5 / rho
        u = [u0[c] + half * force[c] for c in range(3)]
        base = 1.0 - 1.5 * (u[0] * u[0] + u[1] * u[1] + u[2] * u[2])
        dotted = u[0] * force[0] + u[1] * force[1] + u[2] * force[2]
        return u, (base, dotted)

    for x in range(cx):
        for h in range(0, cy, SUB):
            force = [fe[x + 1, c, 2 + h : 2 + h + SUB, :] for c in range(3)]
            rho = mom[3, x, h : h + SUB, :]
            u, common = prepared(rho, [mom[c, x, h : h + SUB, :] for c in range(3)], force)
            for q in range(19):
                post[q, x + 1, base_row + h : base_row + h + SUB, :] = post_of(
                    q, pops[q, x, h : h + SUB, :], rho, u, force, common
                )
    for ref, row, layer, sign in ((from_left, 0, 1, 1), (from_right, cx + 1, 0, -1)):
        force = [fe[row, c] for c in range(3)]
        rho = ref[6]
        u, common = prepared(rho, [ref[2 * c + layer] for c in range(3)], force)
        for k, q in enumerate(outward(0, sign)):
            post[q, row, base_row - 2 : base_row - 2 + YPAD, :] = post_of(q, ref[7 + k], rho, u, force, common)
    for ref, row, at, layer, sign in (
        (from_down, base_row - 1, 1, 1, 1),
        (from_up, base_row + cy, cy + 2, 0, -1),
    ):
        force = [fe[1 : 1 + cx, c, at, :] for c in range(3)]
        rho = ref[6]
        u, common = prepared(rho, [ref[2 * c + layer] for c in range(3)], force)
        for k, q in enumerate(outward(1, sign)):
            post[q, 1 : 1 + cx, row, :] = post_of(q, ref[7 + k], rho, u, force, common)
    for q in range(19):
        dx, dy, dz = lattice_dirs[q]
        for x in range(cx):
            plane = post[q, x + 1 - dx, base_row - dy : base_row - dy + cy, :]
            if dz != 0:
                plane = pltpu.roll(plane, dz % nz, 1)
            moved[q, x] = plane

    at = jnp.int32(0)
    for (a, b, source), count in zip(sets, counts):
        ghost_rows(gb, source(0), at, float(a * cx), float(b * cy), nz)

        def fill(k, carry, source=source, a=a, b=b, at=at):
            ghost_rows(gb, source(k), at + k * LANES, float(a * cx), float(b * cy), nz)
            return carry

        lax.fori_loop(1, chunks_of(count), fill, 0)
        at = at + lax.div(count + (SUB - 1), SUB) * SUB
    gb[0, pl.ds(pl.multiple_of(at, SUB), GROUP * SUB), :] = jnp.full((GROUP * SUB, LANES), FAR, f32)
    groups = lax.div(at + (GROUP * SUB - 1), GROUP * SUB)

    def pair_step(k, carry):
        total = pair_rows(gb, own[k], groups, tuple(pairs[k, c] for c in range(3)), nz)
        sums = jnp.concatenate([jnp.sum(t, axis=0, keepdims=True) for t in total], axis=0)
        sacc[k, 0:3, :] = sacc[k, 0:3, :] + (48.0 * wca_energy) * sums
        return carry

    lax.fori_loop(0, own_chunks, pair_step, 0)

    for k in range(chunks):
        value = jnp.where(own[k, 6:7, :] > 0.0, sacc[k, 0:3, :], 0.0)
        out[0, 0, :, k * LANES : (k + 1) * LANES] = value


def shifted(value, axis, by):
    devices = lax.axis_size(axis)
    return lax.ppermute(value, axis, [(i, (i + by) % devices) for i in range(devices)])


def body(populations, anchor, offsets, heading, velocity, live_count):
    _, cx, cy, nz = populations.shape
    slots = anchor.shape[2]
    chunks = slots // LANES
    sizes = dict(cx=cx, cy=cy, nz=nz, slots=slots)
    vmem = pl.BlockSpec(memory_space=pltpu.VMEM)
    smem = pl.BlockSpec(memory_space=pltpu.SMEM)
    shape = jax.ShapeDtypeStruct

    def call(kernel, name, outs, scratch, *args, last=vmem):
        return pl.pallas_call(
            functools.partial(kernel, **sizes),
            out_shape=outs,
            in_specs=[vmem] * (len(args) - 1) + [last],
            out_specs=(vmem,) * len(outs),
            scratch_shapes=scratch,
            compiler_params=pltpu.CompilerParams(vmem_limit_bytes=40 * 2**20),
            name=name,
        )(*args)

    swim = jnp.concatenate([offsets[0, 0], velocity[0, 0], heading[0, 0]], axis=0)
    face_y = shape((STRIP + chunks, cx, nz), f32)
    tiles = shape((chunks, SUB, LANES), f32)
    mom, own, ranks, up, down = call(
        pack_y, "pack_y",
        (shape((4, cx, cy, nz), f32), tiles, shape((4 * chunks, LANES), f32), face_y, face_y),
        [pltpu.VMEM((SUB, slots), f32)],
        populations, anchor, swim, live_count, last=smem,
    )
    from_down = shifted(up, "gy", 1)
    from_up = shifted(down, "gy", -1)
    part, sides = call(
        own_first, "own_first",
        (tiles, shape((2, chunks, SUB, LANES), f32)),
        [pltpu.VMEM((3 * cx * cy, 2 * nz), bf16)],
        mom, own, ranks,
    )
    face_x = shape((STRIP + 3 * (chunks // 3 + 1), YPAD, nz), f32)
    right, left = call(
        pack_x, "pack_x", (face_x, face_x), [], populations, mom, sides, from_down, from_up,
    )
    from_left = shifted(right, "gx", 1)
    from_right = shifted(left, "gx", -1)
    wide = cx + 2
    spread, react, pairs = call(
        own_second, "own_second",
        (shape((wide, 3, YPAD, nz), f32), tiles, shape((chunks, 3, SUB, LANES), f32)),
        [pltpu.VMEM((3, slots, LANES), f32), pltpu.VMEM((6 * cx, 2 * nz), bf16)],
        own, part, from_down, from_up, mom,
    )
    moved, force = call(
        main_kernel, "main",
        (shape(populations.shape, f32), shape((1, 1, 3, slots), f32)),
        [
            pltpu.VMEM((cx + 4, 3, YPAD, nz), f32),
            pltpu.VMEM((2, 9 * YPAD + SUB, 2 * nz), bf16),
            pltpu.VMEM((2, wide * 3 * SUB, 2 * nz), bf16),
            pltpu.VMEM((4, 10 * SUB, 2 * nz), bf16),
            pltpu.VMEM((6 * YPAD, 2 * nz), bf16),
            pltpu.VMEM((wide, 3, SUB, nz), f32),
            pltpu.VMEM((wide, 3, SUB, nz), f32),
            pltpu.VMEM((19, cx + 2, cy + 2 * SUB, nz), f32),
            pltpu.VMEM((3, 8 * slots + LANES, LANES), f32),
            pltpu.VMEM((chunks, SUB, LANES), f32),
            pltpu.VMEM((wide, 3, YPAD, nz), f32),
        ],
        populations, mom, own, react, pairs, spread, from_down, from_up, from_left, from_right,
    )
    return moved, force


def solution(mesh):
    return jax.shard_map(
        body,
        mesh=mesh,
        in_specs=(
            P(None, "gx", "gy", None),
            P("gx", "gy", None),
            P("gx", "gy", None, None),
            P("gx", "gy", None, None),
            P("gx", "gy", None, None),
            P("gx", "gy"),
        ),
        out_specs=(P(None, "gx", "gy", None), P("gx", "gy", None, None)),
        check_vma=False,
    )
```

```python
import functools

import jax
import jax.numpy as jnp
from jax import lax
from jax.experimental import pallas as pl
from jax.experimental.pallas import tpu as pltpu
from jax.sharding import PartitionSpec as P

lattice_dirs = (
    (0, 0, 0),
    (1, 0, 0),
    (-1, 0, 0),
    (0, 1, 0),
    (0, -1, 0),
    (0, 0, 1),
    (0, 0, -1),
    (1, 1, 0),
    (-1, -1, 0),
    (1, -1, 0),
    (-1, 1, 0),
    (1, 0, 1),
    (-1, 0, -1),
    (1, 0, -1),
    (-1, 0, 1),
    (0, 1, 1),
    (0, -1, -1),
    (0, 1, -1),
    (0, -1, 1),
)
lattice_weights = (1.0 / 3.0,) + (1.0 / 18.0,) * 6 + (1.0 / 36.0,) * 12
relax_time = 0.8
friction = 2.0
propulsion = 0.5
wca_energy = 0.01
floor_square = 0.8
cutoff_square = 2.0 ** (1.0 / 3.0)

f32 = jnp.float32
bf16 = jnp.bfloat16
LANES = 128
SUB = 8
FAR = 1.0e9
YPAD = 24
STRIP = 12


def outward(axis, sign):
    return [q for q in range(19) if lattice_dirs[q][axis] == sign]


def split(value):
    high = value.astype(bf16)
    low = (value - high.astype(f32)).astype(bf16)
    return high, low


REACH = 1.1225


def moments_into(pops, mom):
    rho = pops[0]
    for q in range(1, 19):
        rho = rho + pops[q]
    inverse = 1.0 / rho
    mom[3] = rho
    for c in range(3):
        total = None
        for q in range(19):
            sign = lattice_dirs[q][c]
            if sign == 0:
                continue
            term = pops[q] if sign == 1 else -pops[q]
            total = term if total is None else total + term
        mom[c] = total * inverse


def thirds(fields):
    first = fields.astype(bf16).astype(f32)
    second = (fields - first).astype(bf16).astype(f32)
    third = fields - first - second
    return jnp.concatenate([first, second, third, jnp.zeros_like(first)], axis=0).astype(bf16)


def ranks_of(mask, chunks):
    rows = mask.shape[0]
    i = lax.broadcasted_iota(jnp.int32, (LANES, LANES), 0)
    j = lax.broadcasted_iota(jnp.int32, (LANES, LANES), 1)
    upper = jnp.where(i <= j, 1.0, 0.0).astype(bf16)
    ones = jnp.ones((LANES, LANES), bf16)
    held = mask.astype(bf16)
    inside = jnp.dot(held, upper, preferred_element_type=f32)
    total = jnp.dot(held, ones, preferred_element_type=f32)
    i = lax.broadcasted_iota(jnp.int32, (rows, rows), 0)
    j = lax.broadcasted_iota(jnp.int32, (rows, rows), 1)
    ahead = (i > j) & (lax.div(i, chunks) == lax.div(j, chunks))
    before = jnp.dot(jnp.where(ahead, 1.0, 0.0).astype(bf16), total.astype(bf16), preferred_element_type=f32)
    return jnp.where(mask > 0.5, inside + before - 1.0, -1.0)


def chunks_of(count):
    return lax.div(count + (LANES - 1), LANES)


UNROLL = 2


def steps_of(count):
    return lax.div(count + (UNROLL * LANES - 1), UNROLL * LANES)


def compact_into(put, parts, rank, count, chunks):
    def step(j, carry):
        rows = lax.broadcasted_iota(jnp.int32, (LANES, LANES), 0).astype(f32) + (j * LANES).astype(f32)
        chosen = [jnp.where(rows == rank[k : k + 1], 1.0, 0.0).astype(bf16) for k in range(chunks)]
        got = lax.dot_general(
            parts, jnp.concatenate(chosen, axis=1), (((1,), (1,)), ((), ())), preferred_element_type=f32
        )
        tile = got[0:8] + got[8:16] + got[16:24]
        row = lax.broadcasted_iota(jnp.int32, (SUB, LANES), 0)
        tile = jnp.where((row == 0) & (tile[6:7] < 0.5), FAR, tile)
        tile = jnp.where(row == 7, count.astype(f32), tile)
        put(j, tile)
        return carry

    step(jnp.int32(0), 0)
    lax.fori_loop(1, chunks_of(count), step, 0)


def views(mix, cx, cy, nz, chunks):
    rows = 4 * cx * cy
    mom = mix.at[0:rows].reshape(4, cx, cy, nz)
    own = mix.at[rows : rows + SUB * chunks].reshape(chunks, SUB, LANES)
    ranks = mix.at[rows + SUB * chunks : rows + (SUB + 4) * chunks]
    rows = rows + (SUB + 4) * chunks
    return mom, own, ranks, mix.at[rows : rows + 10 * cy].reshape(10, cy, nz)


def pack_y(pops_in, anchor_in, offsets_in, heading_in, velocity_in, count, mix, up, down,
           pops, anchor, offsets, heading, velocity, angles, sems, *, cx, cy, nz, slots):
    chunks = slots // LANES
    mom, own, ranks, faces = views(mix, cx, cy, nz, chunks)
    copies = [
        pltpu.make_async_copy(source, target, sems.at[n])
        for n, (source, target) in enumerate(
            ((anchor_in, anchor), (offsets_in, offsets), (heading_in, heading), (velocity_in, velocity), (pops_in, pops))
        )
    ]
    for copy in copies:
        copy.start()
    for copy in copies[:4]:
        copy.wait()
    number = anchor[...].astype(f32)
    block_row = (cy + 2) * nz
    cell_x = jnp.floor((number + 0.5) * (1.0 / block_row))
    rest = number - cell_x * block_row
    cell_y = jnp.floor((rest + 0.5) * (1.0 / nz))
    cell_z = rest - cell_y * nz
    slot = lax.broadcasted_iota(jnp.int32, (chunks, LANES), 0) * LANES
    live = slot + lax.broadcasted_iota(jnp.int32, (chunks, LANES), 1) < count[0, 0]
    for n in range(2):
        for k in range(chunks):
            angles[n, k : k + 1, :] = heading[n : n + 1, k * LANES : (k + 1) * LANES]
    cosine = jnp.cos(angles[...])
    sine = jnp.sin(angles[...])
    alive = live.astype(f32)
    place_x = jnp.where(live, cell_x - 1.0 + offsets[0:chunks, :], FAR)
    place_y = cell_y - 1.0 + offsets[chunks : 2 * chunks, :]
    rows = [
        place_x,
        place_y,
        cell_z + offsets[2 * chunks : 3 * chunks, :],
        friction * velocity[0:chunks, :] - propulsion * cosine[0] * cosine[1],
        friction * velocity[chunks : 2 * chunks, :] - propulsion * sine[0] * cosine[1],
        friction * velocity[2 * chunks : 3 * chunks, :] - propulsion * sine[1],
        alive,
        jnp.full((chunks, LANES), count[0, 0].astype(f32)),
    ]
    for f in range(8):
        own[:, f, :] = rows[f]
    masks = [
        jnp.where(place_y > cy - 1 - REACH, alive, 0.0),
        jnp.where(place_y < REACH, alive, 0.0),
        jnp.where(place_x > cx - 1 - REACH, alive, 0.0),
        jnp.where(place_x < REACH, alive, 0.0),
    ]
    place = ranks_of(jnp.concatenate(masks, axis=0), chunks)
    ranks[...] = place
    parts = thirds(jnp.concatenate([own[k] for k in range(chunks)], axis=1))
    for n, ref in ((0, up), (1, down)):
        rank = place[n * chunks : (n + 1) * chunks]
        total = jnp.max(rank).astype(jnp.int32) + 1

        def put(j, tile, ref=ref):
            ref[STRIP + j] = tile

        compact_into(put, parts, rank, total, chunks)

    copies[4].wait()
    moments_into(pops, mom)
    for side, sign, ring in ((0, 1, cx - 1), (1, -1, 0)):
        for k, q in enumerate(outward(0, sign)):
            faces[5 * side + k] = pops[q, ring]
    for ref, rows, sign in ((up, (cy - 2, cy - 1), 1), (down, (0, 1), -1)):
        ring = cy - 1 if sign == 1 else 0
        for c in range(3):
            for k in range(2):
                ref[2 * c + k] = mom[c, :, rows[k], :]
        ref[6] = mom[3, :, ring, :]
        for k, q in enumerate(outward(1, sign)):
            ref[7 + k] = pops[q, :, ring, :]


def tent(length, first, place):
    cell = jnp.floor(place)
    part = place - cell
    rows = lax.broadcasted_iota(jnp.int32, (length, LANES), 0).astype(f32) + first
    return jnp.where(rows == cell, 1.0 - part, jnp.where(rows == cell + 1.0, part, 0.0))


def both(value, rows, padded=None):
    value = value.reshape(rows, LANES)
    if padded is not None:
        value = jnp.concatenate([value, jnp.zeros((padded - rows, LANES), f32)], axis=0)
    high, low = split(value)
    return jnp.concatenate([high, low], axis=1)


def along_z(tile, nz):
    high, low = split(tent(nz, 0.0, tile[2:3]))
    return high, low


def sample_table(high, low):
    top = jnp.concatenate([high, low], axis=1)
    return jnp.concatenate([top, top], axis=0)


def gather_rows(table, right):
    full = jnp.dot(table, right, preferred_element_type=f32)
    return full[:, :LANES] + full[:, LANES:]


def spread_many(lefts, highs, lows):
    tall = jnp.concatenate([jnp.concatenate(highs, axis=1), jnp.concatenate(lows, axis=1)], axis=0)
    left = jnp.concatenate(lefts, axis=1)
    full = lax.dot_general(left, tall, (((1,), (1,)), ((), ())), preferred_element_type=f32)
    return full[:, :LANES] + full[:, LANES:]


def spread_rows(left, high, low):
    return spread_many([left], [high, high], [low, low])


def own_first(mix, part, sides, table, *, cx, cy, nz, slots):
    chunks = slots // LANES
    mom, own, ranks, _ = views(mix, cx, cy, nz, chunks)
    fields = jnp.concatenate([own[k] for k in range(chunks)], axis=1)
    parts = thirds(fields)
    for n in range(2):
        rank = ranks[(2 + n) * chunks : (3 + n) * chunks, :]
        total = jnp.max(rank).astype(jnp.int32) + 1

        def put(j, tile, n=n):
            sides[n, j] = tile

        compact_into(put, parts, rank, total, chunks)
    for c in range(3):
        table[c * cx * cy : (c + 1) * cx * cy, :] = both(mom[c], cx * cy)

    def step(n, carry):
        for k in [n * UNROLL + u for u in range(UNROLL)]:
            tile = own[k]
            right = sample_table(*along_z(tile, nz))
            wx = tent(cx, 0.0, tile[0:1])
            wy = tent(cy, 0.0, tile[1:2])
            sums = []
            for c in range(3):
                full = gather_rows(table[c * cx * cy : (c + 1) * cx * cy, :], right).reshape(cx, cy, LANES)
                total = full[0] * wx[0:1]
                for x in range(1, cx):
                    total = total + full[x] * wx[x : x + 1]
                sums.append(jnp.sum(total * wy, axis=0, keepdims=True))
            part[k, 0:3, :] = jnp.concatenate(sums, axis=0)
        return carry

    count = jnp.max(own[0, 7:8, :]).astype(jnp.int32)
    lax.fori_loop(0, steps_of(count), step, 0)


def pack_x(mix, sides, from_down, from_up, right, left, *, cx, cy, nz, slots):
    chunks = slots // LANES
    mom, _, _, faces = views(mix, cx, cy, nz, chunks)
    for side, ref, cols, sign in ((0, right, (cx - 2, cx - 1), 1), (1, left, (0, 1), -1)):
        ring = cx - 1 if sign == 1 else 0
        names = outward(0, sign)
        zero = jnp.zeros((YPAD, LANES), f32)
        for f in range(STRIP):
            ref[f] = zero
        for c in range(3):
            for k in range(2):
                ref[2 * c + k, 2 : 2 + cy, :] = mom[c, cols[k]]
                ref[2 * c + k, 0:2, :] = from_down[2 * c : 2 * c + 2, cols[k], :]
                ref[2 * c + k, 2 + cy : 4 + cy, :] = from_up[2 * c : 2 * c + 2, cols[k], :]
        ref[6, 2 : 2 + cy, :] = mom[3, ring]
        ref[6, 1:2, :] = from_down[6, ring : ring + 1, :]
        ref[6, 2 + cy : 3 + cy, :] = from_up[6, ring : ring + 1, :]
        for k, q in enumerate(names):
            ref[7 + k, 2 : 2 + cy, :] = faces[5 * side + k]
            if lattice_dirs[q][1] == 1:
                at = 7 + outward(1, 1).index(q)
                ref[7 + k, 1:2, :] = from_down[at, ring : ring + 1, :]
            if lattice_dirs[q][1] == -1:
                at = 7 + outward(1, -1).index(q)
                ref[7 + k, 2 + cy : 3 + cy, :] = from_up[at, ring : ring + 1, :]
        for part in range(3):
            for k in range(chunks):
                tile = (sides[side, k], from_down[STRIP + k], from_up[STRIP + k])[part]
                ref[STRIP + part * (chunks // 3 + 1) + k // 3, (k % 3) * SUB : (k % 3 + 1) * SUB, :] = tile


def ghost_rows(gb, tile, at, shift_x, shift_y, nz):
    flat = jnp.transpose(tile)
    rows = pl.ds(pl.multiple_of(at, SUB), LANES)
    gb[0, rows, :] = jnp.broadcast_to(flat[:, 0:1] + shift_x, (LANES, LANES))
    gb[1, rows, :] = jnp.broadcast_to(flat[:, 1:2] + shift_y, (LANES, LANES))
    gb[2, rows, :] = jnp.broadcast_to(flat[:, 2:3] * (1.0 / nz), (LANES, LANES))


GROUP = 16


def pair_rows(gb, tile, rows, total, nz):
    px, py = (jnp.broadcast_to(tile[c : c + 1], (SUB, LANES)) for c in range(2))
    pz = jnp.broadcast_to(tile[2:3] * (1.0 / nz), (SUB, LANES))

    def step(g, total):
        fx, fy, fz = total
        for r in range(GROUP):
            at = pl.ds(pl.multiple_of((g * GROUP + r) * SUB, SUB), SUB)
            dx = px - gb[0, at, :]
            dy = py - gb[1, at, :]
            dz = pz - gb[2, at, :]
            dz = (dz - jnp.round(dz)) * float(nz)
            raw = dx * dx + dy * dy + dz * dz
            square = jnp.maximum(raw, floor_square)
            inverse = pl.reciprocal(square, approx=True)
            inverse = inverse * (2.0 - square * inverse)
            sixth = inverse * inverse * inverse
            size = (sixth * (sixth - 0.5)) * inverse
            size = jnp.where(raw < cutoff_square, size, 0.0)
            fx = fx + size * dx
            fy = fy + size * dy
            fz = fz + size * dz
        return fx, fy, fz

    return lax.fori_loop(0, rows, step, total)


def own_second(mix, part, from_down, from_up, spread_out, react_out, pairs, gb, ytable, *, cx, cy, nz, slots):
    chunks = slots // LANES
    _, own, _, _ = views(mix, cx, cy, nz, chunks)
    count = jnp.max(own[0, 7:8, :]).astype(jnp.int32)
    live_chunks = chunks_of(count)
    wide = cx + 2
    ring = jnp.concatenate(
        [from_down[2 * c + 1] for c in range(3)] + [from_up[2 * c] for c in range(3)], axis=0
    )
    ytable[...] = both(ring, 6 * cx)
    spread_out[...] = jnp.zeros_like(spread_out)

    def step(n, carry):
        lefts, highs, lows = [], [], []
        for k in [n * UNROLL + u for u in range(UNROLL)]:
            tile = own[k]
            high, low = along_z(tile, nz)
            wx = tent(wide + 6, -1.0, tile[0:1])
            wy = tent(YPAD, -2.0, tile[1:2])
            full = gather_rows(ytable[...], sample_table(high, low)).reshape(2, 3, cx, LANES)
            inner = tent(cx, 0.0, tile[0:1])
            lower = jnp.sum(full[0] * inner[None], axis=1) * wy[1:2]
            upper = jnp.sum(full[1] * inner[None], axis=1) * wy[cy + 2 : cy + 3]
            react = tile[3:6] - friction * (part[k, 0:3, :] + lower + upper)
            react_out[k, 0:3, :] = react
            react = react * tile[6:7]
            pieces = []
            for x in range(wide):
                for c in range(3):
                    pieces.append((wx[x : x + 1] * react[c : c + 1]) * wy)
            lefts.append(both(jnp.stack(pieces), wide * 3 * YPAD))
            highs += [high, high]
            lows += [low, low]
        spread_out[...] += spread_many(lefts, highs, lows).reshape(wide, 3, YPAD, LANES)
        return carry

    lax.fori_loop(0, steps_of(count), step, 0)

    pairs[...] = jnp.zeros_like(pairs)

    def fill(k, carry):
        ghost_rows(gb, own[k], k * LANES, 0.0, 0.0, nz)
        return carry

    lax.fori_loop(0, live_chunks, fill, 0)
    groups = lax.div(count + (GROUP * SUB - 1), GROUP * SUB)

    def own_step(k, carry):
        zero = jnp.zeros((SUB, LANES), f32)
        total = pair_rows(gb, own[k], groups, (zero, zero, zero), nz)
        for c in range(3):
            pairs[k, c] = total[c]
        return carry

    lax.fori_loop(0, live_chunks, own_step, 0)


def post_of(q, pop, rho, u, force, common):
    c = lattice_dirs[q]
    w = lattice_weights[q]

    def dot(v):
        total = None
        for k in range(3):
            if c[k] == 0:
                continue
            term = v[k] if c[k] == 1 else -v[k]
            total = term if total is None else total + term
        return total

    base, dotted = common
    kept = (1.0 - 1.0 / relax_time) * pop
    scale = (1.0 - 0.5 / relax_time) * w
    if q == 0:
        return kept + (w / relax_time) * rho * base - (3.0 * scale) * dotted
    along = dot(u)
    pushed = dot(force)
    balance = (w / relax_time) * rho * (base + along * (3.0 + 4.5 * along))
    source = (3.0 * scale) * (pushed * (1.0 + 3.0 * along) - dotted)
    return kept + balance + source


def main_kernel(pops, mix, sides, react_in, pairs, spread, from_down, from_up, from_left, from_right, moved_out, out,
                moved, sems, ext, tside, tflat, tcorner, xtable, flo, fhi, post, gb, sacc, fe, *, cx, cy, nz, slots):
    chunks = slots // LANES
    wide = cx + 2
    mom, own, _, _ = views(mix, cx, cy, nz, chunks)

    ext[...] = jnp.zeros_like(ext)
    for c in range(3):
        for x in range(cx):
            ext[x + 2, c, 0:2, :] = from_down[2 * c : 2 * c + 2, x, :]
            ext[x + 2, c, 2 + cy : 4 + cy, :] = from_up[2 * c : 2 * c + 2, x, :]
        for x in (0, 1, cx - 2, cx - 1):
            ext[x + 2, c, 2 : 2 + cy, :] = mom[c, x]
        for x in range(2, cx - 2):
            ext[x + 2, c, 2 : 2 + SUB - 2, :] = mom[c, x, 0 : SUB - 2, :]
            ext[x + 2, c, 2 * SUB : 2 + cy, :] = mom[c, x, 2 * SUB - 2 : cy, :]
        for k in range(2):
            ext[k, c] = from_left[2 * c + k]
            ext[cx + 2 + k, c] = from_right[2 * c + k]
    for n, x in ((0, 0), (1, cx + 1)):
        tside[n] = both(ext[x : x + 3], 9 * YPAD, 9 * YPAD + SUB)
        for m, y in ((0, 0), (1, 2 * SUB)):
            tcorner[2 * n + m] = both(ext[x : x + 3, :, y : y + SUB, :], 9 * SUB, 10 * SUB)
    for m, y in ((0, 0), (1, 2 * SUB)):
        tflat[m] = both(ext[1 : cx + 3, :, y : y + SUB, :], wide * 3 * SUB)
    xtable[...] = both(jnp.concatenate([ext[1:2], ext[cx + 2 : cx + 3]], axis=0), 6 * YPAD)
    fe[...] = spread[...]
    flo[...] = jnp.zeros_like(flo)
    fhi[...] = jnp.zeros_like(fhi)

    def y_tile(ref):
        return lambda k: ref[STRIP + k]

    def x_tile(ref, part):
        def at(k):
            row = lax.rem(k, 3) * SUB
            return ref[STRIP + part * (chunks // 3 + 1) + lax.div(k, 3), pl.ds(pl.multiple_of(row, SUB), SUB), :]

        def first(k):
            if isinstance(k, int):
                return ref[STRIP + part * (chunks // 3 + 1) + k // 3, (k % 3) * SUB : (k % 3 + 1) * SUB, :]
            return at(k)

        return first

    sets = [(0, -1, y_tile(from_down)), (0, 1, y_tile(from_up))]
    for a, ref in ((-1, from_left), (1, from_right)):
        for part, b in enumerate((0, -1, 1)):
            sets.append((a, b, x_tile(ref, part)))
    counts = [jnp.max(source(0)[7:8, :]).astype(jnp.int32) for _, _, source in sets]
    own_count = jnp.max(own[0, 7:8, :]).astype(jnp.int32)
    own_chunks = chunks_of(own_count)

    def own_step(n, carry):
        for k in [n * UNROLL + u for u in range(UNROLL)]:
            tile = own[k]
            wx = tent(2 * SUB, -1.0, tile[0:1])
            wy = tent(YPAD, -2.0, tile[1:2])
            full = gather_rows(xtable[...], sample_table(*along_z(tile, nz))).reshape(2, 3, YPAD, LANES)
            total = full[0] * wx[0:1] + full[1] * wx[cx + 1 : cx + 2]
            sacc[k, 0:3, :] = friction * jnp.sum(total * wy[None], axis=1) - react_in[k, 0:3, :]
        return carry

    lax.fori_loop(0, steps_of(own_count), own_step, 0)

    jobs = []
    for (a, b, source), count in zip(sets, counts):
        side = 0 if a == -1 else 1
        half = 0 if b == -1 else 1
        if b == 0:
            depth, first_y, target = YPAD, -2.0, fe
        else:
            depth, first_y, target = SUB, -2.0 + 2 * SUB * half, (flo, fhi)[half]
        if a == 0:
            first_x, cols, slots_x = -1.0, wide, [(x, x) for x in range(wide)]
            table = tflat.at[half]
        else:
            cols = 3
            first_x = -2.0 if a == -1 else float(cx - 1)
            slots_x = [(0, 1), (1, 2)] if a == -1 else [(cx, 0), (cx + 1, 1)]
            table = tside.at[side] if b == 0 else tcorner.at[2 * side + half]
        jobs.append((source, count, float(a * cx), float(b * cy), table, cols, first_x, depth, first_y, slots_x,
                     target, False))
    for side, n in ((0, 1), (1, 0)):
        first_x = -2.0 if side == 0 else float(cx - 1)
        slots_x = [(0, 1), (1, 2)] if side == 0 else [(cx, 0), (cx + 1, 1)]
        source = lambda k, n=n: sides[n, k]
        count = jnp.max(sides[n, 0, 7:8, :]).astype(jnp.int32)
        jobs.append((source, count, 0.0, 0.0, xtable, 1, first_x, YPAD, -2.0, slots_x, fe, True))

    def reaction(job, k):
        source, _, shift_x, shift_y, table, cols, first_x, depth, first_y, _, _, own_list = job
        tile = source(k)
        high, low = along_z(tile, nz)
        wx = tent(2 * SUB, first_x, tile[0:1] + shift_x)
        wy = tent(depth, first_y, tile[1:2] + shift_y)
        right = sample_table(high, low)
        if own_list:
            at = 0 if first_x < 0.0 else 3 * YPAD
            row = 1
            full = gather_rows(xtable[...], right)[at : at + 3 * YPAD].reshape(1, 3, YPAD, LANES)
            total = full[0] * wx[row : row + 1]
            react = -friction * jnp.sum(total * wy[None], axis=1)
        else:
            full = gather_rows(table[...], right)[: cols * 3 * depth].reshape(cols, 3, depth, LANES)
            total = full[0] * wx[0:1]
            for x in range(1, cols):
                total = total + full[x] * wx[x : x + 1]
            react = tile[3:6] - friction * jnp.sum(total * wy[None], axis=1)
        return react * tile[6:7], wx, wy, high, low

    def spread_job(job, parts):
        react, wx, wy, high, low = parts
        depth, slots_x = job[7], job[9]
        pieces = []
        for _, w in slots_x:
            for c in range(3):
                pieces.append((wx[w : w + 1] * react[c : c + 1]) * wy)
        got = spread_rows(both(jnp.stack(pieces), len(slots_x) * 3 * depth), high, low)
        return got.reshape(len(slots_x), 3, depth, LANES)

    def add_job(job, got):
        for n, (f, _) in enumerate(job[9]):
            job[10][f] += got[n]

    parts = [reaction(job, 0) for job in jobs]
    gots = [spread_job(job, part) for job, part in zip(jobs, parts)]
    for job, got in zip(jobs, gots):
        add_job(job, got)
    for job in jobs:

        def more(k, carry, job=job):
            add_job(job, spread_job(job, reaction(job, k)))
            return carry

        lax.fori_loop(1, chunks_of(job[1]), more, 0)

    for x in range(wide):
        fe[x, :, 0:SUB, :] += flo[x]
        fe[x, :, 2 * SUB : 3 * SUB, :] += fhi[x]

    base_row = SUB

    def prepared(rho, u0, force):
        half = 0.5 / rho
        u = [u0[c] + half * force[c] for c in range(3)]
        base = 1.0 - 1.5 * (u[0] * u[0] + u[1] * u[1] + u[2] * u[2])
        dotted = u[0] * force[0] + u[1] * force[1] + u[2] * force[2]
        return u, (base, dotted)

    for x in range(cx):
        for h in range(0, cy, SUB):
            force = [fe[x + 1, c, 2 + h : 2 + h + SUB, :] for c in range(3)]
            rho = mom[3, x, h : h + SUB, :]
            u, common = prepared(rho, [mom[c, x, h : h + SUB, :] for c in range(3)], force)
            for q in range(19):
                post[q, x + 1, base_row + h : base_row + h + SUB, :] = post_of(
                    q, pops[q, x, h : h + SUB, :], rho, u, force, common
                )
    for ref, row, layer, sign in ((from_left, 0, 1, 1), (from_right, cx + 1, 0, -1)):
        force = [fe[row, c] for c in range(3)]
        rho = ref[6]
        u, common = prepared(rho, [ref[2 * c + layer] for c in range(3)], force)
        for k, q in enumerate(outward(0, sign)):
            post[q, row, base_row - 2 : base_row - 2 + YPAD, :] = post_of(q, ref[7 + k], rho, u, force, common)
    for ref, row, at, layer, sign in (
        (from_down, base_row - 1, 1, 1, 1),
        (from_up, base_row + cy, cy + 2, 0, -1),
    ):
        force = [fe[1 : 1 + cx, c, at, :] for c in range(3)]
        rho = ref[6]
        u, common = prepared(rho, [ref[2 * c + layer] for c in range(3)], force)
        for k, q in enumerate(outward(1, sign)):
            post[q, 1 : 1 + cx, row, :] = post_of(q, ref[7 + k], rho, u, force, common)
    copies = []
    for q in range(19):
        dx, dy, dz = lattice_dirs[q]
        for x in range(cx):
            plane = post[q, x + 1 - dx, base_row - dy : base_row - dy + cy, :]
            if dz != 0:
                plane = pltpu.roll(plane, dz % nz, 1)
            moved[q, x] = plane
        copies.append(pltpu.make_async_copy(moved.at[q], moved_out.at[q], sems.at[q]))
        copies[-1].start()

    at = jnp.int32(0)
    for (a, b, source), count in zip(sets, counts):
        ghost_rows(gb, source(0), at, float(a * cx), float(b * cy), nz)

        def fill(k, carry, source=source, a=a, b=b, at=at):
            ghost_rows(gb, source(k), at + k * LANES, float(a * cx), float(b * cy), nz)
            return carry

        lax.fori_loop(1, chunks_of(count), fill, 0)
        at = at + lax.div(count + (SUB - 1), SUB) * SUB
    gb[0, pl.ds(pl.multiple_of(at, SUB), GROUP * SUB), :] = jnp.full((GROUP * SUB, LANES), FAR, f32)
    groups = lax.div(at + (GROUP * SUB - 1), GROUP * SUB)

    def pair_step(k, carry):
        total = pair_rows(gb, own[k], groups, tuple(pairs[k, c] for c in range(3)), nz)
        sums = jnp.concatenate([jnp.sum(t, axis=0, keepdims=True) for t in total], axis=0)
        sacc[k, 0:3, :] = sacc[k, 0:3, :] + (48.0 * wca_energy) * sums
        return carry

    lax.fori_loop(0, own_chunks, pair_step, 0)

    for c in range(3):
        out[c * chunks : (c + 1) * chunks, :] = jnp.where(own[:, 6, :] > 0.0, sacc[:, c, :], 0.0)
    for copy in copies:
        copy.wait()


def shifted(value, axis, by):
    devices = lax.axis_size(axis)
    return lax.ppermute(value, axis, [(i, (i + by) % devices) for i in range(devices)])


def body(populations, anchor, offsets, heading, velocity, live_count):
    _, cx, cy, nz = populations.shape
    slots = anchor.shape[2]
    chunks = slots // LANES
    sizes = dict(cx=cx, cy=cy, nz=nz, slots=slots)
    vmem = pl.BlockSpec(memory_space=pltpu.VMEM)
    smem = pl.BlockSpec(memory_space=pltpu.SMEM)
    shape = jax.ShapeDtypeStruct

    hbm = pl.BlockSpec(memory_space=pltpu.HBM)

    def call(kernel, name, outs, scratch, *args, ins=None, out_specs=None, limit=48):
        return pl.pallas_call(
            functools.partial(kernel, **sizes),
            out_shape=outs,
            in_specs=ins or [vmem] * len(args),
            out_specs=out_specs or (vmem,) * len(outs),
            scratch_shapes=scratch,
            compiler_params=pltpu.CompilerParams(vmem_limit_bytes=limit * 2**20),
            name=name,
        )(*args)

    face_y = shape((STRIP + chunks, cx, nz), f32)
    tiles = shape((chunks, SUB, LANES), f32)
    dma = pltpu.SemaphoreType.DMA
    mix, up, down = call(
        pack_y, "pack_y",
        (shape((4 * cx * cy + (SUB + 4) * chunks + 10 * cy, LANES), f32), face_y, face_y),
        [
            pltpu.VMEM(populations.shape, f32),
            pltpu.VMEM((chunks, LANES), jnp.int32),
            pltpu.VMEM((3 * chunks, LANES), f32),
            pltpu.VMEM((2, slots), f32),
            pltpu.VMEM((3 * chunks, LANES), f32),
            pltpu.VMEM((2, chunks, LANES), f32),
            dma((5,)),
        ],
        populations, anchor.reshape(chunks, LANES), offsets.reshape(3 * chunks, LANES), heading[0, 0],
        velocity.reshape(3 * chunks, LANES), live_count, ins=[hbm] * 5 + [smem], limit=62,
    )
    from_down = shifted(up, "gy", 1)
    from_up = shifted(down, "gy", -1)
    part, sides = call(
        own_first, "own_first",
        (tiles, shape((2, chunks, SUB, LANES), f32)),
        [pltpu.VMEM((3 * cx * cy, 2 * nz), bf16)],
        mix,
    )
    face_x = shape((STRIP + 3 * (chunks // 3 + 1), YPAD, nz), f32)
    right, left = call(
        pack_x, "pack_x", (face_x, face_x), [], mix, sides, from_down, from_up,
    )
    from_left = shifted(right, "gx", 1)
    from_right = shifted(left, "gx", -1)
    wide = cx + 2
    spread, react, pairs = call(
        own_second, "own_second",
        (shape((wide, 3, YPAD, nz), f32), tiles, shape((chunks, 3, SUB, LANES), f32)),
        [pltpu.VMEM((3, slots, LANES), f32), pltpu.VMEM((6 * cx, 2 * nz), bf16)],
        mix, part, from_down, from_up,
    )
    moved, force = call(
        main_kernel, "main",
        (shape(populations.shape, f32), shape((3 * chunks, LANES), f32)),
        [
            pltpu.VMEM(populations.shape, f32),
            dma((19,)),
            pltpu.VMEM((cx + 4, 3, YPAD, nz), f32),
            pltpu.VMEM((2, 9 * YPAD + SUB, 2 * nz), bf16),
            pltpu.VMEM((2, wide * 3 * SUB, 2 * nz), bf16),
            pltpu.VMEM((4, 10 * SUB, 2 * nz), bf16),
            pltpu.VMEM((6 * YPAD, 2 * nz), bf16),
            pltpu.VMEM((wide, 3, SUB, nz), f32),
            pltpu.VMEM((wide, 3, SUB, nz), f32),
            pltpu.VMEM((19, cx + 2, cy + 2 * SUB, nz), f32),
            pltpu.VMEM((3, 8 * slots + LANES, LANES), f32),
            pltpu.VMEM((chunks, SUB, LANES), f32),
            pltpu.VMEM((wide, 3, YPAD, nz), f32),
        ],
        populations, mix, sides, react, pairs, spread, from_down, from_up, from_left, from_right,
        out_specs=(hbm, vmem),
    )
    return moved, force.reshape(1, 1, 3, slots)


def solution(mesh):
    return jax.shard_map(
        body,
        mesh=mesh,
        in_specs=(
            P(None, "gx", "gy", None),
            P("gx", "gy", None),
            P("gx", "gy", None, None),
            P("gx", "gy", None, None),
            P("gx", "gy", None, None),
            P("gx", "gy"),
        ),
        out_specs=(P(None, "gx", "gy", None), P("gx", "gy", None, None)),
        check_vma=False,
    )
```

```python
import functools

import jax
import jax.numpy as jnp
from jax import lax
from jax.experimental import pallas as pl
from jax.experimental.pallas import tpu as pltpu
from jax.sharding import PartitionSpec as P

lattice_dirs = (
    (0, 0, 0),
    (1, 0, 0),
    (-1, 0, 0),
    (0, 1, 0),
    (0, -1, 0),
    (0, 0, 1),
    (0, 0, -1),
    (1, 1, 0),
    (-1, -1, 0),
    (1, -1, 0),
    (-1, 1, 0),
    (1, 0, 1),
    (-1, 0, -1),
    (1, 0, -1),
    (-1, 0, 1),
    (0, 1, 1),
    (0, -1, -1),
    (0, 1, -1),
    (0, -1, 1),
)
lattice_weights = (1.0 / 3.0,) + (1.0 / 18.0,) * 6 + (1.0 / 36.0,) * 12
relax_time = 0.8
friction = 2.0
propulsion = 0.5
wca_energy = 0.01
floor_square = 0.8
cutoff_square = 2.0 ** (1.0 / 3.0)

f32 = jnp.float32
bf16 = jnp.bfloat16
LANES = 128
SUB = 8
FAR = 1.0e9
YPAD = 24
STRIP = 12


def outward(axis, sign):
    return [q for q in range(19) if lattice_dirs[q][axis] == sign]


def split(value):
    high = value.astype(bf16)
    low = (value - high.astype(f32)).astype(bf16)
    return high, low


REACH = 1.1225


def moments_into(pops, mom):
    rho = pops[0]
    for q in range(1, 19):
        rho = rho + pops[q]
    inverse = 1.0 / rho
    mom[3] = rho
    for c in range(3):
        total = None
        for q in range(19):
            sign = lattice_dirs[q][c]
            if sign == 0:
                continue
            term = pops[q] if sign == 1 else -pops[q]
            total = term if total is None else total + term
        mom[c] = total * inverse


def thirds(fields):
    first = fields.astype(bf16).astype(f32)
    second = (fields - first).astype(bf16).astype(f32)
    third = fields - first - second
    return jnp.concatenate([first, second, third, jnp.zeros_like(first)], axis=0).astype(bf16)


def ranks_of(mask, chunks):
    rows = mask.shape[0]
    i = lax.broadcasted_iota(jnp.int32, (LANES, LANES), 0)
    j = lax.broadcasted_iota(jnp.int32, (LANES, LANES), 1)
    upper = jnp.where(i <= j, 1.0, 0.0).astype(bf16)
    ones = jnp.ones((LANES, LANES), bf16)
    held = mask.astype(bf16)
    inside = jnp.dot(held, upper, preferred_element_type=f32)
    total = jnp.dot(held, ones, preferred_element_type=f32)
    i = lax.broadcasted_iota(jnp.int32, (rows, rows), 0)
    j = lax.broadcasted_iota(jnp.int32, (rows, rows), 1)
    ahead = (i > j) & (lax.div(i, chunks) == lax.div(j, chunks))
    before = jnp.dot(jnp.where(ahead, 1.0, 0.0).astype(bf16), total.astype(bf16), preferred_element_type=f32)
    return jnp.where(mask > 0.5, inside + before - 1.0, -1.0)


def chunks_of(count):
    return lax.div(count + (LANES - 1), LANES)


UNROLL = 4


def steps_of(count):
    return lax.div(count + (UNROLL * LANES - 1), UNROLL * LANES)


def compact_into(put, parts, rank, count, chunks):
    def step(j, carry):
        rows = lax.broadcasted_iota(jnp.int32, (LANES, LANES), 0).astype(f32) + (j * LANES).astype(f32)
        chosen = [jnp.where(rows == rank[k : k + 1], 1.0, 0.0).astype(bf16) for k in range(chunks)]
        got = lax.dot_general(
            parts, jnp.concatenate(chosen, axis=1), (((1,), (1,)), ((), ())), preferred_element_type=f32
        )
        tile = got[0:8] + got[8:16] + got[16:24]
        row = lax.broadcasted_iota(jnp.int32, (SUB, LANES), 0)
        tile = jnp.where((row == 0) & (tile[6:7] < 0.5), FAR, tile)
        tile = jnp.where(row == 7, count.astype(f32), tile)
        put(j, tile)
        return carry

    step(jnp.int32(0), 0)
    lax.fori_loop(1, chunks_of(count), step, 0)


def views(mix, cx, cy, nz, chunks):
    rows = 4 * cx * cy
    mom = mix.at[0:rows].reshape(4, cx, cy, nz)
    own = mix.at[rows : rows + SUB * chunks].reshape(chunks, SUB, LANES)
    ranks = mix.at[rows + SUB * chunks : rows + (SUB + 4) * chunks]
    rows = rows + (SUB + 4) * chunks
    return mom, own, ranks, mix.at[rows : rows + 10 * cy].reshape(10, cy, nz)


def pack_y(pops_in, anchor_in, offsets_in, heading_in, velocity_in, count, mix, up, down,
           pops, anchor, offsets, heading, velocity, angles, sems, *, cx, cy, nz, slots):
    chunks = slots // LANES
    mom, own, ranks, faces = views(mix, cx, cy, nz, chunks)
    copies = [
        pltpu.make_async_copy(source, target, sems.at[n])
        for n, (source, target) in enumerate(
            ((anchor_in, anchor), (offsets_in, offsets), (heading_in, heading), (velocity_in, velocity), (pops_in, pops))
        )
    ]
    for copy in copies:
        copy.start()
    for copy in copies[:4]:
        copy.wait()
    number = anchor[...].astype(f32)
    block_row = (cy + 2) * nz
    cell_x = jnp.floor((number + 0.5) * (1.0 / block_row))
    rest = number - cell_x * block_row
    cell_y = jnp.floor((rest + 0.5) * (1.0 / nz))
    cell_z = rest - cell_y * nz
    slot = lax.broadcasted_iota(jnp.int32, (chunks, LANES), 0) * LANES
    live = slot + lax.broadcasted_iota(jnp.int32, (chunks, LANES), 1) < count[0, 0]
    for n in range(2):
        for k in range(chunks):
            angles[n, k : k + 1, :] = heading[n : n + 1, k * LANES : (k + 1) * LANES]
    cosine = jnp.cos(angles[...])
    sine = jnp.sin(angles[...])
    alive = live.astype(f32)
    place_x = jnp.where(live, cell_x - 1.0 + offsets[0:chunks, :], FAR)
    place_y = cell_y - 1.0 + offsets[chunks : 2 * chunks, :]
    rows = [
        place_x,
        place_y,
        cell_z + offsets[2 * chunks : 3 * chunks, :],
        friction * velocity[0:chunks, :] - propulsion * cosine[0] * cosine[1],
        friction * velocity[chunks : 2 * chunks, :] - propulsion * sine[0] * cosine[1],
        friction * velocity[2 * chunks : 3 * chunks, :] - propulsion * sine[1],
        alive,
        jnp.full((chunks, LANES), count[0, 0].astype(f32)),
    ]
    for f in range(8):
        own[:, f, :] = rows[f]
    masks = [
        jnp.where(place_y > cy - 1 - REACH, alive, 0.0),
        jnp.where(place_y < REACH, alive, 0.0),
        jnp.where(place_x >= cx - 1, alive, 0.0),
        jnp.where((place_x > cx - 1 - REACH) & (place_x < cx - 1), alive, 0.0),
        jnp.where(place_x < 0.0, alive, 0.0),
        jnp.where((place_x < REACH) & (place_x >= 0.0), alive, 0.0),
    ]
    place = ranks_of(jnp.concatenate(masks, axis=0), chunks)
    ranks[0 : 2 * chunks, :] = place[0 : 2 * chunks]
    for n in (2, 3):
        ahead = place[(2 * n - 2) * chunks : (2 * n - 1) * chunks]
        after = place[(2 * n - 1) * chunks : 2 * n * chunks]
        begin = jnp.max(jnp.max(ahead, axis=1, keepdims=True), axis=0, keepdims=True) + 1.0
        ranks[n * chunks : (n + 1) * chunks, :] = jnp.where(after >= 0.0, after + begin, ahead)
    parts = thirds(jnp.concatenate([own[k] for k in range(chunks)], axis=1))
    for n, ref in ((0, up), (1, down)):
        rank = place[n * chunks : (n + 1) * chunks]
        total = jnp.max(rank).astype(jnp.int32) + 1

        def put(j, tile, ref=ref):
            ref[STRIP + j] = tile

        compact_into(put, parts, rank, total, chunks)

    copies[4].wait()
    moments_into(pops, mom)
    for side, sign, ring in ((0, 1, cx - 1), (1, -1, 0)):
        for k, q in enumerate(outward(0, sign)):
            faces[5 * side + k] = pops[q, ring]
    for ref, rows, sign in ((up, (cy - 2, cy - 1), 1), (down, (0, 1), -1)):
        ring = cy - 1 if sign == 1 else 0
        for c in range(3):
            for k in range(2):
                ref[2 * c + k] = mom[c, :, rows[k], :]
        ref[6] = mom[3, :, ring, :]
        for k, q in enumerate(outward(1, sign)):
            ref[7 + k] = pops[q, :, ring, :]


def tent(length, first, place):
    cell = jnp.floor(place)
    part = place - cell
    rows = lax.broadcasted_iota(jnp.int32, (length, LANES), 0).astype(f32) + first
    return jnp.where(rows == cell, 1.0 - part, jnp.where(rows == cell + 1.0, part, 0.0))


def both(value, rows, padded=None):
    value = value.reshape(rows, LANES)
    if padded is not None:
        value = jnp.concatenate([value, jnp.zeros((padded - rows, LANES), f32)], axis=0)
    high, low = split(value)
    return jnp.concatenate([high, low], axis=1)


def along_z(tile, nz):
    high, low = split(tent(nz, 0.0, tile[2:3]))
    return high, low


def sample_table(high, low):
    top = jnp.concatenate([high, low], axis=1)
    return jnp.concatenate([top, top], axis=0)


def gather_rows(table, right):
    full = jnp.dot(table, right, preferred_element_type=f32)
    return full[:, :LANES] + full[:, LANES:]


def spread_many(lefts, highs, lows):
    tall = jnp.concatenate([jnp.concatenate(highs, axis=1), jnp.concatenate(lows, axis=1)], axis=0)
    left = jnp.concatenate(lefts, axis=1)
    full = lax.dot_general(left, tall, (((1,), (1,)), ((), ())), preferred_element_type=f32)
    return full[:, :LANES] + full[:, LANES:]


def spread_rows(left, high, low):
    return spread_many([left], [high, high], [low, low])


def turns(z, nz):
    return ((z - 0.5 * nz) * (2.0**32 / nz)).astype(jnp.int32)


def ghost_rows(gb, gz, tile, at, shift_x, shift_y, nz):
    flat = jnp.transpose(tile)
    rows = pl.ds(pl.multiple_of(at, SUB), LANES)
    gb[0, rows, :] = jnp.broadcast_to(flat[:, 0:1] + shift_x, (LANES, LANES))
    gb[1, rows, :] = jnp.broadcast_to(flat[:, 1:2] + shift_y, (LANES, LANES))
    gz[rows, :] = turns(jnp.broadcast_to(flat[:, 2:3], (LANES, LANES)), nz)


GROUP = 16


def pair_rows(gb, gz, tile, rows, total, nz):
    px, py = (jnp.broadcast_to(tile[c : c + 1], (SUB, LANES)) for c in range(2))
    pz = turns(jnp.broadcast_to(tile[2:3], (SUB, LANES)), nz)

    def step(g, total):
        fx, fy, fz = total
        for r in range(GROUP):
            at = pl.ds(pl.multiple_of((g * GROUP + r) * SUB, SUB), SUB)
            dx = px - gb[0, at, :]
            dy = py - gb[1, at, :]
            dz = (pz - gz[at, :]).astype(f32) * (nz / 2.0**32)
            raw = dx * dx + dy * dy + dz * dz
            square = jnp.maximum(raw, floor_square)
            inverse = pl.reciprocal(square, approx=True)
            sixth = inverse * inverse * inverse
            size = (sixth * inverse) * jnp.maximum(sixth - 0.5, 0.0)
            fx = fx + size * dx
            fy = fy + size * dy
            fz = fz + size * dz
        return fx, fy, fz

    return lax.fori_loop(0, rows, step, total)


EARLY = 2


def own_pairs(own, gb, gz, pairs, first, last, count, nz):
    groups = lax.div(count + (GROUP * SUB - 1), GROUP * SUB)

    def own_step(k, carry):
        zero = jnp.zeros((SUB, LANES), f32)
        total = pair_rows(gb, gz, own[k], groups, (zero, zero, zero), nz)
        for c in range(3):
            pairs[k, c] = total[c]
        return carry

    lax.fori_loop(first, last, own_step, 0)


def own_first(mix, part, sides, gb, gz, early, table, *, cx, cy, nz, slots):
    chunks = slots // LANES
    mom, own, ranks, _ = views(mix, cx, cy, nz, chunks)
    fields = jnp.concatenate([own[k] for k in range(chunks)], axis=1)
    parts = thirds(fields)
    for n in range(2):
        rank = ranks[(2 + n) * chunks : (3 + n) * chunks, :]
        total = jnp.max(rank).astype(jnp.int32) + 1

        def put(j, tile, n=n):
            sides[n, j] = tile

        compact_into(put, parts, rank, total, chunks)
    for c in range(3):
        table[c * cx * cy : (c + 1) * cx * cy, :] = both(mom[c], cx * cy)

    def step(n, carry):
        for k in [n * UNROLL + u for u in range(UNROLL)]:
            tile = own[k]
            right = sample_table(*along_z(tile, nz))
            wx = tent(cx, 0.0, tile[0:1])
            wy = tent(cy, 0.0, tile[1:2])
            sums = []
            for c in range(3):
                full = gather_rows(table[c * cx * cy : (c + 1) * cx * cy, :], right).reshape(cx, cy, LANES)
                total = full[0] * wx[0:1]
                for x in range(1, cx):
                    total = total + full[x] * wx[x : x + 1]
                sums.append(jnp.sum(total * wy, axis=0, keepdims=True))
            part[k, 0:3, :] = jnp.concatenate(sums, axis=0)
        return carry

    count = jnp.max(own[0, 7:8, :]).astype(jnp.int32)
    lax.fori_loop(0, steps_of(count), step, 0)

    def fill(n, carry):
        for k in [n * UNROLL + u for u in range(UNROLL)]:
            ghost_rows(gb, gz, own[k], k * LANES, 0.0, 0.0, nz)
        return carry

    lax.fori_loop(0, steps_of(count), fill, 0)
    own_pairs(own, gb, gz, early, 0, jnp.minimum(chunks_of(count), EARLY), count, nz)


def pack_x(mix, sides, from_down, from_up, right, left, *, cx, cy, nz, slots):
    chunks = slots // LANES
    mom, _, _, faces = views(mix, cx, cy, nz, chunks)
    for side, ref, cols, sign in ((0, right, (cx - 2, cx - 1), 1), (1, left, (0, 1), -1)):
        ring = cx - 1 if sign == 1 else 0
        names = outward(0, sign)
        zero = jnp.zeros((YPAD, LANES), f32)
        for f in range(STRIP):
            ref[f] = zero
        for c in range(3):
            for k in range(2):
                ref[2 * c + k, 2 : 2 + cy, :] = mom[c, cols[k]]
                ref[2 * c + k, 0:2, :] = from_down[2 * c : 2 * c + 2, cols[k], :]
                ref[2 * c + k, 2 + cy : 4 + cy, :] = from_up[2 * c : 2 * c + 2, cols[k], :]
        ref[6, 2 : 2 + cy, :] = mom[3, ring]
        ref[6, 1:2, :] = from_down[6, ring : ring + 1, :]
        ref[6, 2 + cy : 3 + cy, :] = from_up[6, ring : ring + 1, :]
        for k, q in enumerate(names):
            ref[7 + k, 2 : 2 + cy, :] = faces[5 * side + k]
            if lattice_dirs[q][1] == 1:
                at = 7 + outward(1, 1).index(q)
                ref[7 + k, 1:2, :] = from_down[at, ring : ring + 1, :]
            if lattice_dirs[q][1] == -1:
                at = 7 + outward(1, -1).index(q)
                ref[7 + k, 2 + cy : 3 + cy, :] = from_up[at, ring : ring + 1, :]
        for part in range(3):
            for k in range(chunks):
                tile = (sides[side, k], from_down[STRIP + k], from_up[STRIP + k])[part]
                ref[STRIP + part * (chunks // 3 + 1) + k // 3, (k % 3) * SUB : (k % 3 + 1) * SUB, :] = tile


def own_second(mix, part, gb, gz, early, from_down, from_up, spread_out, react_out, pairs, ytable, *, cx, cy, nz, slots):
    chunks = slots // LANES
    _, own, _, _ = views(mix, cx, cy, nz, chunks)
    count = jnp.max(own[0, 7:8, :]).astype(jnp.int32)
    live_chunks = chunks_of(count)
    wide = cx + 2
    ring = jnp.concatenate(
        [from_down[2 * c + 1] for c in range(3)] + [from_up[2 * c] for c in range(3)], axis=0
    )
    ytable[...] = both(ring, 6 * cx)
    spread_out[...] = jnp.zeros_like(spread_out)

    def step(n, carry):
        lefts, highs, lows = [], [], []
        for k in [n * UNROLL + u for u in range(UNROLL)]:
            tile = own[k]
            high, low = along_z(tile, nz)
            wx = tent(wide + 6, -1.0, tile[0:1])
            wy = tent(YPAD, -2.0, tile[1:2])
            full = gather_rows(ytable[...], sample_table(high, low)).reshape(2, 3, cx, LANES)
            inner = tent(cx, 0.0, tile[0:1])
            lower = jnp.sum(full[0] * inner[None], axis=1) * wy[1:2]
            upper = jnp.sum(full[1] * inner[None], axis=1) * wy[cy + 2 : cy + 3]
            react = tile[3:6] - friction * (part[k, 0:3, :] + lower + upper)
            react_out[k, 0:3, :] = react
            react = react * tile[6:7]
            pieces = []
            for x in range(wide):
                for c in range(3):
                    pieces.append((wx[x : x + 1] * react[c : c + 1]) * wy)
            lefts.append(both(jnp.stack(pieces), wide * 3 * YPAD))
            highs += [high, high]
            lows += [low, low]
        spread_out[...] += spread_many(lefts, highs, lows).reshape(wide, 3, YPAD, LANES)
        return carry

    lax.fori_loop(0, steps_of(count), step, 0)

    pairs[0:EARLY] = early[...]
    own_pairs(own, gb, gz, pairs, EARLY, live_chunks, count, nz)


def post_of(q, pop, rho, u, force, common):
    c = lattice_dirs[q]
    w = lattice_weights[q]

    def dot(v):
        total = None
        for k in range(3):
            if c[k] == 0:
                continue
            term = v[k] if c[k] == 1 else -v[k]
            total = term if total is None else total + term
        return total

    base, dotted = common
    kept = (1.0 - 1.0 / relax_time) * pop
    scale = (1.0 - 0.5 / relax_time) * w
    if q == 0:
        return kept + (w / relax_time) * rho * base - (3.0 * scale) * dotted
    along = dot(u)
    pushed = dot(force)
    balance = (w / relax_time) * rho * (base + along * (3.0 + 4.5 * along))
    source = (3.0 * scale) * (pushed * (1.0 + 3.0 * along) - dotted)
    return kept + balance + source


def main_kernel(pops, mix, sides, react_in, pairs, spread, from_down, from_up, from_left, from_right, moved_out, out,
                moved, sems, ext, tside, tflat, tcorner, xtable, flo, fhi, post, gb, gz, sacc, fe, *, cx, cy, nz, slots):
    chunks = slots // LANES
    wide = cx + 2
    mom, own, _, _ = views(mix, cx, cy, nz, chunks)

    ext[...] = jnp.zeros_like(ext)
    for c in range(3):
        for x in range(cx):
            ext[x + 2, c, 0:2, :] = from_down[2 * c : 2 * c + 2, x, :]
            ext[x + 2, c, 2 + cy : 4 + cy, :] = from_up[2 * c : 2 * c + 2, x, :]
        for x in (0, 1, cx - 2, cx - 1):
            ext[x + 2, c, 2 : 2 + cy, :] = mom[c, x]
        for x in range(2, cx - 2):
            ext[x + 2, c, 2 : 2 + SUB - 2, :] = mom[c, x, 0 : SUB - 2, :]
            ext[x + 2, c, 2 * SUB : 2 + cy, :] = mom[c, x, 2 * SUB - 2 : cy, :]
        for k in range(2):
            ext[k, c] = from_left[2 * c + k]
            ext[cx + 2 + k, c] = from_right[2 * c + k]
    for n, x in ((0, 0), (1, cx + 1)):
        tside[n] = both(ext[x : x + 3], 9 * YPAD, 9 * YPAD + SUB)
        for m, y in ((0, 0), (1, 2 * SUB)):
            tcorner[2 * n + m] = both(ext[x : x + 3, :, y : y + SUB, :], 9 * SUB, 10 * SUB)
    for m, y in ((0, 0), (1, 2 * SUB)):
        tflat[m] = both(ext[1 : cx + 3, :, y : y + SUB, :], wide * 3 * SUB)
    xtable[...] = both(jnp.concatenate([ext[1:2], ext[cx + 2 : cx + 3]], axis=0), 6 * YPAD)
    fe[...] = spread[...]
    flo[...] = jnp.zeros_like(flo)
    fhi[...] = jnp.zeros_like(fhi)

    def y_tile(ref):
        return lambda k: ref[STRIP + k]

    def x_tile(ref, part):
        def at(k):
            row = lax.rem(k, 3) * SUB
            return ref[STRIP + part * (chunks // 3 + 1) + lax.div(k, 3), pl.ds(pl.multiple_of(row, SUB), SUB), :]

        def first(k):
            if isinstance(k, int):
                return ref[STRIP + part * (chunks // 3 + 1) + k // 3, (k % 3) * SUB : (k % 3 + 1) * SUB, :]
            return at(k)

        return first

    sets = [(0, -1, y_tile(from_down)), (0, 1, y_tile(from_up))]
    for a, ref in ((-1, from_left), (1, from_right)):
        for part, b in enumerate((0, -1, 1)):
            sets.append((a, b, x_tile(ref, part)))
    counts = [jnp.max(source(0)[7:8, :]).astype(jnp.int32) for _, _, source in sets]
    own_count = jnp.max(own[0, 7:8, :]).astype(jnp.int32)
    own_chunks = chunks_of(own_count)

    def own_step(n, carry):
        for k in [n * UNROLL + u for u in range(UNROLL)]:
            tile = own[k]
            wx = tent(2 * SUB, -1.0, tile[0:1])
            wy = tent(YPAD, -2.0, tile[1:2])
            full = gather_rows(xtable[...], sample_table(*along_z(tile, nz))).reshape(2, 3, YPAD, LANES)
            total = full[0] * wx[0:1] + full[1] * wx[cx + 1 : cx + 2]
            sacc[k, 0:3, :] = friction * jnp.sum(total * wy[None], axis=1) - react_in[k, 0:3, :]
        return carry

    lax.fori_loop(0, steps_of(own_count), own_step, 0)

    jobs = []
    for (a, b, source), count in zip(sets, counts):
        side = 0 if a == -1 else 1
        half = 0 if b == -1 else 1
        if b == 0:
            depth, first_y, target = YPAD, -2.0, fe
        else:
            depth, first_y, target = SUB, -2.0 + 2 * SUB * half, (flo, fhi)[half]
        if a == 0:
            first_x, cols, slots_x = -1.0, wide, [(x, x) for x in range(wide)]
            table = tflat.at[half]
        else:
            cols = 3
            first_x = -2.0 if a == -1 else float(cx - 1)
            slots_x = [(0, 1), (1, 2)] if a == -1 else [(cx, 0), (cx + 1, 1)]
            table = tside.at[side] if b == 0 else tcorner.at[2 * side + half]
        jobs.append((source, count, float(a * cx), float(b * cy), table, cols, first_x, depth, first_y, slots_x,
                     target, False))
    for side, n in ((0, 1), (1, 0)):
        first_x = -2.0 if side == 0 else float(cx - 1)
        slots_x = [(0, 1), (1, 2)] if side == 0 else [(cx, 0), (cx + 1, 1)]
        source = lambda k, n=n: sides[n, k]
        near = (own[:, 0, :] < 0.0) if side == 0 else (own[:, 0, :] >= cx - 1)
        count = jnp.sum(jnp.where(near, own[:, 6, :], 0.0)).astype(jnp.int32)
        jobs.append((source, count, 0.0, 0.0, xtable, 1, first_x, YPAD, -2.0, slots_x, fe, True))

    def reaction(job, k):
        source, _, shift_x, shift_y, table, cols, first_x, depth, first_y, _, _, own_list = job
        tile = source(k)
        high, low = along_z(tile, nz)
        wx = tent(2 * SUB, first_x, tile[0:1] + shift_x)
        wy = tent(depth, first_y, tile[1:2] + shift_y)
        right = sample_table(high, low)
        if own_list:
            at = 0 if first_x < 0.0 else 3 * YPAD
            row = 1
            full = gather_rows(xtable[...], right)[at : at + 3 * YPAD].reshape(1, 3, YPAD, LANES)
            total = full[0] * wx[row : row + 1]
            react = -friction * jnp.sum(total * wy[None], axis=1)
        else:
            full = gather_rows(table[...], right)[: cols * 3 * depth].reshape(cols, 3, depth, LANES)
            total = full[0] * wx[0:1]
            for x in range(1, cols):
                total = total + full[x] * wx[x : x + 1]
            react = tile[3:6] - friction * jnp.sum(total * wy[None], axis=1)
        return react * tile[6:7], wx, wy, high, low

    def spread_job(job, parts):
        react, wx, wy, high, low = parts
        depth, slots_x = job[7], job[9]
        pieces = []
        for _, w in slots_x:
            for c in range(3):
                pieces.append((wx[w : w + 1] * react[c : c + 1]) * wy)
        got = spread_rows(both(jnp.stack(pieces), len(slots_x) * 3 * depth), high, low)
        return got.reshape(len(slots_x), 3, depth, LANES)

    def add_job(job, got):
        for n, (f, _) in enumerate(job[9]):
            job[10][f] += got[n]

    parts = [reaction(job, 0) for job in jobs]
    gots = [spread_job(job, part) for job, part in zip(jobs, parts)]
    for job, got in zip(jobs, gots):
        add_job(job, got)
    for job in jobs:

        def more(k, carry, job=job):
            add_job(job, spread_job(job, reaction(job, k)))
            return carry

        lax.fori_loop(1, chunks_of(job[1]), more, 0)

    for x in range(wide):
        fe[x, :, 0:SUB, :] += flo[x]
        fe[x, :, 2 * SUB : 3 * SUB, :] += fhi[x]

    base_row = SUB

    def prepared(rho, u0, force):
        half = 0.5 / rho
        u = [u0[c] + half * force[c] for c in range(3)]
        base = 1.0 - 1.5 * (u[0] * u[0] + u[1] * u[1] + u[2] * u[2])
        dotted = u[0] * force[0] + u[1] * force[1] + u[2] * force[2]
        return u, (base, dotted)

    for x in range(cx):
        for h in range(0, cy, SUB):
            force = [fe[x + 1, c, 2 + h : 2 + h + SUB, :] for c in range(3)]
            rho = mom[3, x, h : h + SUB, :]
            u, common = prepared(rho, [mom[c, x, h : h + SUB, :] for c in range(3)], force)
            for q in range(19):
                post[q, x + 1, base_row + h : base_row + h + SUB, :] = post_of(
                    q, pops[q, x, h : h + SUB, :], rho, u, force, common
                )
    for ref, row, layer, sign in ((from_left, 0, 1, 1), (from_right, cx + 1, 0, -1)):
        force = [fe[row, c] for c in range(3)]
        rho = ref[6]
        u, common = prepared(rho, [ref[2 * c + layer] for c in range(3)], force)
        for k, q in enumerate(outward(0, sign)):
            post[q, row, base_row - 2 : base_row - 2 + YPAD, :] = post_of(q, ref[7 + k], rho, u, force, common)
    for ref, row, at, layer, sign in (
        (from_down, base_row - 1, 1, 1, 1),
        (from_up, base_row + cy, cy + 2, 0, -1),
    ):
        force = [fe[1 : 1 + cx, c, at, :] for c in range(3)]
        rho = ref[6]
        u, common = prepared(rho, [ref[2 * c + layer] for c in range(3)], force)
        for k, q in enumerate(outward(1, sign)):
            post[q, 1 : 1 + cx, row, :] = post_of(q, ref[7 + k], rho, u, force, common)
    copies = []
    for q in range(19):
        dx, dy, dz = lattice_dirs[q]
        for x in range(cx):
            plane = post[q, x + 1 - dx, base_row - dy : base_row - dy + cy, :]
            if dz != 0:
                plane = pltpu.roll(plane, dz % nz, 1)
            moved[q, x] = plane
        copies.append(pltpu.make_async_copy(moved.at[q], moved_out.at[q], sems.at[q]))
        copies[-1].start()

    at = jnp.int32(0)
    places = []
    for (a, b, source), count in zip(sets, counts):
        ghost_rows(gb, gz, source(0), at, float(a * cx), float(b * cy), nz)
        places.append(at)
        at = at + jnp.where(count > LANES, chunks_of(count) * LANES, lax.div(count + (SUB - 1), SUB) * SUB)
    for (a, b, source), count, begin in zip(sets, counts, places):

        def fill(k, carry, source=source, a=a, b=b, begin=begin):
            ghost_rows(gb, gz, source(k), begin + k * LANES, float(a * cx), float(b * cy), nz)
            return carry

        lax.fori_loop(1, chunks_of(count), fill, 0)
    gb[0, pl.ds(pl.multiple_of(at, SUB), GROUP * SUB), :] = jnp.full((GROUP * SUB, LANES), FAR, f32)
    groups = lax.div(at + (GROUP * SUB - 1), GROUP * SUB)

    def pair_step(k, carry):
        total = pair_rows(gb, gz, own[k], groups, tuple(pairs[k, c] for c in range(3)), nz)
        sums = jnp.concatenate([jnp.sum(t, axis=0, keepdims=True) for t in total], axis=0)
        sacc[k, 0:3, :] = sacc[k, 0:3, :] + (48.0 * wca_energy) * sums
        return carry

    lax.fori_loop(0, own_chunks, pair_step, 0)

    for c in range(3):
        out[c * chunks : (c + 1) * chunks, :] = jnp.where(own[:, 6, :] > 0.0, sacc[:, c, :], 0.0)
    for copy in copies:
        copy.wait()


def shifted(value, axis, by):
    devices = lax.axis_size(axis)
    return lax.ppermute(value, axis, [(i, (i + by) % devices) for i in range(devices)])


def body(populations, anchor, offsets, heading, velocity, live_count):
    _, cx, cy, nz = populations.shape
    slots = anchor.shape[2]
    chunks = slots // LANES
    sizes = dict(cx=cx, cy=cy, nz=nz, slots=slots)
    vmem = pl.BlockSpec(memory_space=pltpu.VMEM)
    smem = pl.BlockSpec(memory_space=pltpu.SMEM)
    shape = jax.ShapeDtypeStruct

    hbm = pl.BlockSpec(memory_space=pltpu.HBM)

    def call(kernel, name, outs, scratch, *args, ins=None, out_specs=None, limit=48):
        return pl.pallas_call(
            functools.partial(kernel, **sizes),
            out_shape=outs,
            in_specs=ins or [vmem] * len(args),
            out_specs=out_specs or (vmem,) * len(outs),
            scratch_shapes=scratch,
            compiler_params=pltpu.CompilerParams(vmem_limit_bytes=limit * 2**20),
            name=name,
        )(*args)

    face_y = shape((STRIP + chunks, cx, nz), f32)
    tiles = shape((chunks, SUB, LANES), f32)
    dma = pltpu.SemaphoreType.DMA
    mix, up, down = call(
        pack_y, "pack_y",
        (shape((4 * cx * cy + (SUB + 4) * chunks + 10 * cy, LANES), f32), face_y, face_y),
        [
            pltpu.VMEM(populations.shape, f32),
            pltpu.VMEM((chunks, LANES), jnp.int32),
            pltpu.VMEM((3 * chunks, LANES), f32),
            pltpu.VMEM((2, slots), f32),
            pltpu.VMEM((3 * chunks, LANES), f32),
            pltpu.VMEM((2, chunks, LANES), f32),
            dma((5,)),
        ],
        populations, anchor.reshape(chunks, LANES), offsets.reshape(3 * chunks, LANES), heading[0, 0],
        velocity.reshape(3 * chunks, LANES), live_count, ins=[hbm] * 5 + [smem], limit=62,
    )
    from_down = shifted(up, "gy", 1)
    from_up = shifted(down, "gy", -1)
    part, sides, gb, gz, early = call(
        own_first, "own_first",
        (tiles, shape((2, chunks, SUB, LANES), f32), shape((2, slots, LANES), f32), shape((slots, LANES), jnp.int32),
         shape((EARLY, 3, SUB, LANES), f32)),
        [pltpu.VMEM((3 * cx * cy, 2 * nz), bf16)],
        mix,
    )
    face_x = shape((STRIP + 3 * (chunks // 3 + 1), YPAD, nz), f32)
    right, left = call(
        pack_x, "pack_x", (face_x, face_x), [], mix, sides, from_down, from_up,
    )
    from_left = shifted(right, "gx", 1)
    from_right = shifted(left, "gx", -1)
    wide = cx + 2
    spread, react, pairs = call(
        own_second, "own_second",
        (shape((wide, 3, YPAD, nz), f32), tiles, shape((chunks, 3, SUB, LANES), f32)),
        [pltpu.VMEM((6 * cx, 2 * nz), bf16)],
        mix, part, gb, gz, early, from_down, from_up,
    )
    moved, force = call(
        main_kernel, "main",
        (shape(populations.shape, f32), shape((3 * chunks, LANES), f32)),
        [
            pltpu.VMEM(populations.shape, f32),
            dma((19,)),
            pltpu.VMEM((cx + 4, 3, YPAD, nz), f32),
            pltpu.VMEM((2, 9 * YPAD + SUB, 2 * nz), bf16),
            pltpu.VMEM((2, wide * 3 * SUB, 2 * nz), bf16),
            pltpu.VMEM((4, 10 * SUB, 2 * nz), bf16),
            pltpu.VMEM((6 * YPAD, 2 * nz), bf16),
            pltpu.VMEM((wide, 3, SUB, nz), f32),
            pltpu.VMEM((wide, 3, SUB, nz), f32),
            pltpu.VMEM((19, cx + 2, cy + 2 * SUB, nz), f32),
            pltpu.VMEM((2, 8 * slots + LANES, LANES), f32),
            pltpu.VMEM((8 * slots + LANES, LANES), jnp.int32),
            pltpu.VMEM((chunks, SUB, LANES), f32),
            pltpu.VMEM((wide, 3, YPAD, nz), f32),
        ],
        populations, mix, sides, react, pairs, spread, from_down, from_up, from_left, from_right,
        out_specs=(hbm, vmem),
    )
    return moved, force.reshape(1, 1, 3, slots)


def solution(mesh):
    return jax.shard_map(
        body,
        mesh=mesh,
        in_specs=(
            P(None, "gx", "gy", None),
            P("gx", "gy", None),
            P("gx", "gy", None, None),
            P("gx", "gy", None, None),
            P("gx", "gy", None, None),
            P("gx", "gy"),
        ),
        out_specs=(P(None, "gx", "gy", None), P("gx", "gy", None, None)),
        check_vma=False,
    )
```

```python
import functools

import jax
import jax.numpy as jnp
from jax import lax
from jax.experimental import pallas as pl
from jax.experimental.pallas import tpu as pltpu
from jax.sharding import PartitionSpec as P

lattice_dirs = (
    (0, 0, 0),
    (1, 0, 0),
    (-1, 0, 0),
    (0, 1, 0),
    (0, -1, 0),
    (0, 0, 1),
    (0, 0, -1),
    (1, 1, 0),
    (-1, -1, 0),
    (1, -1, 0),
    (-1, 1, 0),
    (1, 0, 1),
    (-1, 0, -1),
    (1, 0, -1),
    (-1, 0, 1),
    (0, 1, 1),
    (0, -1, -1),
    (0, 1, -1),
    (0, -1, 1),
)
lattice_weights = (1.0 / 3.0,) + (1.0 / 18.0,) * 6 + (1.0 / 36.0,) * 12
relax_time = 0.8
friction = 2.0
propulsion = 0.5
wca_energy = 0.01
floor_square = 0.8
cutoff_square = 2.0 ** (1.0 / 3.0)

f32 = jnp.float32
bf16 = jnp.bfloat16
LANES = 128
SUB = 8
FAR = 1.0e9
YPAD = 24
STRIP = 12


def outward(axis, sign):
    return [q for q in range(19) if lattice_dirs[q][axis] == sign]


def split(value):
    high = value.astype(bf16)
    low = (value - high.astype(f32)).astype(bf16)
    return high, low


REACH = 1.1225


def moments_into(pops, mom):
    rho = pops[0]
    for q in range(1, 19):
        rho = rho + pops[q]
    inverse = 1.0 / rho
    mom[3] = rho
    for c in range(3):
        total = None
        for q in range(19):
            sign = lattice_dirs[q][c]
            if sign == 0:
                continue
            term = pops[q] if sign == 1 else -pops[q]
            total = term if total is None else total + term
        mom[c] = total * inverse


def thirds(fields):
    first = fields.astype(bf16).astype(f32)
    second = (fields - first).astype(bf16).astype(f32)
    third = fields - first - second
    return jnp.concatenate([first, second, third, jnp.zeros_like(first)], axis=0).astype(bf16)


def ranks_of(mask, chunks):
    rows = mask.shape[0]
    i = lax.broadcasted_iota(jnp.int32, (LANES, LANES), 0)
    j = lax.broadcasted_iota(jnp.int32, (LANES, LANES), 1)
    upper = jnp.where(i <= j, 1.0, 0.0).astype(bf16)
    ones = jnp.ones((LANES, LANES), bf16)
    held = mask.astype(bf16)
    inside = jnp.dot(held, upper, preferred_element_type=f32)
    total = jnp.dot(held, ones, preferred_element_type=f32)
    i = lax.broadcasted_iota(jnp.int32, (rows, rows), 0)
    j = lax.broadcasted_iota(jnp.int32, (rows, rows), 1)
    ahead = (i > j) & (lax.div(i, chunks) == lax.div(j, chunks))
    before = jnp.dot(jnp.where(ahead, 1.0, 0.0).astype(bf16), total.astype(bf16), preferred_element_type=f32)
    return jnp.where(mask > 0.5, inside + before - 1.0, -1.0)


def chunks_of(count):
    return lax.div(count + (LANES - 1), LANES)


UNROLL = 4


def steps_of(count):
    return lax.div(count + (UNROLL * LANES - 1), UNROLL * LANES)


def compact_into(put, parts, rank, count, chunks):
    def step(j, carry):
        rows = lax.broadcasted_iota(jnp.int32, (LANES, LANES), 0).astype(f32) + (j * LANES).astype(f32)
        chosen = [jnp.where(rows == rank[k : k + 1], 1.0, 0.0).astype(bf16) for k in range(chunks)]
        got = lax.dot_general(
            parts, jnp.concatenate(chosen, axis=1), (((1,), (1,)), ((), ())), preferred_element_type=f32
        )
        tile = got[0:8] + got[8:16] + got[16:24]
        row = lax.broadcasted_iota(jnp.int32, (SUB, LANES), 0)
        tile = jnp.where((row == 0) & (tile[6:7] < 0.5), FAR, tile)
        tile = jnp.where(row == 7, count.astype(f32), tile)
        put(j, tile)
        return carry

    step(jnp.int32(0), 0)
    lax.fori_loop(1, chunks_of(count), step, 0)


FIELDS = 6


def y_views(ref, cx, chunks):
    rows = STRIP * cx
    return ref.at[0:rows].reshape(STRIP, cx, LANES), ref.at[rows : rows + FIELDS * chunks].reshape(FIELDS, chunks, LANES)


def x_layout(cy, chunks):
    high, ring = cy + 4, cy + 2
    first = 6 * high + 6 * ring
    first = first + (-first) % SUB
    return [f * high for f in range(6)], [6 * high + f * ring for f in range(6)], [
        first + n * FIELDS * chunks for n in range(4)
    ]


def views(mix, cx, cy, nz, chunks):
    rows = 4 * cx * cy
    mom = mix.at[0:rows].reshape(4, cx, cy, nz)
    own = mix.at[rows : rows + SUB * chunks].reshape(chunks, SUB, LANES)
    ranks = mix.at[rows + SUB * chunks : rows + (SUB + 4) * chunks]
    rows = rows + (SUB + 4) * chunks
    return mom, own, ranks, mix.at[rows : rows + 10 * cy].reshape(10, cy, nz)


def pack_y(pops_in, anchor_in, offsets_in, heading_in, velocity_in, count, mix, up_rows, down_rows,
           lists, pops, anchor, offsets, heading, velocity, angles, sems, *, cx, cy, nz, slots):
    chunks = slots // LANES
    mom, own, ranks, faces = views(mix, cx, cy, nz, chunks)
    up, up_list = y_views(up_rows, cx, chunks)
    down, down_list = y_views(down_rows, cx, chunks)
    copies = [
        pltpu.make_async_copy(source, target, sems.at[n])
        for n, (source, target) in enumerate(
            ((anchor_in, anchor), (offsets_in, offsets), (heading_in, heading), (velocity_in, velocity), (pops_in, pops))
        )
    ]
    for copy in copies:
        copy.start()
    for copy in copies[:4]:
        copy.wait()
    number = anchor[...].astype(f32)
    block_row = (cy + 2) * nz
    cell_x = jnp.floor((number + 0.5) * (1.0 / block_row))
    rest = number - cell_x * block_row
    cell_y = jnp.floor((rest + 0.5) * (1.0 / nz))
    cell_z = rest - cell_y * nz
    slot = lax.broadcasted_iota(jnp.int32, (chunks, LANES), 0) * LANES
    live = slot + lax.broadcasted_iota(jnp.int32, (chunks, LANES), 1) < count[0, 0]
    for n in range(2):
        for k in range(chunks):
            angles[n, k : k + 1, :] = heading[n : n + 1, k * LANES : (k + 1) * LANES]
    cosine = jnp.cos(angles[...])
    sine = jnp.sin(angles[...])
    alive = live.astype(f32)
    place_x = jnp.where(live, cell_x - 1.0 + offsets[0:chunks, :], FAR)
    place_y = cell_y - 1.0 + offsets[chunks : 2 * chunks, :]
    rows = [
        place_x,
        place_y,
        cell_z + offsets[2 * chunks : 3 * chunks, :],
        friction * velocity[0:chunks, :] - propulsion * cosine[0] * cosine[1],
        friction * velocity[chunks : 2 * chunks, :] - propulsion * sine[0] * cosine[1],
        friction * velocity[2 * chunks : 3 * chunks, :] - propulsion * sine[1],
        alive,
        jnp.full((chunks, LANES), count[0, 0].astype(f32)),
    ]
    for f in range(8):
        own[:, f, :] = rows[f]
    masks = [
        jnp.where(place_y > cy - 1 - REACH, alive, 0.0),
        jnp.where(place_y < REACH, alive, 0.0),
        jnp.where(place_x >= cx - 1, alive, 0.0),
        jnp.where((place_x > cx - 1 - REACH) & (place_x < cx - 1), alive, 0.0),
        jnp.where(place_x < 0.0, alive, 0.0),
        jnp.where((place_x < REACH) & (place_x >= 0.0), alive, 0.0),
    ]
    place = ranks_of(jnp.concatenate(masks, axis=0), chunks)
    ranks[0 : 2 * chunks, :] = place[0 : 2 * chunks]
    for n in (2, 3):
        ahead = place[(2 * n - 2) * chunks : (2 * n - 1) * chunks]
        after = place[(2 * n - 1) * chunks : 2 * n * chunks]
        begin = jnp.max(jnp.max(ahead, axis=1, keepdims=True), axis=0, keepdims=True) + 1.0
        ranks[n * chunks : (n + 1) * chunks, :] = jnp.where(after >= 0.0, after + begin, ahead)
    parts = thirds(jnp.concatenate([own[k] for k in range(chunks)], axis=1))
    lists[:, :, 0, :] = jnp.full((2, chunks, LANES), FAR, f32)
    for n, ref in ((0, up_list), (1, down_list)):
        rank = place[n * chunks : (n + 1) * chunks]
        total = jnp.max(rank).astype(jnp.int32) + 1

        def put(j, tile, n=n):
            lists[n, j] = tile

        compact_into(put, parts, rank, total, chunks)
        for f in range(FIELDS):
            ref[f] = lists[n, :, f, :]

    copies[4].wait()
    moments_into(pops, mom)
    for side, sign, ring in ((0, 1, cx - 1), (1, -1, 0)):
        for k, q in enumerate(outward(0, sign)):
            faces[5 * side + k] = pops[q, ring]
    for ref, rows, sign in ((up, (cy - 2, cy - 1), 1), (down, (0, 1), -1)):
        ring = cy - 1 if sign == 1 else 0
        for c in range(3):
            for k in range(2):
                ref[2 * c + k] = mom[c, :, rows[k], :]
        ref[6] = mom[3, :, ring, :]
        for k, q in enumerate(outward(1, sign)):
            ref[7 + k] = pops[q, :, ring, :]


def tent(length, first, place):
    cell = jnp.floor(place)
    part = place - cell
    rows = lax.broadcasted_iota(jnp.int32, (length, LANES), 0).astype(f32) + first
    return jnp.where(rows == cell, 1.0 - part, jnp.where(rows == cell + 1.0, part, 0.0))


def both(value, rows, padded=None):
    value = value.reshape(rows, LANES)
    if padded is not None:
        value = jnp.concatenate([value, jnp.zeros((padded - rows, LANES), f32)], axis=0)
    high, low = split(value)
    return jnp.concatenate([high, low], axis=1)


def along_z(tile, nz):
    high, low = split(tent(nz, 0.0, tile[2:3]))
    return high, low


def sample_table(high, low):
    top = jnp.concatenate([high, low], axis=1)
    return jnp.concatenate([top, top], axis=0)


def gather_rows(table, right):
    full = jnp.dot(table, right, preferred_element_type=f32)
    return full[:, :LANES] + full[:, LANES:]


def spread_many(lefts, highs, lows):
    tall = jnp.concatenate([jnp.concatenate(highs, axis=1), jnp.concatenate(lows, axis=1)], axis=0)
    left = jnp.concatenate(lefts, axis=1)
    full = lax.dot_general(left, tall, (((1,), (1,)), ((), ())), preferred_element_type=f32)
    return full[:, :LANES] + full[:, LANES:]


def spread_rows(left, high, low):
    return spread_many([left], [high, high], [low, low])


def turns(z, nz):
    return ((z - 0.5 * nz) * (2.0**32 / nz)).astype(jnp.int32)


def ghost_rows(gb, gz, tile, at, shift_x, shift_y, nz):
    flat = jnp.transpose(tile)
    rows = pl.ds(pl.multiple_of(at, SUB), LANES)
    gb[0, rows, :] = jnp.broadcast_to(flat[:, 0:1] + shift_x, (LANES, LANES))
    gb[1, rows, :] = jnp.broadcast_to(flat[:, 1:2] + shift_y, (LANES, LANES))
    gz[rows, :] = turns(jnp.broadcast_to(flat[:, 2:3], (LANES, LANES)), nz)


GROUP = 16


def pair_rows(gb, gz, tile, rows, total, nz):
    px, py = (jnp.broadcast_to(tile[c : c + 1], (SUB, LANES)) for c in range(2))
    pz = turns(jnp.broadcast_to(tile[2:3], (SUB, LANES)), nz)

    def step(g, total):
        fx, fy, fz = total
        for r in range(GROUP):
            at = pl.ds(pl.multiple_of((g * GROUP + r) * SUB, SUB), SUB)
            dx = px - gb[0, at, :]
            dy = py - gb[1, at, :]
            dz = (pz - gz[at, :]).astype(f32) * (nz / 2.0**32)
            raw = dx * dx + dy * dy + dz * dz
            square = jnp.maximum(raw, floor_square)
            inverse = pl.reciprocal(square, approx=True)
            sixth = inverse * inverse * inverse
            size = (sixth * inverse) * jnp.maximum(sixth - 0.5, 0.0)
            fx = fx + size * dx
            fy = fy + size * dy
            fz = fz + size * dz
        return fx, fy, fz

    return lax.fori_loop(0, rows, step, total)


EARLY = 2


def own_pairs(own, gb, gz, pairs, first, last, count, nz):
    groups = lax.div(count + (GROUP * SUB - 1), GROUP * SUB)

    def own_step(k, carry):
        zero = jnp.zeros((SUB, LANES), f32)
        total = pair_rows(gb, gz, own[k], groups, (zero, zero, zero), nz)
        for c in range(3):
            pairs[k, c] = total[c]
        return carry

    lax.fori_loop(first, last, own_step, 0)


def unpack(lists, n, fields, chunks):
    for f in range(FIELDS):
        lists[n, :, f, :] = fields(f)
    alive = jnp.where(fields(0) < 0.5 * FAR, 1.0, 0.0)
    lists[n, :, 6, :] = alive
    return jnp.sum(alive).astype(jnp.int32)


def gather_ghosts(gb, gz, entries, nz):
    at = jnp.int32(0)
    most = jnp.int32(0)
    places = []
    for source, count, shift_x, shift_y in entries:
        ghost_rows(gb, gz, source(0), at, shift_x, shift_y, nz)
        places.append(at)
        most = jnp.maximum(most, count)
        at = at + jnp.where(count > LANES, chunks_of(count) * LANES, lax.div(count + (SUB - 1), SUB) * SUB)

    @pl.when(most > LANES)
    def _():
        for (source, count, shift_x, shift_y), begin in zip(entries, places):

            def fill(k, carry, source=source, shift_x=shift_x, shift_y=shift_y, begin=begin):
                ghost_rows(gb, gz, source(k), begin + k * LANES, shift_x, shift_y, nz)
                return carry

            lax.fori_loop(1, chunks_of(count), fill, 0)

    gb[0, pl.ds(pl.multiple_of(at, SUB), GROUP * SUB), :] = jnp.full((GROUP * SUB, LANES), FAR, f32)
    return lax.div(at + (GROUP * SUB - 1), GROUP * SUB)


def own_first(mix, part, sides, gb, gz, early, table, *, cx, cy, nz, slots):
    chunks = slots // LANES
    mom, own, ranks, _ = views(mix, cx, cy, nz, chunks)
    fields = jnp.concatenate([own[k] for k in range(chunks)], axis=1)
    parts = thirds(fields)
    sides[:, :, 0, :] = jnp.full((2, chunks, LANES), FAR, f32)
    for n in range(2):
        rank = ranks[(2 + n) * chunks : (3 + n) * chunks, :]
        total = jnp.max(rank).astype(jnp.int32) + 1

        def put(j, tile, n=n):
            sides[n, j] = tile

        compact_into(put, parts, rank, total, chunks)
    for c in range(3):
        table[c * cx * cy : (c + 1) * cx * cy, :] = both(mom[c], cx * cy)

    def step(n, carry):
        for k in [n * UNROLL + u for u in range(UNROLL)]:
            tile = own[k]
            right = sample_table(*along_z(tile, nz))
            wx = tent(cx, 0.0, tile[0:1])
            wy = tent(cy, 0.0, tile[1:2])
            sums = []
            for c in range(3):
                full = gather_rows(table[c * cx * cy : (c + 1) * cx * cy, :], right).reshape(cx, cy, LANES)
                total = full[0] * wx[0:1]
                for x in range(1, cx):
                    total = total + full[x] * wx[x : x + 1]
                sums.append(jnp.sum(total * wy, axis=0, keepdims=True))
            part[k, 0:3, :] = jnp.concatenate(sums, axis=0)
        return carry

    count = jnp.max(own[0, 7:8, :]).astype(jnp.int32)
    lax.fori_loop(0, steps_of(count), step, 0)

    def fill(n, carry):
        for k in [n * UNROLL + u for u in range(UNROLL)]:
            ghost_rows(gb, gz, own[k], k * LANES, 0.0, 0.0, nz)
        return carry

    lax.fori_loop(0, steps_of(count), fill, 0)
    own_pairs(own, gb, gz, early, 0, jnp.minimum(chunks_of(count), EARLY), count, nz)


def pack_x(mix, sides, down_rows, up_rows, right, left, *, cx, cy, nz, slots):
    chunks = slots // LANES
    mom, _, _, faces = views(mix, cx, cy, nz, chunks)
    from_down, down_list = y_views(down_rows, cx, chunks)
    from_up, up_list = y_views(up_rows, cx, chunks)
    columns, rings, begins = x_layout(cy, chunks)
    for side, ref, cols, sign in ((0, right, (cx - 2, cx - 1), 1), (1, left, (0, 1), -1)):
        ring = cx - 1 if sign == 1 else 0
        for c in range(3):
            for k in range(2):
                f = 2 * c + k
                at = columns[f]
                ref[at + 2 : at + 2 + cy, :] = mom[c, cols[k]]
                ref[at : at + 2, :] = from_down[2 * c : 2 * c + 2, cols[k], :]
                ref[at + 2 + cy : at + 4 + cy, :] = from_up[2 * c : 2 * c + 2, cols[k], :]
        at = rings[0]
        ref[at + 1 : at + 1 + cy, :] = mom[3, ring]
        ref[at : at + 1, :] = from_down[6, ring : ring + 1, :]
        ref[at + 1 + cy : at + 2 + cy, :] = from_up[6, ring : ring + 1, :]
        for k, q in enumerate(outward(0, sign)):
            at = rings[1 + k]
            ref[at + 1 : at + 1 + cy, :] = faces[5 * side + k]
            if lattice_dirs[q][1] == 1:
                f = 7 + outward(1, 1).index(q)
                ref[at : at + 1, :] = from_down[f, ring : ring + 1, :]
            if lattice_dirs[q][1] == -1:
                f = 7 + outward(1, -1).index(q)
                ref[at + 1 + cy : at + 2 + cy, :] = from_up[f, ring : ring + 1, :]
        for f in range(FIELDS):
            rows = [slice(begin + f * chunks, begin + (f + 1) * chunks) for begin in begins]
            ref[rows[0], :] = sides[side, :, f, :]
            ref[rows[1], :] = down_list[f]
            ref[rows[2], :] = up_list[f]


def own_second(mix, part, gb, gz, early, down_rows, up_rows, spread_out, react_out, pairs, ytable, lists, gb2, gz2, *, cx, cy, nz, slots):
    chunks = slots // LANES
    _, own, _, _ = views(mix, cx, cy, nz, chunks)
    from_down, down_list = y_views(down_rows, cx, chunks)
    from_up, up_list = y_views(up_rows, cx, chunks)
    count = jnp.max(own[0, 7:8, :]).astype(jnp.int32)
    live_chunks = chunks_of(count)
    wide = cx + 2
    ring = jnp.concatenate(
        [from_down[2 * c + 1] for c in range(3)] + [from_up[2 * c] for c in range(3)], axis=0
    )
    ytable[...] = both(ring, 6 * cx)
    spread_out[...] = jnp.zeros_like(spread_out)

    def step(n, carry):
        lefts, highs, lows = [], [], []
        for k in [n * UNROLL + u for u in range(UNROLL)]:
            tile = own[k]
            high, low = along_z(tile, nz)
            wx = tent(wide + 6, -1.0, tile[0:1])
            wy = tent(YPAD, -2.0, tile[1:2])
            full = gather_rows(ytable[...], sample_table(high, low)).reshape(2, 3, cx, LANES)
            inner = tent(cx, 0.0, tile[0:1])
            lower = jnp.sum(full[0] * inner[None], axis=1) * wy[1:2]
            upper = jnp.sum(full[1] * inner[None], axis=1) * wy[cy + 2 : cy + 3]
            react = tile[3:6] - friction * (part[k, 0:3, :] + lower + upper)
            react_out[k, 0:3, :] = react
            react = react * tile[6:7]
            pieces = []
            for x in range(wide):
                for c in range(3):
                    pieces.append((wx[x : x + 1] * react[c : c + 1]) * wy)
            lefts.append(both(jnp.stack(pieces), wide * 3 * YPAD))
            highs += [high, high]
            lows += [low, low]
        spread_out[...] += spread_many(lefts, highs, lows).reshape(wide, 3, YPAD, LANES)
        return carry

    lax.fori_loop(0, steps_of(count), step, 0)

    pairs[0:EARLY] = early[...]
    own_pairs(own, gb, gz, pairs, EARLY, live_chunks, count, nz)
    entries = []
    for n, (ref, shift) in enumerate(((down_list, -float(cy)), (up_list, float(cy)))):
        number = unpack(lists, n, lambda f, ref=ref: ref[f], chunks)
        entries.append((lambda k, n=n: lists[n, k], number, 0.0, shift))
    groups = gather_ghosts(gb2, gz2, entries, nz)

    def pair_step(k, carry):
        total = pair_rows(gb2, gz2, own[k], groups, tuple(pairs[k, c] for c in range(3)), nz)
        for c in range(3):
            pairs[k, c] = total[c]
        return carry

    lax.fori_loop(0, live_chunks, pair_step, 0)


def post_of(q, pop, rho, u, force, common):
    c = lattice_dirs[q]
    w = lattice_weights[q]

    def dot(v):
        total = None
        for k in range(3):
            if c[k] == 0:
                continue
            term = v[k] if c[k] == 1 else -v[k]
            total = term if total is None else total + term
        return total

    base, dotted = common
    kept = (1.0 - 1.0 / relax_time) * pop
    scale = (1.0 - 0.5 / relax_time) * w
    if q == 0:
        return kept + (w / relax_time) * rho * base - (3.0 * scale) * dotted
    along = dot(u)
    pushed = dot(force)
    balance = (w / relax_time) * rho * (base + along * (3.0 + 4.5 * along))
    source = (3.0 * scale) * (pushed * (1.0 + 3.0 * along) - dotted)
    return kept + balance + source


def main_kernel(pops, mix, sides, react_in, pairs, spread, down_rows, up_rows, from_left, from_right, moved_out, out,
                lists, moved, sems, ext, tside, tflat, tcorner, xtable, flo, fhi, post, gb, gz, sacc, fe, *, cx, cy, nz, slots):
    chunks = slots // LANES
    wide = cx + 2
    mom, own, _, _ = views(mix, cx, cy, nz, chunks)
    from_down, down_list = y_views(down_rows, cx, chunks)
    from_up, up_list = y_views(up_rows, cx, chunks)
    columns, rings, begins = x_layout(cy, chunks)
    high, ring = cy + 4, cy + 2

    ext[...] = jnp.zeros_like(ext)
    for c in range(3):
        for x in range(cx):
            ext[x + 2, c, 0:2, :] = from_down[2 * c : 2 * c + 2, x, :]
            ext[x + 2, c, 2 + cy : 4 + cy, :] = from_up[2 * c : 2 * c + 2, x, :]
        for x in (0, 1, cx - 2, cx - 1):
            ext[x + 2, c, 2 : 2 + cy, :] = mom[c, x]
        for x in range(2, cx - 2):
            ext[x + 2, c, 2 : 2 + SUB - 2, :] = mom[c, x, 0 : SUB - 2, :]
            ext[x + 2, c, 2 * SUB : 2 + cy, :] = mom[c, x, 2 * SUB - 2 : cy, :]
        for k in range(2):
            at = columns[2 * c + k]
            ext[k, c, 0:high, :] = from_left[at : at + high, :]
            ext[cx + 2 + k, c, 0:high, :] = from_right[at : at + high, :]
    for n, x in ((0, 0), (1, cx + 1)):
        tside[n] = both(ext[x : x + 3], 9 * YPAD, 9 * YPAD + SUB)
        for m, y in ((0, 0), (1, 2 * SUB)):
            tcorner[2 * n + m] = both(ext[x : x + 3, :, y : y + SUB, :], 9 * SUB, 10 * SUB)
    for m, y in ((0, 0), (1, 2 * SUB)):
        tflat[m] = both(ext[1 : cx + 3, :, y : y + SUB, :], wide * 3 * SUB)
    xtable[...] = both(jnp.concatenate([ext[1:2], ext[cx + 2 : cx + 3]], axis=0), 6 * YPAD)
    fe[...] = spread[...]
    flo[...] = jnp.zeros_like(flo)
    fhi[...] = jnp.zeros_like(fhi)

    sets = []
    counts = []

    def arrived(a, b, fields):
        n = len(sets)
        counts.append(unpack(lists, n, fields, chunks))
        sets.append((a, b, lambda k, n=n: lists[n, k]))

    arrived(0, -1, lambda f: down_list[f])
    arrived(0, 1, lambda f: up_list[f])
    for a, ref in ((-1, from_left), (1, from_right)):
        for begin, b in zip(begins, (0, -1, 1)):
            arrived(a, b, lambda f, ref=ref, begin=begin: ref[begin + f * chunks : begin + (f + 1) * chunks, :])
    own_count = jnp.max(own[0, 7:8, :]).astype(jnp.int32)
    own_chunks = chunks_of(own_count)

    def own_step(n, carry):
        for k in [n * UNROLL + u for u in range(UNROLL)]:
            tile = own[k]
            wx = tent(2 * SUB, -1.0, tile[0:1])
            wy = tent(YPAD, -2.0, tile[1:2])
            full = gather_rows(xtable[...], sample_table(*along_z(tile, nz))).reshape(2, 3, YPAD, LANES)
            total = full[0] * wx[0:1] + full[1] * wx[cx + 1 : cx + 2]
            sacc[k, 0:3, :] = friction * jnp.sum(total * wy[None], axis=1) - react_in[k, 0:3, :]
        return carry

    lax.fori_loop(0, steps_of(own_count), own_step, 0)

    jobs = []
    for (a, b, source), count in zip(sets, counts):
        side = 0 if a == -1 else 1
        half = 0 if b == -1 else 1
        if b == 0:
            depth, first_y, target = YPAD, -2.0, fe
        else:
            depth, first_y, target = SUB, -2.0 + 2 * SUB * half, (flo, fhi)[half]
        if a == 0:
            first_x, cols, slots_x = -1.0, wide, [(x, x) for x in range(wide)]
            table = tflat.at[half]
        else:
            cols = 3
            first_x = -2.0 if a == -1 else float(cx - 1)
            slots_x = [(0, 1), (1, 2)] if a == -1 else [(cx, 0), (cx + 1, 1)]
            table = tside.at[side] if b == 0 else tcorner.at[2 * side + half]
        jobs.append((source, count, float(a * cx), float(b * cy), table, cols, first_x, depth, first_y, slots_x,
                     target, False))
    for side, n in ((0, 1), (1, 0)):
        first_x = -2.0 if side == 0 else float(cx - 1)
        slots_x = [(0, 1), (1, 2)] if side == 0 else [(cx, 0), (cx + 1, 1)]
        source = lambda k, n=n: sides[n, k]
        near = (own[:, 0, :] < 0.0) if side == 0 else (own[:, 0, :] >= cx - 1)
        count = jnp.sum(jnp.where(near, own[:, 6, :], 0.0)).astype(jnp.int32)
        jobs.append((source, count, 0.0, 0.0, xtable, 1, first_x, YPAD, -2.0, slots_x, fe, True))

    def reaction(job, k):
        source, _, shift_x, shift_y, table, cols, first_x, depth, first_y, _, _, own_list = job
        tile = source(k)
        high, low = along_z(tile, nz)
        wx = tent(2 * SUB, first_x, tile[0:1] + shift_x)
        wy = tent(depth, first_y, tile[1:2] + shift_y)
        right = sample_table(high, low)
        if own_list:
            at = 0 if first_x < 0.0 else 3 * YPAD
            row = 1
            full = gather_rows(xtable[...], right)[at : at + 3 * YPAD].reshape(1, 3, YPAD, LANES)
            total = full[0] * wx[row : row + 1]
            react = -friction * jnp.sum(total * wy[None], axis=1)
        else:
            full = gather_rows(table[...], right)[: cols * 3 * depth].reshape(cols, 3, depth, LANES)
            total = full[0] * wx[0:1]
            for x in range(1, cols):
                total = total + full[x] * wx[x : x + 1]
            react = tile[3:6] - friction * jnp.sum(total * wy[None], axis=1)
        return react * tile[6:7], wx, wy, high, low

    def spread_job(job, parts):
        react, wx, wy, high, low = parts
        depth, slots_x = job[7], job[9]
        pieces = []
        for _, w in slots_x:
            for c in range(3):
                pieces.append((wx[w : w + 1] * react[c : c + 1]) * wy)
        got = spread_rows(both(jnp.stack(pieces), len(slots_x) * 3 * depth), high, low)
        return got.reshape(len(slots_x), 3, depth, LANES)

    def add_job(job, got):
        for n, (f, _) in enumerate(job[9]):
            job[10][f] += got[n]

    parts = [reaction(job, 0) for job in jobs]
    gots = [spread_job(job, part) for job, part in zip(jobs, parts)]
    for job, got in zip(jobs, gots):
        add_job(job, got)
    most = jobs[0][1]
    for job in jobs[1:]:
        most = jnp.maximum(most, job[1])

    @pl.when(most > LANES)
    def _():
        for job in jobs:

            def more(k, carry, job=job):
                add_job(job, spread_job(job, reaction(job, k)))
                return carry

            lax.fori_loop(1, chunks_of(job[1]), more, 0)

    for x in range(wide):
        fe[x, :, 0:SUB, :] += flo[x]
        fe[x, :, 2 * SUB : 3 * SUB, :] += fhi[x]

    base_row = SUB

    def prepared(rho, u0, force):
        half = 0.5 / rho
        u = [u0[c] + half * force[c] for c in range(3)]
        base = 1.0 - 1.5 * (u[0] * u[0] + u[1] * u[1] + u[2] * u[2])
        dotted = u[0] * force[0] + u[1] * force[1] + u[2] * force[2]
        return u, (base, dotted)

    for x in range(cx):
        for h in range(0, cy, SUB):
            force = [fe[x + 1, c, 2 + h : 2 + h + SUB, :] for c in range(3)]
            rho = mom[3, x, h : h + SUB, :]
            u, common = prepared(rho, [mom[c, x, h : h + SUB, :] for c in range(3)], force)
            for q in range(19):
                post[q, x + 1, base_row + h : base_row + h + SUB, :] = post_of(
                    q, pops[q, x, h : h + SUB, :], rho, u, force, common
                )
    for ref, row, layer, sign in ((from_left, 0, 1, 1), (from_right, cx + 1, 0, -1)):
        force = [fe[row, c, 1 : 1 + ring, :] for c in range(3)]
        rho = ref[rings[0] : rings[0] + ring, :]
        starts = [columns[2 * c + layer] + 1 for c in range(3)]
        u, common = prepared(rho, [ref[start : start + ring, :] for start in starts], force)
        for k, q in enumerate(outward(0, sign)):
            pop = ref[rings[1 + k] : rings[1 + k] + ring, :]
            post[q, row, base_row - 1 : base_row - 1 + ring, :] = post_of(q, pop, rho, u, force, common)
    for ref, row, at, layer, sign in (
        (from_down, base_row - 1, 1, 1, 1),
        (from_up, base_row + cy, cy + 2, 0, -1),
    ):
        force = [fe[1 : 1 + cx, c, at, :] for c in range(3)]
        rho = ref[6]
        u, common = prepared(rho, [ref[2 * c + layer] for c in range(3)], force)
        for k, q in enumerate(outward(1, sign)):
            post[q, 1 : 1 + cx, row, :] = post_of(q, ref[7 + k], rho, u, force, common)
    copies = []
    for q in range(19):
        dx, dy, dz = lattice_dirs[q]
        for x in range(cx):
            plane = post[q, x + 1 - dx, base_row - dy : base_row - dy + cy, :]
            if dz != 0:
                plane = pltpu.roll(plane, dz % nz, 1)
            moved[q, x] = plane
        copies.append(pltpu.make_async_copy(moved.at[q], moved_out.at[q], sems.at[q]))
        copies[-1].start()

    groups = gather_ghosts(
        gb, gz, [(source, count, float(a * cx), float(b * cy)) for (a, b, source), count in zip(sets, counts) if a != 0], nz
    )

    def pair_step(k, carry):
        total = pair_rows(gb, gz, own[k], groups, tuple(pairs[k, c] for c in range(3)), nz)
        sums = jnp.concatenate([jnp.sum(t, axis=0, keepdims=True) for t in total], axis=0)
        sacc[k, 0:3, :] = sacc[k, 0:3, :] + (48.0 * wca_energy) * sums
        return carry

    lax.fori_loop(0, own_chunks, pair_step, 0)

    for c in range(3):
        out[c * chunks : (c + 1) * chunks, :] = jnp.where(own[:, 6, :] > 0.0, sacc[:, c, :], 0.0)
    for copy in copies:
        copy.wait()


def shifted(value, axis, by):
    devices = lax.axis_size(axis)
    return lax.ppermute(value, axis, [(i, (i + by) % devices) for i in range(devices)])


def body(populations, anchor, offsets, heading, velocity, live_count):
    _, cx, cy, nz = populations.shape
    slots = anchor.shape[2]
    chunks = slots // LANES
    sizes = dict(cx=cx, cy=cy, nz=nz, slots=slots)
    vmem = pl.BlockSpec(memory_space=pltpu.VMEM)
    smem = pl.BlockSpec(memory_space=pltpu.SMEM)
    shape = jax.ShapeDtypeStruct

    hbm = pl.BlockSpec(memory_space=pltpu.HBM)

    def call(kernel, name, outs, scratch, *args, ins=None, out_specs=None, limit=48):
        return pl.pallas_call(
            functools.partial(kernel, **sizes),
            out_shape=outs,
            in_specs=ins or [vmem] * len(args),
            out_specs=out_specs or (vmem,) * len(outs),
            scratch_shapes=scratch,
            compiler_params=pltpu.CompilerParams(vmem_limit_bytes=limit * 2**20),
            name=name,
        )(*args)

    face_y = shape((STRIP * cx + FIELDS * chunks, nz), f32)
    tiles = shape((chunks, SUB, LANES), f32)
    dma = pltpu.SemaphoreType.DMA
    mix, up, down = call(
        pack_y, "pack_y",
        (shape((4 * cx * cy + (SUB + 4) * chunks + 10 * cy, LANES), f32), face_y, face_y),
        [
            pltpu.VMEM((2, chunks, SUB, LANES), f32),
            pltpu.VMEM(populations.shape, f32),
            pltpu.VMEM((chunks, LANES), jnp.int32),
            pltpu.VMEM((3 * chunks, LANES), f32),
            pltpu.VMEM((2, slots), f32),
            pltpu.VMEM((3 * chunks, LANES), f32),
            pltpu.VMEM((2, chunks, LANES), f32),
            dma((5,)),
        ],
        populations, anchor.reshape(chunks, LANES), offsets.reshape(3 * chunks, LANES), heading[0, 0],
        velocity.reshape(3 * chunks, LANES), live_count, ins=[hbm] * 5 + [smem], limit=62,
    )
    from_down = shifted(up, "gy", 1)
    from_up = shifted(down, "gy", -1)
    part, sides, gb, gz, early = call(
        own_first, "own_first",
        (tiles, shape((2, chunks, SUB, LANES), f32), shape((2, slots, LANES), f32), shape((slots, LANES), jnp.int32),
         shape((EARLY, 3, SUB, LANES), f32)),
        [pltpu.VMEM((3 * cx * cy, 2 * nz), bf16)],
        mix,
    )
    face_x = shape((x_layout(cy, chunks)[2][3], nz), f32)
    right, left = call(
        pack_x, "pack_x", (face_x, face_x), [], mix, sides, from_down, from_up,
    )
    from_left = shifted(right, "gx", 1)
    from_right = shifted(left, "gx", -1)
    wide = cx + 2
    spread, react, pairs = call(
        own_second, "own_second",
        (shape((wide, 3, YPAD, nz), f32), tiles, shape((chunks, 3, SUB, LANES), f32)),
        [
            pltpu.VMEM((6 * cx, 2 * nz), bf16),
            pltpu.VMEM((2, chunks, SUB, LANES), f32),
            pltpu.VMEM((2, 2 * slots + LANES, LANES), f32),
            pltpu.VMEM((2 * slots + LANES, LANES), jnp.int32),
        ],
        mix, part, gb, gz, early, from_down, from_up,
    )
    moved, force = call(
        main_kernel, "main",
        (shape(populations.shape, f32), shape((3 * chunks, LANES), f32)),
        [
            pltpu.VMEM((8, chunks, SUB, LANES), f32),
            pltpu.VMEM(populations.shape, f32),
            dma((19,)),
            pltpu.VMEM((cx + 4, 3, YPAD, nz), f32),
            pltpu.VMEM((2, 9 * YPAD + SUB, 2 * nz), bf16),
            pltpu.VMEM((2, wide * 3 * SUB, 2 * nz), bf16),
            pltpu.VMEM((4, 10 * SUB, 2 * nz), bf16),
            pltpu.VMEM((6 * YPAD, 2 * nz), bf16),
            pltpu.VMEM((wide, 3, SUB, nz), f32),
            pltpu.VMEM((wide, 3, SUB, nz), f32),
            pltpu.VMEM((19, cx + 2, cy + 2 * SUB, nz), f32),
            pltpu.VMEM((2, 6 * slots + LANES, LANES), f32),
            pltpu.VMEM((6 * slots + LANES, LANES), jnp.int32),
            pltpu.VMEM((chunks, SUB, LANES), f32),
            pltpu.VMEM((wide, 3, YPAD, nz), f32),
        ],
        populations, mix, sides, react, pairs, spread, from_down, from_up, from_left, from_right,
        out_specs=(hbm, vmem),
    )
    return moved, force.reshape(1, 1, 3, slots)


def solution(mesh):
    return jax.shard_map(
        body,
        mesh=mesh,
        in_specs=(
            P(None, "gx", "gy", None),
            P("gx", "gy", None),
            P("gx", "gy", None, None),
            P("gx", "gy", None, None),
            P("gx", "gy", None, None),
            P("gx", "gy"),
        ),
        out_specs=(P(None, "gx", "gy", None), P("gx", "gy", None, None)),
        check_vma=False,
    )
```

```python
import functools

import jax
import jax.numpy as jnp
from jax import lax
from jax.experimental import pallas as pl
from jax.experimental.pallas import tpu as pltpu
from jax.sharding import PartitionSpec as P

lattice_dirs = (
    (0, 0, 0),
    (1, 0, 0),
    (-1, 0, 0),
    (0, 1, 0),
    (0, -1, 0),
    (0, 0, 1),
    (0, 0, -1),
    (1, 1, 0),
    (-1, -1, 0),
    (1, -1, 0),
    (-1, 1, 0),
    (1, 0, 1),
    (-1, 0, -1),
    (1, 0, -1),
    (-1, 0, 1),
    (0, 1, 1),
    (0, -1, -1),
    (0, 1, -1),
    (0, -1, 1),
)
lattice_weights = (1.0 / 3.0,) + (1.0 / 18.0,) * 6 + (1.0 / 36.0,) * 12
relax_time = 0.8
friction = 2.0
propulsion = 0.5
wca_energy = 0.01
floor_square = 0.8
cutoff_square = 2.0 ** (1.0 / 3.0)

f32 = jnp.float32
bf16 = jnp.bfloat16
LANES = 128
SUB = 8
FAR = 1.0e9
YPAD = 24
STRIP = 12


def outward(axis, sign):
    return [q for q in range(19) if lattice_dirs[q][axis] == sign]


def split(value):
    high = value.astype(bf16)
    low = (value - high.astype(f32)).astype(bf16)
    return high, low


REACH = 1.1225


def moments_into(pops, mom):
    rho = pops[0]
    for q in range(1, 19):
        rho = rho + pops[q]
    inverse = 1.0 / rho
    mom[3] = rho
    for c in range(3):
        total = None
        for q in range(19):
            sign = lattice_dirs[q][c]
            if sign == 0:
                continue
            term = pops[q] if sign == 1 else -pops[q]
            total = term if total is None else total + term
        mom[c] = total * inverse


def thirds(fields):
    first = fields.astype(bf16).astype(f32)
    second = (fields - first).astype(bf16).astype(f32)
    third = fields - first - second
    return jnp.concatenate([first, second, third, jnp.zeros_like(first)], axis=0).astype(bf16)


def ranks_of(mask, chunks):
    rows = mask.shape[0]
    i = lax.broadcasted_iota(jnp.int32, (LANES, LANES), 0)
    j = lax.broadcasted_iota(jnp.int32, (LANES, LANES), 1)
    upper = jnp.where(i <= j, 1.0, 0.0).astype(bf16)
    ones = jnp.ones((LANES, LANES), bf16)
    held = mask.astype(bf16)
    inside = jnp.dot(held, upper, preferred_element_type=f32)
    total = jnp.dot(held, ones, preferred_element_type=f32)
    i = lax.broadcasted_iota(jnp.int32, (rows, rows), 0)
    j = lax.broadcasted_iota(jnp.int32, (rows, rows), 1)
    ahead = (i > j) & (lax.div(i, chunks) == lax.div(j, chunks))
    before = jnp.dot(jnp.where(ahead, 1.0, 0.0).astype(bf16), total.astype(bf16), preferred_element_type=f32)
    return jnp.where(mask > 0.5, inside + before - 1.0, -1.0)


def chunks_of(count):
    return lax.div(count + (LANES - 1), LANES)


UNROLL = 4


def steps_of(count):
    return lax.div(count + (UNROLL * LANES - 1), UNROLL * LANES)


def compact_into(put, parts, rank, count, chunks):
    def step(j, carry):
        rows = lax.broadcasted_iota(jnp.int32, (LANES, LANES), 0).astype(f32) + (j * LANES).astype(f32)
        chosen = [jnp.where(rows == rank[k : k + 1], 1.0, 0.0).astype(bf16) for k in range(chunks)]
        got = lax.dot_general(
            parts, jnp.concatenate(chosen, axis=1), (((1,), (1,)), ((), ())), preferred_element_type=f32
        )
        tile = got[0:8] + got[8:16] + got[16:24]
        row = lax.broadcasted_iota(jnp.int32, (SUB, LANES), 0)
        tile = jnp.where((row == 0) & (tile[6:7] < 0.5), FAR, tile)
        tile = jnp.where(row == 7, count.astype(f32), tile)
        put(j, tile)
        return carry

    step(jnp.int32(0), 0)
    lax.fori_loop(1, chunks_of(count), step, 0)


FIELDS = 6


def y_views(ref, cx, chunks):
    rows = STRIP * cx
    return ref.at[0:rows].reshape(STRIP, cx, LANES), ref.at[rows : rows + FIELDS * chunks].reshape(FIELDS, chunks, LANES)


def x_layout(cy, chunks):
    high, ring = cy + 4, cy + 2
    first = 6 * high + 6 * ring
    first = first + (-first) % SUB
    return [f * high for f in range(6)], [6 * high + f * ring for f in range(6)], [
        first + n * FIELDS * chunks for n in range(4)
    ]


def views(mix, cx, cy, nz, chunks):
    rows = 4 * cx * cy
    mom = mix.at[0:rows].reshape(4, cx, cy, nz)
    own = mix.at[rows : rows + SUB * chunks].reshape(chunks, SUB, LANES)
    ranks = mix.at[rows + SUB * chunks : rows + (SUB + 4) * chunks]
    rows = rows + (SUB + 4) * chunks
    return mom, own, ranks, mix.at[rows : rows + 10 * cy].reshape(10, cy, nz)


def pack_y(pops_in, anchor_in, offsets_in, heading_in, velocity_in, count, mix, up_rows, down_rows,
           lists, pops, anchor, offsets, heading, velocity, angles, sems, *, cx, cy, nz, slots):
    chunks = slots // LANES
    mom, own, ranks, faces = views(mix, cx, cy, nz, chunks)
    up, up_list = y_views(up_rows, cx, chunks)
    down, down_list = y_views(down_rows, cx, chunks)
    copies = [
        pltpu.make_async_copy(source, target, sems.at[n])
        for n, (source, target) in enumerate(
            ((anchor_in, anchor), (offsets_in, offsets), (heading_in, heading), (velocity_in, velocity), (pops_in, pops))
        )
    ]
    for copy in copies:
        copy.start()
    for copy in copies[:4]:
        copy.wait()
    number = anchor[...].astype(f32)
    block_row = (cy + 2) * nz
    cell_x = jnp.floor((number + 0.5) * (1.0 / block_row))
    rest = number - cell_x * block_row
    cell_y = jnp.floor((rest + 0.5) * (1.0 / nz))
    cell_z = rest - cell_y * nz
    slot = lax.broadcasted_iota(jnp.int32, (chunks, LANES), 0) * LANES
    live = slot + lax.broadcasted_iota(jnp.int32, (chunks, LANES), 1) < count[0, 0]
    for n in range(2):
        for k in range(chunks):
            angles[n, k : k + 1, :] = heading[n : n + 1, k * LANES : (k + 1) * LANES]
    cosine = jnp.cos(angles[...])
    sine = jnp.sin(angles[...])
    alive = live.astype(f32)
    place_x = jnp.where(live, cell_x - 1.0 + offsets[0:chunks, :], FAR)
    place_y = cell_y - 1.0 + offsets[chunks : 2 * chunks, :]
    rows = [
        place_x,
        place_y,
        cell_z + offsets[2 * chunks : 3 * chunks, :],
        friction * velocity[0:chunks, :] - propulsion * cosine[0] * cosine[1],
        friction * velocity[chunks : 2 * chunks, :] - propulsion * sine[0] * cosine[1],
        friction * velocity[2 * chunks : 3 * chunks, :] - propulsion * sine[1],
        alive,
        jnp.full((chunks, LANES), count[0, 0].astype(f32)),
    ]
    for f in range(8):
        own[:, f, :] = rows[f]
    masks = [
        jnp.where(place_y > cy - 1 - REACH, alive, 0.0),
        jnp.where(place_y < REACH, alive, 0.0),
        jnp.where(place_x >= cx - 1, alive, 0.0),
        jnp.where((place_x > cx - 1 - REACH) & (place_x < cx - 1), alive, 0.0),
        jnp.where(place_x < 0.0, alive, 0.0),
        jnp.where((place_x < REACH) & (place_x >= 0.0), alive, 0.0),
    ]
    place = ranks_of(jnp.concatenate(masks, axis=0), chunks)
    ranks[0 : 2 * chunks, :] = place[0 : 2 * chunks]
    for n in (2, 3):
        ahead = place[(2 * n - 2) * chunks : (2 * n - 1) * chunks]
        after = place[(2 * n - 1) * chunks : 2 * n * chunks]
        begin = jnp.max(jnp.max(ahead, axis=1, keepdims=True), axis=0, keepdims=True) + 1.0
        ranks[n * chunks : (n + 1) * chunks, :] = jnp.where(after >= 0.0, after + begin, ahead)
    parts = thirds(jnp.concatenate([own[k] for k in range(chunks)], axis=1))
    lists[:, :, 0, :] = jnp.full((2, chunks, LANES), FAR, f32)
    for n, ref in ((0, up_list), (1, down_list)):
        rank = place[n * chunks : (n + 1) * chunks]
        total = jnp.max(rank).astype(jnp.int32) + 1

        def put(j, tile, n=n):
            lists[n, j] = tile

        compact_into(put, parts, rank, total, chunks)
        for f in range(FIELDS):
            ref[f] = lists[n, :, f, :]

    copies[4].wait()
    moments_into(pops, mom)
    for side, sign, ring in ((0, 1, cx - 1), (1, -1, 0)):
        for k, q in enumerate(outward(0, sign)):
            faces[5 * side + k] = pops[q, ring]
    for ref, rows, sign in ((up, (cy - 2, cy - 1), 1), (down, (0, 1), -1)):
        ring = cy - 1 if sign == 1 else 0
        for c in range(3):
            for k in range(2):
                ref[2 * c + k] = mom[c, :, rows[k], :]
        ref[6] = mom[3, :, ring, :]
        for k, q in enumerate(outward(1, sign)):
            ref[7 + k] = pops[q, :, ring, :]


def tent(length, first, place):
    cell = jnp.floor(place)
    part = place - cell
    rows = lax.broadcasted_iota(jnp.int32, (length, LANES), 0).astype(f32) + first
    return jnp.where(rows == cell, 1.0 - part, jnp.where(rows == cell + 1.0, part, 0.0))


def both(value, rows, padded=None):
    value = value.reshape(rows, LANES)
    if padded is not None:
        value = jnp.concatenate([value, jnp.zeros((padded - rows, LANES), f32)], axis=0)
    high, low = split(value)
    return jnp.concatenate([high, low], axis=1)


def along_z(tile, nz):
    high, low = split(tent(nz, 0.0, tile[2:3]))
    return high, low


def sample_table(high, low):
    top = jnp.concatenate([high, low], axis=1)
    return jnp.concatenate([top, top], axis=0)


def gather_rows(table, right):
    full = jnp.dot(table, right, preferred_element_type=f32)
    return full[:, :LANES] + full[:, LANES:]


def spread_many(lefts, highs, lows):
    tall = jnp.concatenate([jnp.concatenate(highs, axis=1), jnp.concatenate(lows, axis=1)], axis=0)
    left = jnp.concatenate(lefts, axis=1)
    full = lax.dot_general(left, tall, (((1,), (1,)), ((), ())), preferred_element_type=f32)
    return full[:, :LANES] + full[:, LANES:]


def spread_rows(left, high, low):
    return spread_many([left], [high, high], [low, low])


def turns(z, nz):
    return ((z - 0.5 * nz) * (2.0**32 / nz)).astype(jnp.int32)


def ghost_rows(gb, gz, tile, at, shift_x, shift_y, nz):
    flat = jnp.transpose(tile)
    rows = pl.ds(pl.multiple_of(at, SUB), LANES)
    gb[0, rows, :] = jnp.broadcast_to(flat[:, 0:1] + shift_x, (LANES, LANES))
    gb[1, rows, :] = jnp.broadcast_to(flat[:, 1:2] + shift_y, (LANES, LANES))
    gz[rows, :] = turns(jnp.broadcast_to(flat[:, 2:3], (LANES, LANES)), nz)


LIST_GROUP = 8
GROUP = 16


def pair_rows(gb, gz, tile, rows, total, nz, group=GROUP):
    px, py = (jnp.broadcast_to(tile[c : c + 1], (SUB, LANES)) for c in range(2))
    pz = turns(jnp.broadcast_to(tile[2:3], (SUB, LANES)), nz)

    def step(g, total):
        fx, fy, fz = total
        for r in range(group):
            at = pl.ds(pl.multiple_of((g * group + r) * SUB, SUB), SUB)
            dx = px - gb[0, at, :]
            dy = py - gb[1, at, :]
            dz = (pz - gz[at, :]).astype(f32) * (nz / 2.0**32)
            raw = dx * dx + dy * dy + dz * dz
            square = jnp.maximum(raw, floor_square)
            inverse = pl.reciprocal(square, approx=True)
            sixth = inverse * inverse * inverse
            size = (sixth * inverse) * jnp.maximum(sixth - 0.5, 0.0)
            fx = fx + size * dx
            fy = fy + size * dy
            fz = fz + size * dz
        return fx, fy, fz

    return lax.fori_loop(0, rows, step, total)


EARLY = 2


def own_pairs(own, gb, gz, pairs, first, last, count, nz):
    groups = lax.div(count + (GROUP * SUB - 1), GROUP * SUB)

    def own_step(k, carry):
        zero = jnp.zeros((SUB, LANES), f32)
        total = pair_rows(gb, gz, own[k], groups, (zero, zero, zero), nz)
        for c in range(3):
            pairs[k, c] = total[c]
        return carry

    lax.fori_loop(first, last, own_step, 0)


def unpack(lists, n, fields, chunks):
    for f in range(FIELDS):
        lists[n, :, f, :] = fields(f)
    alive = jnp.where(fields(0) < 0.5 * FAR, 1.0, 0.0)
    lists[n, :, 6, :] = alive
    return jnp.sum(alive).astype(jnp.int32)


def gather_ghosts(gb, gz, entries, nz):
    at = jnp.int32(0)
    most = jnp.int32(0)
    places = []
    for source, count, shift_x, shift_y in entries:
        ghost_rows(gb, gz, source(0), at, shift_x, shift_y, nz)
        places.append(at)
        most = jnp.maximum(most, count)
        at = at + jnp.where(count > LANES, chunks_of(count) * LANES, lax.div(count + (SUB - 1), SUB) * SUB)

    @pl.when(most > LANES)
    def _():
        for (source, count, shift_x, shift_y), begin in zip(entries, places):

            def fill(k, carry, source=source, shift_x=shift_x, shift_y=shift_y, begin=begin):
                ghost_rows(gb, gz, source(k), begin + k * LANES, shift_x, shift_y, nz)
                return carry

            lax.fori_loop(1, chunks_of(count), fill, 0)

    gb[0, pl.ds(pl.multiple_of(at, SUB), GROUP * SUB), :] = jnp.full((GROUP * SUB, LANES), FAR, f32)
    return lax.div(at + (LIST_GROUP * SUB - 1), LIST_GROUP * SUB)


def own_first(mix, part, sides, gb, gz, early, table, *, cx, cy, nz, slots):
    chunks = slots // LANES
    mom, own, ranks, _ = views(mix, cx, cy, nz, chunks)
    fields = jnp.concatenate([own[k] for k in range(chunks)], axis=1)
    parts = thirds(fields)
    sides[:, :, 0, :] = jnp.full((2, chunks, LANES), FAR, f32)
    for n in range(2):
        rank = ranks[(2 + n) * chunks : (3 + n) * chunks, :]
        total = jnp.max(rank).astype(jnp.int32) + 1

        def put(j, tile, n=n):
            sides[n, j] = tile

        compact_into(put, parts, rank, total, chunks)
    for c in range(3):
        table[c * cx * cy : (c + 1) * cx * cy, :] = both(mom[c], cx * cy)

    def step(n, carry):
        for k in [n * UNROLL + u for u in range(UNROLL)]:
            tile = own[k]
            right = sample_table(*along_z(tile, nz))
            wx = tent(cx, 0.0, tile[0:1])
            wy = tent(cy, 0.0, tile[1:2])
            sums = []
            for c in range(3):
                full = gather_rows(table[c * cx * cy : (c + 1) * cx * cy, :], right).reshape(cx, cy, LANES)
                total = full[0] * wx[0:1]
                for x in range(1, cx):
                    total = total + full[x] * wx[x : x + 1]
                sums.append(jnp.sum(total * wy, axis=0, keepdims=True))
            part[k, 0:3, :] = jnp.concatenate(sums, axis=0)
        return carry

    count = jnp.max(own[0, 7:8, :]).astype(jnp.int32)
    lax.fori_loop(0, steps_of(count), step, 0)

    def fill(n, carry):
        for k in [n * UNROLL + u for u in range(UNROLL)]:
            ghost_rows(gb, gz, own[k], k * LANES, 0.0, 0.0, nz)
        return carry

    lax.fori_loop(0, steps_of(count), fill, 0)
    own_pairs(own, gb, gz, early, 0, jnp.minimum(chunks_of(count), EARLY), count, nz)


def pack_x(mix, sides, down_rows, up_rows, right, left, *, cx, cy, nz, slots):
    chunks = slots // LANES
    mom, _, _, faces = views(mix, cx, cy, nz, chunks)
    from_down, down_list = y_views(down_rows, cx, chunks)
    from_up, up_list = y_views(up_rows, cx, chunks)
    columns, rings, begins = x_layout(cy, chunks)
    for side, ref, cols, sign in ((0, right, (cx - 2, cx - 1), 1), (1, left, (0, 1), -1)):
        ring = cx - 1 if sign == 1 else 0
        for c in range(3):
            for k in range(2):
                f = 2 * c + k
                at = columns[f]
                ref[at + 2 : at + 2 + cy, :] = mom[c, cols[k]]
                ref[at : at + 2, :] = from_down[2 * c : 2 * c + 2, cols[k], :]
                ref[at + 2 + cy : at + 4 + cy, :] = from_up[2 * c : 2 * c + 2, cols[k], :]
        at = rings[0]
        ref[at + 1 : at + 1 + cy, :] = mom[3, ring]
        ref[at : at + 1, :] = from_down[6, ring : ring + 1, :]
        ref[at + 1 + cy : at + 2 + cy, :] = from_up[6, ring : ring + 1, :]
        for k, q in enumerate(outward(0, sign)):
            at = rings[1 + k]
            ref[at + 1 : at + 1 + cy, :] = faces[5 * side + k]
            if lattice_dirs[q][1] == 1:
                f = 7 + outward(1, 1).index(q)
                ref[at : at + 1, :] = from_down[f, ring : ring + 1, :]
            if lattice_dirs[q][1] == -1:
                f = 7 + outward(1, -1).index(q)
                ref[at + 1 + cy : at + 2 + cy, :] = from_up[f, ring : ring + 1, :]
        for f in range(FIELDS):
            rows = [slice(begin + f * chunks, begin + (f + 1) * chunks) for begin in begins]
            ref[rows[0], :] = sides[side, :, f, :]
            ref[rows[1], :] = down_list[f]
            ref[rows[2], :] = up_list[f]


def own_second(mix, part, gb, gz, early, down_rows, up_rows, spread_out, react_out, pairs, ytable, lists, gb2, gz2, *, cx, cy, nz, slots):
    chunks = slots // LANES
    _, own, _, _ = views(mix, cx, cy, nz, chunks)
    from_down, down_list = y_views(down_rows, cx, chunks)
    from_up, up_list = y_views(up_rows, cx, chunks)
    count = jnp.max(own[0, 7:8, :]).astype(jnp.int32)
    live_chunks = chunks_of(count)
    wide = cx + 2
    ring = jnp.concatenate(
        [from_down[2 * c + 1] for c in range(3)] + [from_up[2 * c] for c in range(3)], axis=0
    )
    ytable[...] = both(ring, 6 * cx)
    spread_out[...] = jnp.zeros_like(spread_out)

    def step(n, carry):
        lefts, highs, lows = [], [], []
        for k in [n * UNROLL + u for u in range(UNROLL)]:
            tile = own[k]
            high, low = along_z(tile, nz)
            wx = tent(wide + 6, -1.0, tile[0:1])
            wy = tent(YPAD, -2.0, tile[1:2])
            full = gather_rows(ytable[...], sample_table(high, low)).reshape(2, 3, cx, LANES)
            inner = tent(cx, 0.0, tile[0:1])
            lower = jnp.sum(full[0] * inner[None], axis=1) * wy[1:2]
            upper = jnp.sum(full[1] * inner[None], axis=1) * wy[cy + 2 : cy + 3]
            react = tile[3:6] - friction * (part[k, 0:3, :] + lower + upper)
            react_out[k, 0:3, :] = react
            react = react * tile[6:7]
            pieces = []
            for x in range(wide):
                for c in range(3):
                    pieces.append((wx[x : x + 1] * react[c : c + 1]) * wy)
            lefts.append(both(jnp.stack(pieces), wide * 3 * YPAD))
            highs += [high, high]
            lows += [low, low]
        spread_out[...] += spread_many(lefts, highs, lows).reshape(wide, 3, YPAD, LANES)
        return carry

    lax.fori_loop(0, steps_of(count), step, 0)

    pairs[0:EARLY] = early[...]
    own_pairs(own, gb, gz, pairs, EARLY, live_chunks, count, nz)
    entries = []
    for n, (ref, shift) in enumerate(((down_list, -float(cy)), (up_list, float(cy)))):
        number = unpack(lists, n, lambda f, ref=ref: ref[f], chunks)
        entries.append((lambda k, n=n: lists[n, k], number, 0.0, shift))
    groups = gather_ghosts(gb2, gz2, entries, nz)

    def pair_step(k, carry):
        total = pair_rows(gb2, gz2, own[k], groups, tuple(pairs[k, c] for c in range(3)), nz, LIST_GROUP)
        for c in range(3):
            pairs[k, c] = total[c]
        return carry

    lax.fori_loop(0, live_chunks, pair_step, 0)


def post_of(q, pop, rho, u, force, common):
    c = lattice_dirs[q]
    w = lattice_weights[q]

    def dot(v):
        total = None
        for k in range(3):
            if c[k] == 0:
                continue
            term = v[k] if c[k] == 1 else -v[k]
            total = term if total is None else total + term
        return total

    base, dotted = common
    kept = (1.0 - 1.0 / relax_time) * pop
    scale = (1.0 - 0.5 / relax_time) * w
    if q == 0:
        return kept + (w / relax_time) * rho * base - (3.0 * scale) * dotted
    along = dot(u)
    pushed = dot(force)
    balance = (w / relax_time) * rho * (base + along * (3.0 + 4.5 * along))
    source = (3.0 * scale) * (pushed * (1.0 + 3.0 * along) - dotted)
    return kept + balance + source


def main_kernel(pops, mix, sides, react_in, pairs, spread, down_rows, up_rows, from_left, from_right, moved_out, out,
                lists, moved, sems, ext, tside, tflat, tcorner, xtable, flo, fhi, post, gb, gz, sacc, fe, *, cx, cy, nz, slots):
    chunks = slots // LANES
    wide = cx + 2
    mom, own, _, _ = views(mix, cx, cy, nz, chunks)
    from_down, down_list = y_views(down_rows, cx, chunks)
    from_up, up_list = y_views(up_rows, cx, chunks)
    columns, rings, begins = x_layout(cy, chunks)
    high, ring = cy + 4, cy + 2

    ext[...] = jnp.zeros_like(ext)
    for c in range(3):
        for x in range(cx):
            ext[x + 2, c, 0:2, :] = from_down[2 * c : 2 * c + 2, x, :]
            ext[x + 2, c, 2 + cy : 4 + cy, :] = from_up[2 * c : 2 * c + 2, x, :]
        for x in (0, 1, cx - 2, cx - 1):
            ext[x + 2, c, 2 : 2 + cy, :] = mom[c, x]
        for x in range(2, cx - 2):
            ext[x + 2, c, 2 : 2 + SUB - 2, :] = mom[c, x, 0 : SUB - 2, :]
            ext[x + 2, c, 2 * SUB : 2 + cy, :] = mom[c, x, 2 * SUB - 2 : cy, :]
        for k in range(2):
            at = columns[2 * c + k]
            ext[k, c, 0:high, :] = from_left[at : at + high, :]
            ext[cx + 2 + k, c, 0:high, :] = from_right[at : at + high, :]
    for n, x in ((0, 0), (1, cx + 1)):
        tside[n] = both(ext[x : x + 3], 9 * YPAD, 9 * YPAD + SUB)
        for m, y in ((0, 0), (1, 2 * SUB)):
            tcorner[2 * n + m] = both(ext[x : x + 3, :, y : y + SUB, :], 9 * SUB, 10 * SUB)
    for m, y in ((0, 0), (1, 2 * SUB)):
        tflat[m] = both(ext[1 : cx + 3, :, y : y + SUB, :], wide * 3 * SUB)
    xtable[...] = both(jnp.concatenate([ext[1:2], ext[cx + 2 : cx + 3]], axis=0), 6 * YPAD)
    fe[...] = spread[...]
    flo[...] = jnp.zeros_like(flo)
    fhi[...] = jnp.zeros_like(fhi)

    sets = []
    counts = []

    def arrived(a, b, fields):
        n = len(sets)
        counts.append(unpack(lists, n, fields, chunks))
        sets.append((a, b, lambda k, n=n: lists[n, k]))

    arrived(0, -1, lambda f: down_list[f])
    arrived(0, 1, lambda f: up_list[f])
    for a, ref in ((-1, from_left), (1, from_right)):
        for begin, b in zip(begins, (0, -1, 1)):
            arrived(a, b, lambda f, ref=ref, begin=begin: ref[begin + f * chunks : begin + (f + 1) * chunks, :])
    own_count = jnp.max(own[0, 7:8, :]).astype(jnp.int32)
    own_chunks = chunks_of(own_count)

    def own_step(n, carry):
        for k in [n * UNROLL + u for u in range(UNROLL)]:
            tile = own[k]
            wx = tent(2 * SUB, -1.0, tile[0:1])
            wy = tent(YPAD, -2.0, tile[1:2])
            full = gather_rows(xtable[...], sample_table(*along_z(tile, nz))).reshape(2, 3, YPAD, LANES)
            total = full[0] * wx[0:1] + full[1] * wx[cx + 1 : cx + 2]
            sacc[k, 0:3, :] = friction * jnp.sum(total * wy[None], axis=1) - react_in[k, 0:3, :]
        return carry

    lax.fori_loop(0, steps_of(own_count), own_step, 0)

    jobs = []
    for (a, b, source), count in zip(sets, counts):
        side = 0 if a == -1 else 1
        half = 0 if b == -1 else 1
        if b == 0:
            depth, first_y, target = YPAD, -2.0, fe
        else:
            depth, first_y, target = SUB, -2.0 + 2 * SUB * half, (flo, fhi)[half]
        if a == 0:
            first_x, cols, slots_x = -1.0, wide, [(x, x) for x in range(wide)]
            table = tflat.at[half]
        else:
            cols = 3
            first_x = -2.0 if a == -1 else float(cx - 1)
            slots_x = [(0, 1), (1, 2)] if a == -1 else [(cx, 0), (cx + 1, 1)]
            table = tside.at[side] if b == 0 else tcorner.at[2 * side + half]
        jobs.append((source, count, float(a * cx), float(b * cy), table, cols, first_x, depth, first_y, slots_x,
                     target, False))
    for side, n in ((0, 1), (1, 0)):
        first_x = -2.0 if side == 0 else float(cx - 1)
        slots_x = [(0, 1), (1, 2)] if side == 0 else [(cx, 0), (cx + 1, 1)]
        source = lambda k, n=n: sides[n, k]
        near = (own[:, 0, :] < 0.0) if side == 0 else (own[:, 0, :] >= cx - 1)
        count = jnp.sum(jnp.where(near, own[:, 6, :], 0.0)).astype(jnp.int32)
        jobs.append((source, count, 0.0, 0.0, xtable, 1, first_x, YPAD, -2.0, slots_x, fe, True))

    def reaction(job, k):
        source, _, shift_x, shift_y, table, cols, first_x, depth, first_y, _, _, own_list = job
        tile = source(k)
        high, low = along_z(tile, nz)
        wx = tent(2 * SUB, first_x, tile[0:1] + shift_x)
        wy = tent(depth, first_y, tile[1:2] + shift_y)
        right = sample_table(high, low)
        if own_list:
            at = 0 if first_x < 0.0 else 3 * YPAD
            row = 1
            full = gather_rows(xtable[...], right)[at : at + 3 * YPAD].reshape(1, 3, YPAD, LANES)
            total = full[0] * wx[row : row + 1]
            react = -friction * jnp.sum(total * wy[None], axis=1)
        else:
            full = gather_rows(table[...], right)[: cols * 3 * depth].reshape(cols, 3, depth, LANES)
            total = full[0] * wx[0:1]
            for x in range(1, cols):
                total = total + full[x] * wx[x : x + 1]
            react = tile[3:6] - friction * jnp.sum(total * wy[None], axis=1)
        return react * tile[6:7], wx, wy, high, low

    def spread_job(job, parts):
        react, wx, wy, high, low = parts
        depth, slots_x = job[7], job[9]
        pieces = []
        for _, w in slots_x:
            for c in range(3):
                pieces.append((wx[w : w + 1] * react[c : c + 1]) * wy)
        got = spread_rows(both(jnp.stack(pieces), len(slots_x) * 3 * depth), high, low)
        return got.reshape(len(slots_x), 3, depth, LANES)

    def add_job(job, got):
        for n, (f, _) in enumerate(job[9]):
            job[10][f] += got[n]

    parts = [reaction(job, 0) for job in jobs]
    gots = [spread_job(job, part) for job, part in zip(jobs, parts)]
    for job, got in zip(jobs, gots):
        add_job(job, got)
    most = jobs[0][1]
    for job in jobs[1:]:
        most = jnp.maximum(most, job[1])

    @pl.when(most > LANES)
    def _():
        for job in jobs:

            def more(k, carry, job=job):
                add_job(job, spread_job(job, reaction(job, k)))
                return carry

            lax.fori_loop(1, chunks_of(job[1]), more, 0)

    for x in range(wide):
        fe[x, :, 0:SUB, :] += flo[x]
        fe[x, :, 2 * SUB : 3 * SUB, :] += fhi[x]

    base_row = SUB

    def prepared(rho, u0, force):
        half = 0.5 / rho
        u = [u0[c] + half * force[c] for c in range(3)]
        base = 1.0 - 1.5 * (u[0] * u[0] + u[1] * u[1] + u[2] * u[2])
        dotted = u[0] * force[0] + u[1] * force[1] + u[2] * force[2]
        return u, (base, dotted)

    for x in range(cx):
        for h in range(0, cy, SUB):
            force = [fe[x + 1, c, 2 + h : 2 + h + SUB, :] for c in range(3)]
            rho = mom[3, x, h : h + SUB, :]
            u, common = prepared(rho, [mom[c, x, h : h + SUB, :] for c in range(3)], force)
            for q in range(19):
                post[q, x + 1, base_row + h : base_row + h + SUB, :] = post_of(
                    q, pops[q, x, h : h + SUB, :], rho, u, force, common
                )
    for ref, row, layer, sign in ((from_left, 0, 1, 1), (from_right, cx + 1, 0, -1)):
        force = [fe[row, c, 1 : 1 + ring, :] for c in range(3)]
        rho = ref[rings[0] : rings[0] + ring, :]
        starts = [columns[2 * c + layer] + 1 for c in range(3)]
        u, common = prepared(rho, [ref[start : start + ring, :] for start in starts], force)
        for k, q in enumerate(outward(0, sign)):
            pop = ref[rings[1 + k] : rings[1 + k] + ring, :]
            post[q, row, base_row - 1 : base_row - 1 + ring, :] = post_of(q, pop, rho, u, force, common)
    for ref, row, at, layer, sign in (
        (from_down, base_row - 1, 1, 1, 1),
        (from_up, base_row + cy, cy + 2, 0, -1),
    ):
        force = [fe[1 : 1 + cx, c, at, :] for c in range(3)]
        rho = ref[6]
        u, common = prepared(rho, [ref[2 * c + layer] for c in range(3)], force)
        for k, q in enumerate(outward(1, sign)):
            post[q, 1 : 1 + cx, row, :] = post_of(q, ref[7 + k], rho, u, force, common)
    copies = []
    for q in range(19):
        dx, dy, dz = lattice_dirs[q]
        for x in range(cx):
            plane = post[q, x + 1 - dx, base_row - dy : base_row - dy + cy, :]
            if dz != 0:
                plane = pltpu.roll(plane, dz % nz, 1)
            moved[q, x] = plane
        copies.append(pltpu.make_async_copy(moved.at[q], moved_out.at[q], sems.at[q]))
        copies[-1].start()

    groups = gather_ghosts(
        gb, gz, [(source, count, float(a * cx), float(b * cy)) for (a, b, source), count in zip(sets, counts) if a != 0], nz
    )

    def pair_step(k, carry):
        total = pair_rows(gb, gz, own[k], groups, tuple(pairs[k, c] for c in range(3)), nz, LIST_GROUP)
        sums = jnp.concatenate([jnp.sum(t, axis=0, keepdims=True) for t in total], axis=0)
        sacc[k, 0:3, :] = sacc[k, 0:3, :] + (48.0 * wca_energy) * sums
        return carry

    lax.fori_loop(0, own_chunks, pair_step, 0)

    for c in range(3):
        out[c * chunks : (c + 1) * chunks, :] = jnp.where(own[:, 6, :] > 0.0, sacc[:, c, :], 0.0)
    for copy in copies:
        copy.wait()


def shifted(value, axis, by):
    devices = lax.axis_size(axis)
    return lax.ppermute(value, axis, [(i, (i + by) % devices) for i in range(devices)])


def body(populations, anchor, offsets, heading, velocity, live_count):
    _, cx, cy, nz = populations.shape
    slots = anchor.shape[2]
    chunks = slots // LANES
    sizes = dict(cx=cx, cy=cy, nz=nz, slots=slots)
    vmem = pl.BlockSpec(memory_space=pltpu.VMEM)
    smem = pl.BlockSpec(memory_space=pltpu.SMEM)
    shape = jax.ShapeDtypeStruct

    hbm = pl.BlockSpec(memory_space=pltpu.HBM)

    def call(kernel, name, outs, scratch, *args, ins=None, out_specs=None, limit=48):
        return pl.pallas_call(
            functools.partial(kernel, **sizes),
            out_shape=outs,
            in_specs=ins or [vmem] * len(args),
            out_specs=out_specs or (vmem,) * len(outs),
            scratch_shapes=scratch,
            compiler_params=pltpu.CompilerParams(vmem_limit_bytes=limit * 2**20),
            name=name,
        )(*args)

    face_y = shape((STRIP * cx + FIELDS * chunks, nz), f32)
    tiles = shape((chunks, SUB, LANES), f32)
    dma = pltpu.SemaphoreType.DMA
    mix, up, down = call(
        pack_y, "pack_y",
        (shape((4 * cx * cy + (SUB + 4) * chunks + 10 * cy, LANES), f32), face_y, face_y),
        [
            pltpu.VMEM((2, chunks, SUB, LANES), f32),
            pltpu.VMEM(populations.shape, f32),
            pltpu.VMEM((chunks, LANES), jnp.int32),
            pltpu.VMEM((3 * chunks, LANES), f32),
            pltpu.VMEM((2, slots), f32),
            pltpu.VMEM((3 * chunks, LANES), f32),
            pltpu.VMEM((2, chunks, LANES), f32),
            dma((5,)),
        ],
        populations, anchor.reshape(chunks, LANES), offsets.reshape(3 * chunks, LANES), heading[0, 0],
        velocity.reshape(3 * chunks, LANES), live_count, ins=[hbm] * 5 + [smem], limit=62,
    )
    from_down = shifted(up, "gy", 1)
    from_up = shifted(down, "gy", -1)
    part, sides, gb, gz, early = call(
        own_first, "own_first",
        (tiles, shape((2, chunks, SUB, LANES), f32), shape((2, slots, LANES), f32), shape((slots, LANES), jnp.int32),
         shape((EARLY, 3, SUB, LANES), f32)),
        [pltpu.VMEM((3 * cx * cy, 2 * nz), bf16)],
        mix,
    )
    face_x = shape((x_layout(cy, chunks)[2][3], nz), f32)
    right, left = call(
        pack_x, "pack_x", (face_x, face_x), [], mix, sides, from_down, from_up,
    )
    from_left = shifted(right, "gx", 1)
    from_right = shifted(left, "gx", -1)
    wide = cx + 2
    spread, react, pairs = call(
        own_second, "own_second",
        (shape((wide, 3, YPAD, nz), f32), tiles, shape((chunks, 3, SUB, LANES), f32)),
        [
            pltpu.VMEM((6 * cx, 2 * nz), bf16),
            pltpu.VMEM((2, chunks, SUB, LANES), f32),
            pltpu.VMEM((2, 2 * slots + LANES, LANES), f32),
            pltpu.VMEM((2 * slots + LANES, LANES), jnp.int32),
        ],
        mix, part, gb, gz, early, from_down, from_up,
    )
    moved, force = call(
        main_kernel, "main",
        (shape(populations.shape, f32), shape((3 * chunks, LANES), f32)),
        [
            pltpu.VMEM((8, chunks, SUB, LANES), f32),
            pltpu.VMEM(populations.shape, f32),
            dma((19,)),
            pltpu.VMEM((cx + 4, 3, YPAD, nz), f32),
            pltpu.VMEM((2, 9 * YPAD + SUB, 2 * nz), bf16),
            pltpu.VMEM((2, wide * 3 * SUB, 2 * nz), bf16),
            pltpu.VMEM((4, 10 * SUB, 2 * nz), bf16),
            pltpu.VMEM((6 * YPAD, 2 * nz), bf16),
            pltpu.VMEM((wide, 3, SUB, nz), f32),
            pltpu.VMEM((wide, 3, SUB, nz), f32),
            pltpu.VMEM((19, cx + 2, cy + 2 * SUB, nz), f32),
            pltpu.VMEM((2, 6 * slots + LANES, LANES), f32),
            pltpu.VMEM((6 * slots + LANES, LANES), jnp.int32),
            pltpu.VMEM((chunks, SUB, LANES), f32),
            pltpu.VMEM((wide, 3, YPAD, nz), f32),
        ],
        populations, mix, sides, react, pairs, spread, from_down, from_up, from_left, from_right,
        out_specs=(hbm, vmem),
    )
    return moved, force.reshape(1, 1, 3, slots)


def solution(mesh):
    return jax.shard_map(
        body,
        mesh=mesh,
        in_specs=(
            P(None, "gx", "gy", None),
            P("gx", "gy", None),
            P("gx", "gy", None, None),
            P("gx", "gy", None, None),
            P("gx", "gy", None, None),
            P("gx", "gy"),
        ),
        out_specs=(P(None, "gx", "gy", None), P("gx", "gy", None, None)),
        check_vma=False,
    )
```
